32 devices in a mesh: groups: 2 (over y), expert: 16 (over z, x, core), node: 1.
Axes of the slice: x: 2, y: 2, z: 4, core: 2. Of those that a mesh axis runs over, the one named last changes fastest.
Arguments:
- tokens: bfloat16 [768, 2048], P(('groups', 'expert')), parts along dimension 0, may hold values from -6 to 6
- norm_gain: float32 [2048], replicated, may hold values from 0.5 to 1.5
- probe_signs: int32 [768, 2048], P(('groups', 'expert')), parts along dimension 0, may hold values from 0 to 1
- cotangent: bfloat16 [768, 2048], P(('groups', 'expert')), parts along dimension 0, may hold values from -6 to 6
- routes: int32 [2, 768, 4], P('node', ('groups', 'expert')), parts along dimension 1, may hold values from 0 to 7, all different within a row; in each aligned block of 24 rows (0 to 23, 24 to 47, ..., all dimensions but the last counted through in order) at most 16 rows name the same one
- gates: float32 [2, 768, 4], P('node', ('groups', 'expert')), parts along dimension 1, may hold values from 0.05 to 0.5
- expert_weights: bfloat16 [3, 2048, 6144], P(None, None, ('expert', 'node')), may hold values from -0.125 to 0.125
Outputs:
- hvp: float32 [768, 2048], P(('groups', 'expert'), 'node'), parts along dimension 0
- quad: float32 [768], P(('groups', 'expert')), parts along dimension 0
The draws below stay inside these ranges and needn't reach their ends.
There are 2 independent parts, one for each index of `groups`. The reference program is written for one: setup_inputs(seed, part) draws one part's arguments, and reference() takes and returns one part's arrays. A program takes and returns all parts, laid end to end along the dimension named above; an argument that names none is the same for every part. Nothing has to cross between parts.
Inputs may be any that keep to these rules, and one draw needn't show every extreme that they name: Each row of routes names 4 different experts. In every aligned block of 24 rows of one node group no expert is named more than 16 times, a bound that some block reaches.
All inputs are finite; a program needn't handle non-finite values.
Results may differ from the reference program's by a relative error of at most 0.0048.
Values may be sent and summed in bfloat16 or wider, within the bound.
No kernel may reach another device: no remote copies, remote signals or barrier semaphores. Data moves between devices by JAX's collectives and lax.ppermute only.
A program may use at most 64 MiB of HBM per device.

```python
import math
import jax
import jax.numpy as jnp
import numpy as np
from jax import lax

D = 2048
FF = 768
HALF = 4
TOK_DEV = 24
EXPERTS = 8
TOKENS = 384
CAP = 16
N_EXPERT = 16


def shared_bits(key):
    return jax.random.randint(jax.random.fold_in(key, 11), (TOKENS, D), 0, 2).astype(jnp.int32)


def draw_probe_signs(key, part):
    return shared_bits(key)


def draw_tokens(key, part):
    signs = (2 * shared_bits(key) - 1).astype(jnp.float32)
    key = jax.random.fold_in(key, 5)
    key_noise, key_amount = jax.random.split(key, 2)
    amount = jax.random.uniform(key_amount, (TOKENS, 1), jnp.float32, 0.6, 1.4)
    noise = jnp.clip(jax.random.normal(key_noise, (TOKENS, D), jnp.float32), -4.0, 4.0)
    return (noise + amount * signs).astype(jnp.bfloat16)


def level_of(rng, extent, pieces, least, high):
    factor_of = 1.0
    for axis_at, blocks in pieces:
        draws = jax.random.uniform(jax.random.fold_in(jax.random.fold_in(rng, 6), axis_at), (blocks,), jnp.float32, least / len(pieces), high / len(pieces))
        factor_of = factor_of * jnp.repeat(jnp.exp(draws), extent[axis_at] // blocks).reshape((-1,) + (1,) * (len(extent) - 1 - axis_at))
    return factor_of


def deal_out(stream_key, own, number, rows, number_of, top, most, skew):
    order = jax.random.permutation(stream_key, number_of)
    heavy_load, usual = load_shares(number_of, rows * top, most, skew, True), load_shares(number_of, rows * top, most, skew, False)
    places = jnp.arange(number_of)

    def named(tallies, turn):
        used = int((tallies > 0).sum())
        fixed = max(1, used // 4)
        passed = fixed + (places - fixed + turn * (used - fixed)) % max(1, number_of - fixed)
        return jnp.zeros((number_of,), jnp.int32).at[order[jnp.where(places < fixed, places, passed)]].set(jnp.asarray(tallies, jnp.int32))

    tallies = jnp.where(number % 4 == 0, named(heavy_load, number // 4), named(usual, number - number // 4 - 1))
    mixed = jax.random.permutation(jax.random.fold_in(own, 3), number_of)
    giver, taker = mixed[0:number_of // 2 * 2:2], mixed[1:number_of // 2 * 2:2]
    room = jnp.minimum(tallies[giver] - 1, most - tallies[taker]) // 2
    room = jnp.where((giver == order[0]) | (taker == order[0]) | (tallies[taker] == 0), 0, jnp.maximum(room, 0))
    passed = jax.random.randint(jax.random.fold_in(own, 4), (number_of // 2,), 0, 1 << 20) % (room + 1)
    tallies = tallies.at[giver].add(-passed).at[taker].add(passed)
    labels = jnp.searchsorted(jnp.cumsum(tallies), jnp.arange(rows * top), side="right").astype(jnp.int32)
    grid = labels.reshape(top, rows).T
    grid = grid[jax.random.permutation(jax.random.fold_in(own, 1), rows)]
    turn = jax.random.randint(jax.random.fold_in(own, 2), (rows, 1), 0, top)
    return jnp.take_along_axis(grid, (jnp.arange(top)[None, :] + turn) % top, axis=1)


def load_shares(count, total, reach, skew, full):
    weights = [(1 << 20) // math.isqrt(rank ** skew) + 1 for rank in range(1, count + 1)]
    largest = reach if full else min(reach, max(-(-total // count), total * weights[0] // sum(weights)))
    least = 1 if total - largest >= count - 1 else 0
    given, surplus = [largest] + [least] * (count - 1), total - largest - least * (count - 1)
    while surplus > 0:
        movable = [i for i in range(1, count) if given[i] < largest] or [i for i in range(1, count) if given[i] < reach]
        pool, left = sum([weights[i] for i in movable]), surplus
        for i in movable:
            addition = min(reach - given[i], max(1, left * weights[i] // pool), surplus)
            given[i] = given[i] + addition
            surplus = surplus - addition
    return np.array(given)


def centred(key, shape, width, most, cuts=(), kind=jnp.bfloat16):
    values = width * jax.random.normal(key, shape, jnp.float32)
    if cuts:
        values = values * level_of(key, shape, cuts, -0.22, 0.18)
    return jnp.clip(values, -most, most).astype(kind)


def setup_inputs(seed: int = 0, part: int = 0) -> dict:
    keys = jax.random.split(jax.random.key(seed), 8)
    part_splits = jax.random.split(jax.random.fold_in(keys[7], part), 8)
    tokens = draw_tokens(jax.random.fold_in(jax.random.fold_in(keys[7], part), 71), part)
    norm_gain = jnp.clip(1.0 + 0.1 * jax.random.normal(keys[1], (D,), jnp.float32), 0.5, 1.5)
    probe_signs = draw_probe_signs(jax.random.fold_in(jax.random.fold_in(keys[7], part), 71), part)
    cotangent = centred(part_splits[3], (TOKENS, D), 1.0, 6.0, ((0, 16),))
    routes_keys = jax.random.split(jax.random.fold_in(part_splits[4], 1), 2 * TOKENS // TOK_DEV)
    routes_turns = jax.random.permutation(jax.random.fold_in(part_splits[4], 3), 2 * TOKENS // TOK_DEV)
    routes = jax.vmap(lambda own, number: deal_out(jax.random.fold_in(part_splits[4], 2), own, number, TOK_DEV, EXPERTS, HALF, CAP, 2))(routes_keys, routes_turns).reshape((2, TOKENS, HALF))
    gates = jnp.clip(jnp.exp(math.log(0.5) - 2.3025851 * jax.random.uniform(part_splits[5], (2, TOKENS, HALF), jnp.float32) ** level_of(part_splits[5], (2, TOKENS, HALF), ((1, 16),), -0.2, 0.2)), 0.05, 0.5)
    expert_weights = centred(keys[6], (3, D, EXPERTS * FF), D ** -0.5, 0.125, ((2, 16),))
    return dict(tokens=tokens, norm_gain=norm_gain, probe_signs=probe_signs, cotangent=cotangent, routes=routes, gates=gates, expert_weights=expert_weights)


EPS = 1e-06

def expert_terms(weights, rows, rows_t, cotan):
    count = rows.shape[0]
    both = jnp.concatenate([rows, rows_t], 0)
    pre_gate = jnp.dot(both, weights[0], preferred_element_type=jnp.float32)
    pre_up = jnp.dot(both, weights[1], preferred_element_type=jnp.float32)
    gate, gate_t = (pre_gate[:count], pre_gate[count:])
    up, up_t = (pre_up[:count], pre_up[count:])
    back = jnp.dot(cotan, weights[2], preferred_element_type=jnp.float32)
    sig = jax.nn.sigmoid(gate)
    act = gate * sig
    slope = sig * (1.0 + gate * (1.0 - sig))
    bend = sig * (1.0 - sig) * (2.0 + gate * (1.0 - 2.0 * sig))
    d_gate = (back * slope * up).astype(jnp.bfloat16)
    d_up = (back * act).astype(jnp.bfloat16)
    t_gate = (back * (bend * gate_t * up + slope * up_t)).astype(jnp.bfloat16)
    t_up = (back * slope * gate_t).astype(jnp.bfloat16)
    contract = (((1,), (1,)), ((), ()))
    lhs_gate = jnp.concatenate([d_gate, t_gate], 0)
    lhs_up = jnp.concatenate([d_up, t_up], 0)
    total = lax.dot_general(lhs_gate, weights[0], contract, preferred_element_type=jnp.float32)
    total = total + lax.dot_general(lhs_up, weights[1], contract, preferred_element_type=jnp.float32)
    return (total[:count], total[count:])

def reference(tokens, norm_gain, probe_signs, cotangent, routes, gates, expert_weights):
    xf = tokens.astype(jnp.float32)
    probe = (2 * probe_signs - 1).astype(jnp.float32)

    def normalize(a):
        return a * lax.rsqrt(lax.optimization_barrier(jnp.mean(a * a, axis=-1, keepdims=True)) + EPS) * norm_gain
    normed = normalize(xf).astype(jnp.bfloat16)
    normed_t = jax.jvp(normalize, (xf,), (probe,))[1].astype(jnp.bfloat16)
    flat = routes.reshape(-1)
    wflat = gates.reshape(-1)
    total = flat.shape[0]
    bound = 2 * N_EXPERT * CAP
    tok_of = (jnp.arange(total) // HALF % TOKENS).astype(jnp.int32)

    def one_expert(carry, index):
        grad_sum, tan_sum = carry
        found = jnp.nonzero(flat == index, size=bound, fill_value=total)[0].astype(jnp.int32)
        valid = found < total
        safe = jnp.where(valid, found, 0).astype(jnp.int32)
        tok = tok_of[safe]
        weight = jnp.where(valid, wflat[safe], jnp.zeros_like(wflat[safe]))
        block = lax.dynamic_slice_in_dim(expert_weights, (index * FF).astype(jnp.int32), FF, 2)
        g_rows, t_rows = expert_terms(block, normed[tok], normed_t[tok], cotangent[tok])
        grad_sum = grad_sum.at[tok].add(weight[:, None] * g_rows)
        tan_sum = tan_sum.at[tok].add(weight[:, None] * t_rows)
        return ((grad_sum, tan_sum), None)
    zeros = jnp.zeros((TOKENS, D), jnp.float32)
    (grad_z, tan_z), _ = lax.scan(one_expert, (zeros, zeros), jnp.arange(EXPERTS, dtype=jnp.int32))

    def pull(a, g):
        return jax.vjp(normalize, a)[1](g)[0]
    hvp = jax.jvp(pull, (xf, grad_z), (probe, tan_z))[1]
    quad = lax.optimization_barrier(jnp.mean(probe * hvp, axis=-1))
    return (hvp, quad)
```

```python
import jax
import jax.numpy as jnp
from jax import lax
from jax.sharding import PartitionSpec as P

EPS = 1e-06


def expert_terms(weights, rows, rows_t, cotan):
    count = rows.shape[0]
    both = jnp.concatenate([rows, rows_t], 0)
    pre_gate = jnp.dot(both, weights[0], preferred_element_type=jnp.float32)
    pre_up = jnp.dot(both, weights[1], preferred_element_type=jnp.float32)
    gate, gate_t = (pre_gate[:count], pre_gate[count:])
    up, up_t = (pre_up[:count], pre_up[count:])
    back = jnp.dot(cotan, weights[2], preferred_element_type=jnp.float32)
    sig = jax.nn.sigmoid(gate)
    act = gate * sig
    slope = sig * (1.0 + gate * (1.0 - sig))
    bend = sig * (1.0 - sig) * (2.0 + gate * (1.0 - 2.0 * sig))
    d_gate = (back * slope * up).astype(jnp.bfloat16)
    d_up = (back * act).astype(jnp.bfloat16)
    t_gate = (back * (bend * gate_t * up + slope * up_t)).astype(jnp.bfloat16)
    t_up = (back * slope * gate_t).astype(jnp.bfloat16)
    contract = (((1,), (1,)), ((), ()))
    lhs_gate = jnp.concatenate([d_gate, t_gate], 0)
    lhs_up = jnp.concatenate([d_up, t_up], 0)
    total = lax.dot_general(lhs_gate, weights[0], contract, preferred_element_type=jnp.float32)
    total = total + lax.dot_general(
        lhs_up, weights[1], contract, preferred_element_type=jnp.float32
    )
    return (total[:count], total[count:])


def slot_targets(route_ids, expert_count, capacity):
    flat = route_ids.reshape(-1)
    count = flat.shape[0]
    onehot = (flat[:, None] == jnp.arange(expert_count, dtype=jnp.int32)[None, :]).astype(
        jnp.float32
    )
    lower = (jnp.arange(count)[:, None] > jnp.arange(count)[None, :]).astype(jnp.float32)
    before = jnp.dot(lower, onehot, precision=lax.Precision.HIGHEST)
    rank = jnp.sum(before * onehot, axis=1).astype(jnp.int32)
    return flat * capacity + rank


def capacity(tok_dev, half, expert_count):
    return min(2 * ((2 * tok_dev * half + 3 * expert_count - 1) // (3 * expert_count)), tok_dev)


def summed_gates(routes, gates, expert_count):
    named = routes[..., None] == jnp.arange(expert_count, dtype=jnp.int32)
    return jnp.sum(jnp.where(named, gates[..., None], 0.0), axis=(0, 2))


def dense_rows(normed, normed_t, cotangent, routes, gates, weights):
    width = normed.shape[1]
    expert_count = lax.axis_size("expert") // 2
    gate = summed_gates(routes, gates, expert_count)
    high = lax.reduce_precision(gate, 8, 7)
    low = gate - high
    pad = jnp.zeros((gate.shape[0], -2 * expert_count % 128), jnp.bfloat16)
    pack = jnp.concatenate(
        [normed, normed_t, cotangent, high.astype(jnp.bfloat16), low.astype(jnp.bfloat16), pad], 1
    )
    got = lax.all_gather(pack, "expert", axis=0, tiled=True)
    mine = lax.axis_index("expert") // 2
    pick = (jnp.arange(expert_count) == mine).astype(jnp.float32)
    tail = got[:, 3 * width :].astype(jnp.float32)
    weight = jnp.sum(
        (tail[:, :expert_count] + tail[:, expert_count : 2 * expert_count]) * pick, 1, keepdims=True
    )
    g_rows, t_rows = expert_terms(
        weights, got[:, :width], got[:, width : 2 * width], got[:, 2 * width : 3 * width]
    )
    both = jnp.concatenate([weight * g_rows, weight * t_rows], 1).astype(jnp.bfloat16)
    total = lax.psum_scatter(both, "expert", scatter_dimension=0, tiled=True).astype(jnp.float32)
    return (total[:, :width], total[:, width:])


def routed_rows(normed, normed_t, cotangent, routes, gates, weights):
    tok_dev, width = normed.shape
    groups_here = routes.shape[0]
    half = routes.shape[2]
    n_exp = lax.axis_size("expert")
    expert_count = n_exp // 2
    cap = capacity(tok_dev, half, expert_count)
    buffer_rows = expert_count * cap
    stack_z, stack_t, stack_c, stack_w = ([], [], [], [])
    for group in range(groups_here):
        target = slot_targets(routes[group], expert_count, cap)
        place = (jnp.arange(buffer_rows, dtype=jnp.int32)[:, None] == target[None, :]).reshape(
            buffer_rows, tok_dev, half
        )
        place_tok = jnp.sum(place.astype(jnp.float32), axis=2).astype(jnp.bfloat16)
        stack_w.append(jnp.sum(place.astype(jnp.float32) * gates[group][None, :, :], axis=2))
        stack_z.append(
            jnp.dot(place_tok, normed, preferred_element_type=jnp.float32).astype(jnp.bfloat16)
        )
        stack_t.append(
            jnp.dot(place_tok, normed_t, preferred_element_type=jnp.float32).astype(jnp.bfloat16)
        )
        stack_c.append(
            jnp.dot(place_tok, cotangent, preferred_element_type=jnp.float32).astype(jnp.bfloat16)
        )
    rows_z = jnp.stack(stack_z, 0)
    rows_t = jnp.stack(stack_t, 0)
    rows_c = jnp.stack(stack_c, 0)
    weighted = jnp.stack(stack_w, 0)

    def arrange(rows):
        shaped = rows.reshape(groups_here, expert_count, 1, cap, width)
        shaped = jnp.broadcast_to(shaped, (groups_here, expert_count, 2, cap, width))
        return jnp.transpose(shaped, (1, 2, 0, 3, 4)).reshape(n_exp, groups_here * cap, width)

    send_z, send_t, send_c = (arrange(rows_z), arrange(rows_t), arrange(rows_c))
    got_z = lax.all_to_all(send_z, "expert", split_axis=0, concat_axis=0, tiled=True)
    got_t = lax.all_to_all(send_t, "expert", split_axis=0, concat_axis=0, tiled=True)
    got_c = lax.all_to_all(send_c, "expert", split_axis=0, concat_axis=0, tiled=True)
    sources, items, cols = got_z.shape
    g_rows, t_rows = expert_terms(
        weights, got_z.reshape(-1, cols), got_t.reshape(-1, cols), got_c.reshape(-1, cols)
    )
    g_rows = g_rows.reshape(sources, items, cols)
    t_rows = t_rows.reshape(sources, items, cols)
    back_g = lax.all_to_all(g_rows, "expert", split_axis=0, concat_axis=0, tiled=True)
    back_t = lax.all_to_all(t_rows, "expert", split_axis=0, concat_axis=0, tiled=True)

    def restore(rows):
        shaped = jnp.sum(rows.reshape(expert_count, 2, groups_here, cap, width), axis=1)
        return jnp.transpose(shaped, (1, 0, 2, 3)).reshape(groups_here, buffer_rows, width)

    back_g = restore(back_g)
    back_t = restore(back_t)
    contract = (((0, 1), (0, 1)), ((), ()))
    grad_z = lax.dot_general(weighted, back_g, contract, precision=lax.Precision.HIGHEST)
    tan_z = lax.dot_general(weighted, back_t, contract, precision=lax.Precision.HIGHEST)
    return (grad_z, tan_z)


def local(tokens, norm_gain, probe_signs, cotangent, routes, gates, expert_weights):
    xf = tokens.astype(jnp.float32)
    probe = (2 * probe_signs - 1).astype(jnp.float32)
    tok_dev, width = xf.shape
    cap = capacity(tok_dev, routes.shape[2], lax.axis_size("expert") // 2)
    scale = lax.rsqrt(jnp.mean(xf * xf, axis=1, keepdims=True) + EPS)
    along = jnp.mean(xf * probe, axis=1, keepdims=True)
    normed = (xf * scale * norm_gain).astype(jnp.bfloat16)
    normed_t = (norm_gain * (scale * probe - scale**3 * xf * along)).astype(jnp.bfloat16)
    own_half = lax.all_gather(expert_weights, "node", axis=2, tiled=True)
    rows = dense_rows if routes.shape[0] * cap >= tok_dev else routed_rows
    grad_z, tan_z = rows(normed, normed_t, cotangent, routes, gates, own_half)
    share = width // lax.axis_size("node")
    start = lax.axis_index("node") * share
    slope_r = -(scale**3) * along
    grad_z, tan_z = lax.psum((grad_z, tan_z), "node")
    lifted = norm_gain * grad_z
    lifted_t = norm_gain * tan_z
    first = jnp.mean(xf * lifted, axis=1, keepdims=True)
    second = jnp.mean(xf * lifted_t, axis=1, keepdims=True)
    third = jnp.mean(probe * lifted, axis=1, keepdims=True)
    whole_hvp = (
        scale * lifted_t
        + slope_r * lifted
        - 3.0 * scale**2 * slope_r * first * xf
        - scale**3 * first * probe
        - scale**3 * (second + third) * xf
    )
    quad = jnp.mean(probe * whole_hvp, axis=1)
    hvp = lax.dynamic_slice_in_dim(whole_hvp, start, share, 1)
    return (hvp, quad)


def solution(mesh):
    placed = (
        P(("groups", "expert"), None),
        P(),
        P(("groups", "expert"), None),
        P(("groups", "expert"), None),
        P("node", ("groups", "expert"), None),
        P("node", ("groups", "expert"), None),
        P(None, None, ("expert", "node")),
    )
    return jax.shard_map(
        local,
        mesh=mesh,
        in_specs=placed,
        out_specs=(P(("groups", "expert"), "node"), P(("groups", "expert"))),
        check_vma=False,
    )
```

```python
import jax
import jax.numpy as jnp
from jax import lax
from jax.sharding import PartitionSpec as P

EPS = 1e-06


def expert_terms(weights, rows, rows_t, cotan):
    count = rows.shape[0]
    both = jnp.concatenate([rows, rows_t], 0)
    pre_gate = jnp.dot(both, weights[0], preferred_element_type=jnp.float32)
    pre_up = jnp.dot(both, weights[1], preferred_element_type=jnp.float32)
    gate, gate_t = (pre_gate[:count], pre_gate[count:])
    up, up_t = (pre_up[:count], pre_up[count:])
    back = jnp.dot(cotan, weights[2], preferred_element_type=jnp.float32)
    sig = jax.nn.sigmoid(gate)
    act = gate * sig
    slope = sig * (1.0 + gate * (1.0 - sig))
    bend = sig * (1.0 - sig) * (2.0 + gate * (1.0 - 2.0 * sig))
    d_gate = (back * slope * up).astype(jnp.bfloat16)
    d_up = (back * act).astype(jnp.bfloat16)
    t_gate = (back * (bend * gate_t * up + slope * up_t)).astype(jnp.bfloat16)
    t_up = (back * slope * gate_t).astype(jnp.bfloat16)
    contract = (((1,), (1,)), ((), ()))
    lhs_gate = jnp.concatenate([d_gate, t_gate], 0)
    lhs_up = jnp.concatenate([d_up, t_up], 0)
    total = lax.dot_general(lhs_gate, weights[0], contract, preferred_element_type=jnp.float32)
    total = total + lax.dot_general(
        lhs_up, weights[1], contract, preferred_element_type=jnp.float32
    )
    return (total[:count], total[count:])


def slot_targets(route_ids, expert_count, capacity):
    flat = route_ids.reshape(-1)
    count = flat.shape[0]
    onehot = (flat[:, None] == jnp.arange(expert_count, dtype=jnp.int32)[None, :]).astype(
        jnp.float32
    )
    lower = (jnp.arange(count)[:, None] > jnp.arange(count)[None, :]).astype(jnp.float32)
    before = jnp.dot(lower, onehot, precision=lax.Precision.HIGHEST)
    rank = jnp.sum(before * onehot, axis=1).astype(jnp.int32)
    return flat * capacity + rank


def capacity(tok_dev, half, expert_count):
    return min(2 * ((2 * tok_dev * half + 3 * expert_count - 1) // (3 * expert_count)), tok_dev)


def summed_gates(routes, gates, expert_count):
    named = routes[..., None] == jnp.arange(expert_count, dtype=jnp.int32)
    return jnp.sum(jnp.where(named, gates[..., None], 0.0), axis=(0, 2))


def moved(rows, turns, flip_x=False, flip_core=False):
    count = lax.axis_size("expert")
    pairs = [
        (i, (i + 4 * turns) % count ^ (2 * flip_x) ^ (1 * flip_core)) for i in range(count)
    ]
    return lax.ppermute(rows, "expert", pairs)


def dense_rows(normed, normed_t, cotangent, routes, gates, weights):
    tok_dev, width = normed.shape
    n_exp = lax.axis_size("expert")
    expert_count = n_exp // 2
    turns = n_exp // 4
    weights_other = moved(weights, 0, flip_core=True)
    gate = summed_gates(routes, gates, expert_count)
    high = lax.reduce_precision(gate, 8, 7)
    low = gate - high
    pad = jnp.zeros((gate.shape[0], -2 * expert_count % 128), jnp.bfloat16)
    pack = jnp.concatenate(
        [normed, normed_t, cotangent, high.astype(jnp.bfloat16), low.astype(jnp.bfloat16), pad], 1
    )
    same = {0: pack}
    ahead, behind = turns // 2, (turns - 1) // 2
    for k in range(1, ahead + 1):
        same[k] = moved(same[k - 1], 1)
    for k in range(1, behind + 1):
        same[turns - k] = moved(same[(turns - k + 1) % turns], -1)
    across = {k: moved(same[k], 0, flip_x=True) for k in same}
    got = jnp.concatenate([same[k] for k in range(turns)] + [across[k] for k in range(turns)], 0)
    mine = lax.axis_index("expert") // 2
    pick = (jnp.arange(expert_count) == mine).astype(jnp.float32)
    tail = got[:, 3 * width :].astype(jnp.float32)
    weight = jnp.sum(
        (tail[:, :expert_count] + tail[:, expert_count : 2 * expert_count]) * pick, 1, keepdims=True
    )
    rows = (got[:, :width], got[:, width : 2 * width], got[:, 2 * width : 3 * width])
    g_own, t_own = expert_terms(weights, *rows)
    g_other, t_other = expert_terms(weights_other, *rows)
    both = jnp.concatenate([weight * (g_own + g_other), weight * (t_own + t_other)], 1)
    both = both.reshape(2, turns, tok_dev, 2 * width)

    def summed(k):
        return both[0, k] + moved(both[1, k].astype(jnp.bfloat16), 0, flip_x=True).astype(jnp.float32)

    def passed(rows, step):
        return moved(rows.astype(jnp.bfloat16), step).astype(jnp.float32)

    forward, backward = None, None
    for k in range(ahead, 0, -1):
        part = summed(k)
        forward = passed(part if forward is None else part + forward, -1)
    for k in range(behind, 0, -1):
        part = summed(turns - k)
        backward = passed(part if backward is None else part + backward, 1)
    total = summed(0) + forward + backward
    return (total[:, :width], total[:, width:])


def routed_rows(normed, normed_t, cotangent, routes, gates, weights):
    tok_dev, width = normed.shape
    groups_here = routes.shape[0]
    half = routes.shape[2]
    n_exp = lax.axis_size("expert")
    expert_count = n_exp // 2
    cap = capacity(tok_dev, half, expert_count)
    buffer_rows = expert_count * cap
    stack_z, stack_t, stack_c, stack_w = ([], [], [], [])
    for group in range(groups_here):
        target = slot_targets(routes[group], expert_count, cap)
        place = (jnp.arange(buffer_rows, dtype=jnp.int32)[:, None] == target[None, :]).reshape(
            buffer_rows, tok_dev, half
        )
        place_tok = jnp.sum(place.astype(jnp.float32), axis=2).astype(jnp.bfloat16)
        stack_w.append(jnp.sum(place.astype(jnp.float32) * gates[group][None, :, :], axis=2))
        stack_z.append(
            jnp.dot(place_tok, normed, preferred_element_type=jnp.float32).astype(jnp.bfloat16)
        )
        stack_t.append(
            jnp.dot(place_tok, normed_t, preferred_element_type=jnp.float32).astype(jnp.bfloat16)
        )
        stack_c.append(
            jnp.dot(place_tok, cotangent, preferred_element_type=jnp.float32).astype(jnp.bfloat16)
        )
    rows_z = jnp.stack(stack_z, 0)
    rows_t = jnp.stack(stack_t, 0)
    rows_c = jnp.stack(stack_c, 0)
    weighted = jnp.stack(stack_w, 0)

    def arrange(rows):
        shaped = rows.reshape(groups_here, expert_count, 1, cap, width)
        shaped = jnp.broadcast_to(shaped, (groups_here, expert_count, 2, cap, width))
        return jnp.transpose(shaped, (1, 2, 0, 3, 4)).reshape(n_exp, groups_here * cap, width)

    send_z, send_t, send_c = (arrange(rows_z), arrange(rows_t), arrange(rows_c))
    got_z = lax.all_to_all(send_z, "expert", split_axis=0, concat_axis=0, tiled=True)
    got_t = lax.all_to_all(send_t, "expert", split_axis=0, concat_axis=0, tiled=True)
    got_c = lax.all_to_all(send_c, "expert", split_axis=0, concat_axis=0, tiled=True)
    sources, items, cols = got_z.shape
    g_rows, t_rows = expert_terms(
        weights, got_z.reshape(-1, cols), got_t.reshape(-1, cols), got_c.reshape(-1, cols)
    )
    g_rows = g_rows.reshape(sources, items, cols)
    t_rows = t_rows.reshape(sources, items, cols)
    back_g = lax.all_to_all(g_rows, "expert", split_axis=0, concat_axis=0, tiled=True)
    back_t = lax.all_to_all(t_rows, "expert", split_axis=0, concat_axis=0, tiled=True)

    def restore(rows):
        shaped = jnp.sum(rows.reshape(expert_count, 2, groups_here, cap, width), axis=1)
        return jnp.transpose(shaped, (1, 0, 2, 3)).reshape(groups_here, buffer_rows, width)

    back_g = restore(back_g)
    back_t = restore(back_t)
    contract = (((0, 1), (0, 1)), ((), ()))
    grad_z = lax.dot_general(weighted, back_g, contract, precision=lax.Precision.HIGHEST)
    tan_z = lax.dot_general(weighted, back_t, contract, precision=lax.Precision.HIGHEST)
    return (grad_z, tan_z)


def local(tokens, norm_gain, probe_signs, cotangent, routes, gates, expert_weights):
    xf = tokens.astype(jnp.float32)
    probe = (2 * probe_signs - 1).astype(jnp.float32)
    tok_dev, width = xf.shape
    cap = capacity(tok_dev, routes.shape[2], lax.axis_size("expert") // 2)
    scale = lax.rsqrt(jnp.mean(xf * xf, axis=1, keepdims=True) + EPS)
    along = jnp.mean(xf * probe, axis=1, keepdims=True)
    normed = (xf * scale * norm_gain).astype(jnp.bfloat16)
    normed_t = (norm_gain * (scale * probe - scale**3 * xf * along)).astype(jnp.bfloat16)
    own_half = lax.all_gather(expert_weights, "node", axis=2, tiled=True)
    rows = dense_rows if routes.shape[0] * cap >= tok_dev else routed_rows
    grad_z, tan_z = rows(normed, normed_t, cotangent, routes, gates, own_half)
    share = width // lax.axis_size("node")
    start = lax.axis_index("node") * share
    slope_r = -(scale**3) * along
    grad_z, tan_z = lax.psum((grad_z, tan_z), "node")
    lifted = norm_gain * grad_z
    lifted_t = norm_gain * tan_z
    first = jnp.mean(xf * lifted, axis=1, keepdims=True)
    second = jnp.mean(xf * lifted_t, axis=1, keepdims=True)
    third = jnp.mean(probe * lifted, axis=1, keepdims=True)
    whole_hvp = (
        scale * lifted_t
        + slope_r * lifted
        - 3.0 * scale**2 * slope_r * first * xf
        - scale**3 * first * probe
        - scale**3 * (second + third) * xf
    )
    quad = jnp.mean(probe * whole_hvp, axis=1)
    hvp = lax.dynamic_slice_in_dim(whole_hvp, start, share, 1)
    return (hvp, quad)


def solution(mesh):
    placed = (
        P(("groups", "expert"), None),
        P(),
        P(("groups", "expert"), None),
        P(("groups", "expert"), None),
        P("node", ("groups", "expert"), None),
        P("node", ("groups", "expert"), None),
        P(None, None, ("expert", "node")),
    )
    return jax.shard_map(
        local,
        mesh=mesh,
        in_specs=placed,
        out_specs=(P(("groups", "expert"), "node"), P(("groups", "expert"))),
        check_vma=False,
    )
```

```python
import functools

import jax
import jax.numpy as jnp
from jax import lax
from jax.experimental import pallas as pl
from jax.experimental.pallas import tpu as pltpu
from jax.sharding import PartitionSpec as P

EPS = 1e-06
VMEM = 32 * 1024 * 1024


def expert_terms(weights, rows, rows_t, cotan):
    count = rows.shape[0]
    both = jnp.concatenate([rows, rows_t], 0)
    pre_gate = jnp.dot(both, weights[0], preferred_element_type=jnp.float32)
    pre_up = jnp.dot(both, weights[1], preferred_element_type=jnp.float32)
    gate, gate_t = (pre_gate[:count], pre_gate[count:])
    up, up_t = (pre_up[:count], pre_up[count:])
    back = jnp.dot(cotan, weights[2], preferred_element_type=jnp.float32)
    sig = jax.nn.sigmoid(gate)
    act = gate * sig
    slope = sig * (1.0 + gate * (1.0 - sig))
    bend = sig * (1.0 - sig) * (2.0 + gate * (1.0 - 2.0 * sig))
    d_gate = (back * slope * up).astype(jnp.bfloat16)
    d_up = (back * act).astype(jnp.bfloat16)
    t_gate = (back * (bend * gate_t * up + slope * up_t)).astype(jnp.bfloat16)
    t_up = (back * slope * gate_t).astype(jnp.bfloat16)
    contract = (((1,), (1,)), ((), ()))
    lhs_gate = jnp.concatenate([d_gate, t_gate], 0)
    lhs_up = jnp.concatenate([d_up, t_up], 0)
    total = lax.dot_general(lhs_gate, weights[0], contract, preferred_element_type=jnp.float32)
    total = total + lax.dot_general(
        lhs_up, weights[1], contract, preferred_element_type=jnp.float32
    )
    return (total[:count], total[count:])


def slot_targets(route_ids, expert_count, capacity):
    flat = route_ids.reshape(-1)
    count = flat.shape[0]
    onehot = (flat[:, None] == jnp.arange(expert_count, dtype=jnp.int32)[None, :]).astype(
        jnp.float32
    )
    lower = (jnp.arange(count)[:, None] > jnp.arange(count)[None, :]).astype(jnp.float32)
    before = jnp.dot(lower, onehot, precision=lax.Precision.HIGHEST)
    rank = jnp.sum(before * onehot, axis=1).astype(jnp.int32)
    return flat * capacity + rank


def capacity(tok_dev, half, expert_count):
    return min(2 * ((2 * tok_dev * half + 3 * expert_count - 1) // (3 * expert_count)), tok_dev)


def rms_terms(xf, probe):
    scale = lax.rsqrt(jnp.mean(xf * xf, axis=1, keepdims=True) + EPS)
    along = jnp.mean(xf * probe, axis=1, keepdims=True)
    return scale, along


def pack_kernel(expert_count, tokens, gain, signs, cotangent, routes, gates, pack):
    width = tokens.shape[1]
    xf = tokens[...].astype(jnp.float32)
    probe = (2 * signs[...] - 1).astype(jnp.float32)
    scale, along = rms_terms(xf, probe)
    pack[:, :width] = (xf * scale * gain[...]).astype(jnp.bfloat16)
    tangent = gain[...] * (scale * probe - scale**3 * xf * along)
    pack[:, width : 2 * width] = tangent.astype(jnp.bfloat16)
    pack[:, 2 * width : 3 * width] = cotangent[...]
    lane = lax.broadcasted_iota(jnp.int32, (tokens.shape[0], pack.shape[1] - 3 * width), 1)
    expert = lax.rem(lane, expert_count)
    gate = jnp.zeros(lane.shape, jnp.float32)
    for group in range(routes.shape[0]):
        for slot in range(routes.shape[2]):
            named = routes[group, :, slot : slot + 1] == expert
            gate = gate + jnp.where(named, gates[group, :, slot : slot + 1], 0.0)
    high = gate.astype(jnp.bfloat16).astype(jnp.float32)
    tail = jnp.where(lane < expert_count, high, gate - high)
    tail = jnp.where(lane < 2 * expert_count, tail, 0.0)
    pack[:, 3 * width :] = tail.astype(jnp.bfloat16)


def packed(tokens, norm_gain, probe_signs, cotangent, routes, gates, expert_count):
    tok_dev, width = tokens.shape
    tail = -(-2 * expert_count // 128) * 128
    return pl.pallas_call(
        functools.partial(pack_kernel, expert_count),
        out_shape=jax.ShapeDtypeStruct((tok_dev, 3 * width + tail), jnp.bfloat16),
        compiler_params=pltpu.CompilerParams(vmem_limit_bytes=VMEM),
        cost_estimate=pl.CostEstimate(
            flops=20 * tok_dev * width, bytes_accessed=14 * tok_dev * width, transcendentals=0
        ),
    )(tokens, norm_gain.reshape(1, width), probe_signs, cotangent, routes, gates)


def expert_kernel(count, expert_count, *refs):
    packs, halves, outs = (refs[:count], refs[count : count + 2], refs[count + 2 : 2 * count + 2])
    held, both, cotan, acc, sems = refs[2 * count + 2 :]
    tok_dev = packs[0].shape[0]
    _, width, hidden = held.shape
    half = hidden // 2
    rows = count * tok_dev
    copies = [
        [
            pltpu.make_async_copy(
                halves[h].at[part], held.at[part, :, pl.ds(h * half, half)], sems.at[h, part]
            )
            for part in range(3)
        ]
        for h in range(2)
    ]
    for h in range(2):
        for part in range(3):
            copies[h][part].start()

    def stacked(start, size):
        return jnp.concatenate([p[:, start : start + size].astype(jnp.float32) for p in packs], 0)

    both[:rows, :] = stacked(0, width).astype(jnp.bfloat16)
    both[rows:, :] = stacked(width, width).astype(jnp.bfloat16)
    cotan[...] = stacked(2 * width, width).astype(jnp.bfloat16)
    tail = stacked(3 * width, packs[0].shape[1] - 3 * width)
    mine = lax.axis_index("expert") // 2
    lane = lax.broadcasted_iota(jnp.int32, tail.shape, 1)
    picked = (lane == mine) | (lane == mine + expert_count)
    gate_row = jnp.sum(jnp.where(picked, tail, 0.0), axis=1, keepdims=True)
    waited = set()

    def weights(part, start, size):
        for h in range(2):
            if start < (h + 1) * half and start + size > h * half and (h, part) not in waited:
                copies[h][part].wait()
                waited.add((h, part))
        return held[part, :, start : start + size]

    block = 256 if hidden % 256 == 0 else half
    contract = (((1,), (1,)), ((), ()))
    for start in range(0, hidden, block):
        pre_gate = jnp.dot(
            both[...], weights(0, start, block), preferred_element_type=jnp.float32
        )
        pre_up = jnp.dot(both[...], weights(1, start, block), preferred_element_type=jnp.float32)
        back = jnp.dot(cotan[...], weights(2, start, block), preferred_element_type=jnp.float32)
        gate, gate_t = (pre_gate[:rows], pre_gate[rows:])
        up, up_t = (pre_up[:rows], pre_up[rows:])
        sig = jax.nn.sigmoid(gate)
        act = gate * sig
        slope = sig * (1.0 + gate * (1.0 - sig))
        bend = sig * (1.0 - sig) * (2.0 + gate * (1.0 - 2.0 * sig))
        d_gate = (back * slope * up).astype(jnp.bfloat16)
        d_up = (back * act).astype(jnp.bfloat16)
        t_gate = (back * (bend * gate_t * up + slope * up_t)).astype(jnp.bfloat16)
        t_up = (back * slope * gate_t).astype(jnp.bfloat16)
        total = lax.dot_general(
            jnp.concatenate([d_gate, t_gate], 0),
            weights(0, start, block),
            contract,
            preferred_element_type=jnp.float32,
        )
        total = total + lax.dot_general(
            jnp.concatenate([d_up, t_up], 0),
            weights(1, start, block),
            contract,
            preferred_element_type=jnp.float32,
        )
        acc[...] = total if start == 0 else acc[...] + total
    for n in range(count):
        part = slice(n * tok_dev, (n + 1) * tok_dev)
        later = slice(rows + n * tok_dev, rows + (n + 1) * tok_dev)
        outs[n][:, :width] = (acc[part] * gate_row[part]).astype(outs[n].dtype)
        outs[n][:, width:] = (acc[later] * gate_row[part]).astype(outs[n].dtype)


def experts(packs, kinds, own, other, expert_count):
    count = len(packs)
    tok_dev = packs[0].shape[0]
    _, width, half = own.shape
    rows = count * tok_dev
    whole = pl.BlockSpec(memory_space=pltpu.VMEM)
    flops = 2 * 9 * rows * width * 2 * half
    return pl.pallas_call(
        functools.partial(expert_kernel, count, expert_count),
        out_shape=[jax.ShapeDtypeStruct((tok_dev, 2 * width), kind) for kind in kinds],
        in_specs=[whole] * count + [pl.BlockSpec(memory_space=pl.ANY)] * 2,
        out_specs=[whole] * count,
        scratch_shapes=[
            pltpu.VMEM((3, width, 2 * half), jnp.bfloat16),
            pltpu.VMEM((2 * rows, width), jnp.bfloat16),
            pltpu.VMEM((rows, width), jnp.bfloat16),
            pltpu.VMEM((2 * rows, width), jnp.float32),
            pltpu.SemaphoreType.DMA((2, 3)),
        ],
        compiler_params=pltpu.CompilerParams(vmem_limit_bytes=VMEM),
        cost_estimate=pl.CostEstimate(
            flops=flops, bytes_accessed=12 * width * half, transcendentals=2 * rows * half
        ),
    )(*packs, own, other)


def finish_kernel(tokens, gain, signs, kept, forward, backward, hvp, quad):
    width = tokens.shape[1]
    xf = tokens[...].astype(jnp.float32)
    probe = (2 * signs[...] - 1).astype(jnp.float32)
    scale, along = rms_terms(xf, probe)
    slope_r = -(scale**3) * along
    rows = kept[...] + forward[...].astype(jnp.float32) + backward[...].astype(jnp.float32)
    lifted = gain[...] * rows[:, :width]
    lifted_t = gain[...] * rows[:, width:]
    first = jnp.mean(xf * lifted, axis=1, keepdims=True)
    second = jnp.mean(xf * lifted_t, axis=1, keepdims=True)
    third = jnp.mean(probe * lifted, axis=1, keepdims=True)
    whole = (
        scale * lifted_t
        + slope_r * lifted
        - 3.0 * scale**2 * slope_r * first * xf
        - scale**3 * first * probe
        - scale**3 * (second + third) * xf
    )
    hvp[...] = whole
    quad[...] = jnp.mean(probe * whole, axis=1, keepdims=True)


def moved(rows, turns, flip_x=False, flip_core=False):
    count = lax.axis_size("expert")
    pairs = [
        (i, (i + 4 * turns) % count ^ (2 * flip_x) ^ (1 * flip_core)) for i in range(count)
    ]
    return lax.ppermute(rows, "expert", pairs)


def dense_local(tokens, norm_gain, probe_signs, cotangent, routes, gates, weights):
    tok_dev, width = tokens.shape
    n_exp = lax.axis_size("expert")
    expert_count = n_exp // 2
    turns = n_exp // 4
    ahead, behind = turns // 2, (turns - 1) // 2
    pack = packed(tokens, norm_gain, probe_signs, cotangent, routes, gates, expert_count)
    same, across = {0: pack}, {}
    across[0] = moved(pack, 0, flip_x=True)
    weights_other = moved(weights, 0, flip_core=True)
    for k in range(1, ahead + 1):
        same[k] = moved(same[k - 1], 1)
        across[k] = moved(same[k], 0, flip_x=True) if k == 1 else moved(across[k - 1], 1)
    for k in range(turns - 1, turns - 1 - behind, -1):
        same[k] = moved(same[(k + 1) % turns], -1)
        across[k] = moved(same[k], 0, flip_x=True)
    here, there = {}, {}
    distance = [(0,)] + [
        tuple(sorted({d, turns - d})) for d in range(1, ahead + 1)
    ]
    for batch in distance:
        packs = [same[k] for k in batch] + [across[k] for k in batch]
        kinds = [jnp.float32] * len(batch) + [jnp.bfloat16] * len(batch)
        results = experts(packs, kinds, weights, weights_other, expert_count)
        for n, k in enumerate(batch):
            here[k], there[k] = (results[n], results[n + len(batch)])
    summed = {k: here[k] + moved(there[k], 0, flip_x=True).astype(jnp.float32) for k in here}

    def passed(ks, step):
        rows = None
        for k in ks:
            part = summed[k] if rows is None else summed[k] + rows.astype(jnp.float32)
            rows = moved(part.astype(jnp.bfloat16), step)
        return rows

    forward = passed(range(ahead, 0, -1), -1)
    backward = passed(range(turns - behind, turns), 1)
    hvp, quad = pl.pallas_call(
        finish_kernel,
        out_shape=[
            jax.ShapeDtypeStruct((tok_dev, width), jnp.float32),
            jax.ShapeDtypeStruct((tok_dev, 1), jnp.float32),
        ],
        compiler_params=pltpu.CompilerParams(vmem_limit_bytes=VMEM),
        cost_estimate=pl.CostEstimate(
            flops=40 * tok_dev * width, bytes_accessed=26 * tok_dev * width, transcendentals=0
        ),
    )(tokens, norm_gain.reshape(1, width), probe_signs, summed[0], forward, backward)
    return (hvp, quad.reshape(tok_dev))


def routed_rows(normed, normed_t, cotangent, routes, gates, weights):
    tok_dev, width = normed.shape
    groups_here = routes.shape[0]
    half = routes.shape[2]
    n_exp = lax.axis_size("expert")
    expert_count = n_exp // 2
    cap = capacity(tok_dev, half, expert_count)
    buffer_rows = expert_count * cap
    stack_z, stack_t, stack_c, stack_w = ([], [], [], [])
    for group in range(groups_here):
        target = slot_targets(routes[group], expert_count, cap)
        place = (jnp.arange(buffer_rows, dtype=jnp.int32)[:, None] == target[None, :]).reshape(
            buffer_rows, tok_dev, half
        )
        place_tok = jnp.sum(place.astype(jnp.float32), axis=2).astype(jnp.bfloat16)
        stack_w.append(jnp.sum(place.astype(jnp.float32) * gates[group][None, :, :], axis=2))
        stack_z.append(
            jnp.dot(place_tok, normed, preferred_element_type=jnp.float32).astype(jnp.bfloat16)
        )
        stack_t.append(
            jnp.dot(place_tok, normed_t, preferred_element_type=jnp.float32).astype(jnp.bfloat16)
        )
        stack_c.append(
            jnp.dot(place_tok, cotangent, preferred_element_type=jnp.float32).astype(jnp.bfloat16)
        )
    rows_z = jnp.stack(stack_z, 0)
    rows_t = jnp.stack(stack_t, 0)
    rows_c = jnp.stack(stack_c, 0)
    weighted = jnp.stack(stack_w, 0)

    def arrange(rows):
        shaped = rows.reshape(groups_here, expert_count, 1, cap, width)
        shaped = jnp.broadcast_to(shaped, (groups_here, expert_count, 2, cap, width))
        return jnp.transpose(shaped, (1, 2, 0, 3, 4)).reshape(n_exp, groups_here * cap, width)

    send_z, send_t, send_c = (arrange(rows_z), arrange(rows_t), arrange(rows_c))
    got_z = lax.all_to_all(send_z, "expert", split_axis=0, concat_axis=0, tiled=True)
    got_t = lax.all_to_all(send_t, "expert", split_axis=0, concat_axis=0, tiled=True)
    got_c = lax.all_to_all(send_c, "expert", split_axis=0, concat_axis=0, tiled=True)
    sources, items, cols = got_z.shape
    g_rows, t_rows = expert_terms(
        weights, got_z.reshape(-1, cols), got_t.reshape(-1, cols), got_c.reshape(-1, cols)
    )
    g_rows = g_rows.reshape(sources, items, cols)
    t_rows = t_rows.reshape(sources, items, cols)
    back_g = lax.all_to_all(g_rows, "expert", split_axis=0, concat_axis=0, tiled=True)
    back_t = lax.all_to_all(t_rows, "expert", split_axis=0, concat_axis=0, tiled=True)

    def restore(rows):
        shaped = jnp.sum(rows.reshape(expert_count, 2, groups_here, cap, width), axis=1)
        return jnp.transpose(shaped, (1, 0, 2, 3)).reshape(groups_here, buffer_rows, width)

    back_g = restore(back_g)
    back_t = restore(back_t)
    contract = (((0, 1), (0, 1)), ((), ()))
    grad_z = lax.dot_general(weighted, back_g, contract, precision=lax.Precision.HIGHEST)
    tan_z = lax.dot_general(weighted, back_t, contract, precision=lax.Precision.HIGHEST)
    return (grad_z, tan_z)


def local(tokens, norm_gain, probe_signs, cotangent, routes, gates, expert_weights):
    cap = capacity(tokens.shape[0], routes.shape[2], lax.axis_size("expert") // 2)
    if lax.axis_size("node") == 1 and routes.shape[0] * cap >= tokens.shape[0]:
        return dense_local(
            tokens, norm_gain, probe_signs, cotangent, routes, gates, expert_weights
        )
    xf = tokens.astype(jnp.float32)
    probe = (2 * probe_signs - 1).astype(jnp.float32)
    tok_dev, width = xf.shape
    scale = lax.rsqrt(jnp.mean(xf * xf, axis=1, keepdims=True) + EPS)
    along = jnp.mean(xf * probe, axis=1, keepdims=True)
    normed = (xf * scale * norm_gain).astype(jnp.bfloat16)
    normed_t = (norm_gain * (scale * probe - scale**3 * xf * along)).astype(jnp.bfloat16)
    own_half = lax.all_gather(expert_weights, "node", axis=2, tiled=True)
    grad_z, tan_z = routed_rows(normed, normed_t, cotangent, routes, gates, own_half)
    share = width // lax.axis_size("node")
    start = lax.axis_index("node") * share
    slope_r = -(scale**3) * along
    grad_z, tan_z = lax.psum((grad_z, tan_z), "node")
    lifted = norm_gain * grad_z
    lifted_t = norm_gain * tan_z
    first = jnp.mean(xf * lifted, axis=1, keepdims=True)
    second = jnp.mean(xf * lifted_t, axis=1, keepdims=True)
    third = jnp.mean(probe * lifted, axis=1, keepdims=True)
    whole_hvp = (
        scale * lifted_t
        + slope_r * lifted
        - 3.0 * scale**2 * slope_r * first * xf
        - scale**3 * first * probe
        - scale**3 * (second + third) * xf
    )
    quad = jnp.mean(probe * whole_hvp, axis=1)
    hvp = lax.dynamic_slice_in_dim(whole_hvp, start, share, 1)
    return (hvp, quad)


def solution(mesh):
    placed = (
        P(("groups", "expert"), None),
        P(),
        P(("groups", "expert"), None),
        P(("groups", "expert"), None),
        P("node", ("groups", "expert"), None),
        P("node", ("groups", "expert"), None),
        P(None, None, ("expert", "node")),
    )
    return jax.shard_map(
        local,
        mesh=mesh,
        in_specs=placed,
        out_specs=(P(("groups", "expert"), "node"), P(("groups", "expert"))),
        check_vma=False,
    )
```

```python
import functools

import jax
import jax.numpy as jnp
from jax import lax
from jax.experimental import pallas as pl
from jax.experimental.pallas import tpu as pltpu
from jax.sharding import PartitionSpec as P

EPS = 1e-06
VMEM = 24 * 1024 * 1024
VMEM_ALONE = 60 * 1024 * 1024


def expert_terms(weights, rows, rows_t, cotan):
    count = rows.shape[0]
    both = jnp.concatenate([rows, rows_t], 0)
    pre_gate = jnp.dot(both, weights[0], preferred_element_type=jnp.float32)
    pre_up = jnp.dot(both, weights[1], preferred_element_type=jnp.float32)
    gate, gate_t = (pre_gate[:count], pre_gate[count:])
    up, up_t = (pre_up[:count], pre_up[count:])
    back = jnp.dot(cotan, weights[2], preferred_element_type=jnp.float32)
    sig = jax.nn.sigmoid(gate)
    act = gate * sig
    slope = sig * (1.0 + gate * (1.0 - sig))
    bend = sig * (1.0 - sig) * (2.0 + gate * (1.0 - 2.0 * sig))
    d_gate = (back * slope * up).astype(jnp.bfloat16)
    d_up = (back * act).astype(jnp.bfloat16)
    t_gate = (back * (bend * gate_t * up + slope * up_t)).astype(jnp.bfloat16)
    t_up = (back * slope * gate_t).astype(jnp.bfloat16)
    contract = (((1,), (1,)), ((), ()))
    lhs_gate = jnp.concatenate([d_gate, t_gate], 0)
    lhs_up = jnp.concatenate([d_up, t_up], 0)
    total = lax.dot_general(lhs_gate, weights[0], contract, preferred_element_type=jnp.float32)
    total = total + lax.dot_general(
        lhs_up, weights[1], contract, preferred_element_type=jnp.float32
    )
    return (total[:count], total[count:])


def slot_targets(route_ids, expert_count, capacity):
    flat = route_ids.reshape(-1)
    count = flat.shape[0]
    onehot = (flat[:, None] == jnp.arange(expert_count, dtype=jnp.int32)[None, :]).astype(
        jnp.float32
    )
    lower = (jnp.arange(count)[:, None] > jnp.arange(count)[None, :]).astype(jnp.float32)
    before = jnp.dot(lower, onehot, precision=lax.Precision.HIGHEST)
    rank = jnp.sum(before * onehot, axis=1).astype(jnp.int32)
    return flat * capacity + rank


def capacity(tok_dev, half, expert_count):
    return min(2 * ((2 * tok_dev * half + 3 * expert_count - 1) // (3 * expert_count)), tok_dev)


def rms_terms(xf, probe):
    scale = lax.rsqrt(jnp.mean(xf * xf, axis=1, keepdims=True) + EPS)
    along = jnp.mean(xf * probe, axis=1, keepdims=True)
    return scale, along


def pack_kernel(expert_count, *refs):
    sources, pack, held, sems = (refs[:6], refs[6], refs[7:13], refs[13])
    copies = [
        pltpu.make_async_copy(source, target, sems.at[n])
        for n, (source, target) in enumerate(zip(sources, held))
    ]
    for copy in copies:
        copy.start()
    for copy in copies:
        copy.wait()
    tokens, gain, signs, cotangent, routes, gates = held
    width = tokens.shape[1]
    xf = tokens[...].astype(jnp.float32)
    probe = (2 * signs[...] - 1).astype(jnp.float32)
    scale, along = rms_terms(xf, probe)
    pack[:, :width] = (xf * scale * gain[...]).astype(jnp.bfloat16)
    tangent = gain[...] * (scale * probe - scale**3 * xf * along)
    pack[:, width : 2 * width] = tangent.astype(jnp.bfloat16)
    pack[:, 2 * width : 3 * width] = cotangent[...]
    lane = lax.broadcasted_iota(jnp.int32, (tokens.shape[0], pack.shape[1] - 3 * width), 1)
    expert = lax.rem(lane, expert_count)
    gate = jnp.zeros(lane.shape, jnp.float32)
    for group in range(routes.shape[0]):
        for slot in range(routes.shape[2]):
            named = routes[group, :, slot : slot + 1] == expert
            gate = gate + jnp.where(named, gates[group, :, slot : slot + 1], 0.0)
    high = gate.astype(jnp.bfloat16).astype(jnp.float32)
    tail = jnp.where(lane < expert_count, high, gate - high)
    tail = jnp.where(lane < 2 * expert_count, tail, 0.0)
    pack[:, 3 * width :] = tail.astype(jnp.bfloat16)


def packed(tokens, norm_gain, probe_signs, cotangent, routes, gates, expert_count):
    tok_dev, width = tokens.shape
    tail = -(-2 * expert_count // 128) * 128
    operands = (tokens, norm_gain.reshape(1, width), probe_signs, cotangent, routes, gates)
    return pl.pallas_call(
        functools.partial(pack_kernel, expert_count),
        out_shape=jax.ShapeDtypeStruct((tok_dev, 3 * width + tail), jnp.bfloat16),
        in_specs=[pl.BlockSpec(memory_space=pl.ANY)] * 6,
        out_specs=pl.BlockSpec(memory_space=pltpu.VMEM),
        scratch_shapes=[pltpu.VMEM(array.shape, array.dtype) for array in operands]
        + [pltpu.SemaphoreType.DMA((6,))],
        compiler_params=pltpu.CompilerParams(vmem_limit_bytes=VMEM_ALONE),
        cost_estimate=pl.CostEstimate(
            flops=20 * tok_dev * width, bytes_accessed=14 * tok_dev * width, transcendentals=0
        ),
    )(*operands)


def join_kernel(own, other, held, sems):
    half = own.shape[2]
    copies = [
        pltpu.make_async_copy(
            source.at[part], held.at[part, :, pl.ds(h * half, half)], sems.at[h, part]
        )
        for h, source in enumerate((own, other))
        for part in range(3)
    ]
    for copy in copies:
        copy.start()
    for copy in copies:
        copy.wait()


def joined(own, other):
    parts, width, half = own.shape
    return pl.pallas_call(
        join_kernel,
        out_shape=jax.ShapeDtypeStruct((parts, width, 2 * half), own.dtype),
        in_specs=[pl.BlockSpec(memory_space=pl.ANY)] * 2,
        out_specs=pl.BlockSpec(memory_space=pltpu.VMEM),
        scratch_shapes=[pltpu.SemaphoreType.DMA((2, parts))],
        compiler_params=pltpu.CompilerParams(vmem_limit_bytes=VMEM),
        cost_estimate=pl.CostEstimate(
            flops=0, bytes_accessed=8 * parts * width * half, transcendentals=0
        ),
    )(own, other)


def expert_kernel(count, expert_count, *refs):
    packs, held, outs = (refs[:count], refs[count], refs[count + 1 : 2 * count + 1])
    both, cotan, acc = refs[2 * count + 1 :]
    tok_dev = packs[0].shape[0]
    _, width, hidden = held.shape
    rows = count * tok_dev

    def stacked(start, size):
        return jnp.concatenate([p[:, start : start + size].astype(jnp.float32) for p in packs], 0)

    both[:rows, :] = stacked(0, width).astype(jnp.bfloat16)
    both[rows:, :] = stacked(width, width).astype(jnp.bfloat16)
    cotan[...] = stacked(2 * width, width).astype(jnp.bfloat16)
    tail = stacked(3 * width, packs[0].shape[1] - 3 * width)
    mine = lax.axis_index("expert") // 2
    lane = lax.broadcasted_iota(jnp.int32, tail.shape, 1)
    picked = (lane == mine) | (lane == mine + expert_count)
    gate_row = jnp.sum(jnp.where(picked, tail, 0.0), axis=1, keepdims=True)

    def weights(part, start, size):
        return held[part, :, start : start + size]

    block = 256 if hidden % 256 == 0 else 128
    contract = (((1,), (1,)), ((), ()))
    for start in range(0, hidden, block):
        pre_gate = jnp.dot(
            both[...], weights(0, start, block), preferred_element_type=jnp.float32
        )
        pre_up = jnp.dot(both[...], weights(1, start, block), preferred_element_type=jnp.float32)
        back = jnp.dot(cotan[...], weights(2, start, block), preferred_element_type=jnp.float32)
        gate, gate_t = (pre_gate[:rows], pre_gate[rows:])
        up, up_t = (pre_up[:rows], pre_up[rows:])
        sig = jax.nn.sigmoid(gate)
        act = gate * sig
        slope = sig * (1.0 + gate * (1.0 - sig))
        bend = sig * (1.0 - sig) * (2.0 + gate * (1.0 - 2.0 * sig))
        d_gate = (back * slope * up).astype(jnp.bfloat16)
        d_up = (back * act).astype(jnp.bfloat16)
        t_gate = (back * (bend * gate_t * up + slope * up_t)).astype(jnp.bfloat16)
        t_up = (back * slope * gate_t).astype(jnp.bfloat16)
        total = lax.dot_general(
            jnp.concatenate([d_gate, t_gate], 0),
            weights(0, start, block),
            contract,
            preferred_element_type=jnp.float32,
        )
        total = total + lax.dot_general(
            jnp.concatenate([d_up, t_up], 0),
            weights(1, start, block),
            contract,
            preferred_element_type=jnp.float32,
        )
        acc[...] = total if start == 0 else acc[...] + total
    for n in range(count):
        part = slice(n * tok_dev, (n + 1) * tok_dev)
        later = slice(rows + n * tok_dev, rows + (n + 1) * tok_dev)
        outs[n][:, :width] = (acc[part] * gate_row[part]).astype(outs[n].dtype)
        outs[n][:, width:] = (acc[later] * gate_row[part]).astype(outs[n].dtype)


def experts(packs, kind, weights, expert_count):
    count = len(packs)
    tok_dev = packs[0].shape[0]
    _, width, hidden = weights.shape
    rows = count * tok_dev
    whole = pl.BlockSpec(memory_space=pltpu.VMEM)
    return pl.pallas_call(
        functools.partial(expert_kernel, count, expert_count),
        out_shape=[jax.ShapeDtypeStruct((tok_dev, 2 * width), kind)] * count,
        in_specs=[whole] * (count + 1),
        out_specs=[whole] * count,
        scratch_shapes=[
            pltpu.VMEM((2 * rows, width), jnp.bfloat16),
            pltpu.VMEM((rows, width), jnp.bfloat16),
            pltpu.VMEM((2 * rows, width), jnp.float32),
        ],
        compiler_params=pltpu.CompilerParams(vmem_limit_bytes=VMEM),
        cost_estimate=pl.CostEstimate(
            flops=2 * 9 * rows * width * hidden,
            bytes_accessed=6 * width * hidden,
            transcendentals=rows * hidden,
        ),
    )(*packs, weights)


def finish_kernel(tokens, gain, signs, here, there, forward, backward, hvp, quad):
    width = tokens.shape[1]
    xf = tokens[...].astype(jnp.float32)
    probe = (2 * signs[...] - 1).astype(jnp.float32)
    scale, along = rms_terms(xf, probe)
    slope_r = -(scale**3) * along
    rows = here[...]
    for part in (there, forward, backward):
        rows = rows + part[...].astype(jnp.float32)
    lifted = gain[...] * rows[:, :width]
    lifted_t = gain[...] * rows[:, width:]
    first = jnp.mean(xf * lifted, axis=1, keepdims=True)
    second = jnp.mean(xf * lifted_t, axis=1, keepdims=True)
    third = jnp.mean(probe * lifted, axis=1, keepdims=True)
    whole = (
        scale * lifted_t
        + slope_r * lifted
        - 3.0 * scale**2 * slope_r * first * xf
        - scale**3 * first * probe
        - scale**3 * (second + third) * xf
    )
    hvp[...] = whole
    column = jnp.mean(probe * whole, axis=1, keepdims=True)
    tok_dev = column.shape[0]
    own = lax.broadcasted_iota(jnp.int32, (tok_dev, tok_dev), 0) == lax.broadcasted_iota(
        jnp.int32, (tok_dev, tok_dev), 1
    )
    quad[...] = jnp.sum(jnp.where(own, column, 0.0), axis=0, keepdims=True)


def moved(rows, turns, flip_x=False, flip_core=False):
    count = lax.axis_size("expert")
    pairs = [
        (i, (i + 4 * turns) % count ^ (2 * flip_x) ^ (1 * flip_core)) for i in range(count)
    ]
    return lax.ppermute(rows, "expert", pairs)


def dense_local(tokens, norm_gain, probe_signs, cotangent, routes, gates, weights):
    tok_dev, width = tokens.shape
    n_exp = lax.axis_size("expert")
    expert_count = n_exp // 2
    turns = n_exp // 4
    ahead, behind = turns // 2, (turns - 1) // 2
    pack = packed(tokens, norm_gain, probe_signs, cotangent, routes, gates, expert_count)
    same, across = {0: pack}, {}
    across[0] = moved(pack, 0, flip_x=True)
    weights_other = moved(weights, 0, flip_core=True)
    for k in range(1, ahead + 1):
        same[k] = moved(same[k - 1], 1)
        across[k] = moved(same[k], 0, flip_x=True)
    for k in range(turns - 1, turns - 1 - behind, -1):
        same[k] = moved(same[(k + 1) % turns], -1)
        across[k] = moved(same[k], 0, flip_x=True)
    order = range(turns)
    held = joined(weights, weights_other)
    results = experts([same[k] for k in order], jnp.float32, held, expert_count)
    here = dict(zip(order, results))
    packs = [across[k] for k in order]
    packs[0], here[0] = lax.optimization_barrier((packs[0], here[0]))
    results = experts(packs, jnp.bfloat16, held, expert_count)
    there = {k: moved(rows, 0, flip_x=True) for k, rows in zip(order, results)}

    def passed(ks, step):
        rows = None
        for k in ks:
            part = here[k] + there[k].astype(jnp.float32)
            part = part if rows is None else part + rows.astype(jnp.float32)
            rows = moved(part.astype(jnp.bfloat16), step)
        return rows

    forward = passed(range(ahead, 0, -1), -1)
    backward = passed(range(turns - behind, turns), 1)
    hvp, quad = pl.pallas_call(
        finish_kernel,
        out_shape=[
            jax.ShapeDtypeStruct((tok_dev, width), jnp.float32),
            jax.ShapeDtypeStruct((1, tok_dev), jnp.float32),
        ],
        compiler_params=pltpu.CompilerParams(vmem_limit_bytes=VMEM),
        cost_estimate=pl.CostEstimate(
            flops=40 * tok_dev * width, bytes_accessed=26 * tok_dev * width, transcendentals=0
        ),
    )(tokens, norm_gain.reshape(1, width), probe_signs, here[0], there[0], forward, backward)
    return (hvp, quad.reshape(tok_dev))


def routed_rows(normed, normed_t, cotangent, routes, gates, weights):
    tok_dev, width = normed.shape
    groups_here = routes.shape[0]
    half = routes.shape[2]
    n_exp = lax.axis_size("expert")
    expert_count = n_exp // 2
    cap = capacity(tok_dev, half, expert_count)
    buffer_rows = expert_count * cap
    stack_z, stack_t, stack_c, stack_w = ([], [], [], [])
    for group in range(groups_here):
        target = slot_targets(routes[group], expert_count, cap)
        place = (jnp.arange(buffer_rows, dtype=jnp.int32)[:, None] == target[None, :]).reshape(
            buffer_rows, tok_dev, half
        )
        place_tok = jnp.sum(place.astype(jnp.float32), axis=2).astype(jnp.bfloat16)
        stack_w.append(jnp.sum(place.astype(jnp.float32) * gates[group][None, :, :], axis=2))
        stack_z.append(
            jnp.dot(place_tok, normed, preferred_element_type=jnp.float32).astype(jnp.bfloat16)
        )
        stack_t.append(
            jnp.dot(place_tok, normed_t, preferred_element_type=jnp.float32).astype(jnp.bfloat16)
        )
        stack_c.append(
            jnp.dot(place_tok, cotangent, preferred_element_type=jnp.float32).astype(jnp.bfloat16)
        )
    rows_z = jnp.stack(stack_z, 0)
    rows_t = jnp.stack(stack_t, 0)
    rows_c = jnp.stack(stack_c, 0)
    weighted = jnp.stack(stack_w, 0)

    def arrange(rows):
        shaped = rows.reshape(groups_here, expert_count, 1, cap, width)
        shaped = jnp.broadcast_to(shaped, (groups_here, expert_count, 2, cap, width))
        return jnp.transpose(shaped, (1, 2, 0, 3, 4)).reshape(n_exp, groups_here * cap, width)

    send_z, send_t, send_c = (arrange(rows_z), arrange(rows_t), arrange(rows_c))
    got_z = lax.all_to_all(send_z, "expert", split_axis=0, concat_axis=0, tiled=True)
    got_t = lax.all_to_all(send_t, "expert", split_axis=0, concat_axis=0, tiled=True)
    got_c = lax.all_to_all(send_c, "expert", split_axis=0, concat_axis=0, tiled=True)
    sources, items, cols = got_z.shape
    g_rows, t_rows = expert_terms(
        weights, got_z.reshape(-1, cols), got_t.reshape(-1, cols), got_c.reshape(-1, cols)
    )
    g_rows = g_rows.reshape(sources, items, cols)
    t_rows = t_rows.reshape(sources, items, cols)
    back_g = lax.all_to_all(g_rows, "expert", split_axis=0, concat_axis=0, tiled=True)
    back_t = lax.all_to_all(t_rows, "expert", split_axis=0, concat_axis=0, tiled=True)

    def restore(rows):
        shaped = jnp.sum(rows.reshape(expert_count, 2, groups_here, cap, width), axis=1)
        return jnp.transpose(shaped, (1, 0, 2, 3)).reshape(groups_here, buffer_rows, width)

    back_g = restore(back_g)
    back_t = restore(back_t)
    contract = (((0, 1), (0, 1)), ((), ()))
    grad_z = lax.dot_general(weighted, back_g, contract, precision=lax.Precision.HIGHEST)
    tan_z = lax.dot_general(weighted, back_t, contract, precision=lax.Precision.HIGHEST)
    return (grad_z, tan_z)


def local(tokens, norm_gain, probe_signs, cotangent, routes, gates, expert_weights):
    cap = capacity(tokens.shape[0], routes.shape[2], lax.axis_size("expert") // 2)
    if lax.axis_size("node") == 1 and routes.shape[0] * cap >= tokens.shape[0]:
        return dense_local(
            tokens, norm_gain, probe_signs, cotangent, routes, gates, expert_weights
        )
    xf = tokens.astype(jnp.float32)
    probe = (2 * probe_signs - 1).astype(jnp.float32)
    tok_dev, width = xf.shape
    scale = lax.rsqrt(jnp.mean(xf * xf, axis=1, keepdims=True) + EPS)
    along = jnp.mean(xf * probe, axis=1, keepdims=True)
    normed = (xf * scale * norm_gain).astype(jnp.bfloat16)
    normed_t = (norm_gain * (scale * probe - scale**3 * xf * along)).astype(jnp.bfloat16)
    own_half = lax.all_gather(expert_weights, "node", axis=2, tiled=True)
    grad_z, tan_z = routed_rows(normed, normed_t, cotangent, routes, gates, own_half)
    share = width // lax.axis_size("node")
    start = lax.axis_index("node") * share
    slope_r = -(scale**3) * along
    grad_z, tan_z = lax.psum((grad_z, tan_z), "node")
    lifted = norm_gain * grad_z
    lifted_t = norm_gain * tan_z
    first = jnp.mean(xf * lifted, axis=1, keepdims=True)
    second = jnp.mean(xf * lifted_t, axis=1, keepdims=True)
    third = jnp.mean(probe * lifted, axis=1, keepdims=True)
    whole_hvp = (
        scale * lifted_t
        + slope_r * lifted
        - 3.0 * scale**2 * slope_r * first * xf
        - scale**3 * first * probe
        - scale**3 * (second + third) * xf
    )
    quad = jnp.mean(probe * whole_hvp, axis=1)
    hvp = lax.dynamic_slice_in_dim(whole_hvp, start, share, 1)
    return (hvp, quad)


def solution(mesh):
    placed = (
        P(("groups", "expert"), None),
        P(),
        P(("groups", "expert"), None),
        P(("groups", "expert"), None),
        P("node", ("groups", "expert"), None),
        P("node", ("groups", "expert"), None),
        P(None, None, ("expert", "node")),
    )
    return jax.shard_map(
        local,
        mesh=mesh,
        in_specs=placed,
        out_specs=(P(("groups", "expert"), "node"), P(("groups", "expert"))),
        check_vma=False,
    )
```

```python
import functools

import jax
import jax.numpy as jnp
from jax import lax
from jax.experimental import pallas as pl
from jax.experimental.pallas import tpu as pltpu
from jax.sharding import PartitionSpec as P

EPS = 1e-06
VMEM = 24 * 1024 * 1024


def expert_terms(weights, rows, rows_t, cotan):
    count = rows.shape[0]
    both = jnp.concatenate([rows, rows_t], 0)
    pre_gate = jnp.dot(both, weights[0], preferred_element_type=jnp.float32)
    pre_up = jnp.dot(both, weights[1], preferred_element_type=jnp.float32)
    gate, gate_t = (pre_gate[:count], pre_gate[count:])
    up, up_t = (pre_up[:count], pre_up[count:])
    back = jnp.dot(cotan, weights[2], preferred_element_type=jnp.float32)
    sig = jax.nn.sigmoid(gate)
    act = gate * sig
    slope = sig * (1.0 + gate * (1.0 - sig))
    bend = sig * (1.0 - sig) * (2.0 + gate * (1.0 - 2.0 * sig))
    d_gate = (back * slope * up).astype(jnp.bfloat16)
    d_up = (back * act).astype(jnp.bfloat16)
    t_gate = (back * (bend * gate_t * up + slope * up_t)).astype(jnp.bfloat16)
    t_up = (back * slope * gate_t).astype(jnp.bfloat16)
    contract = (((1,), (1,)), ((), ()))
    lhs_gate = jnp.concatenate([d_gate, t_gate], 0)
    lhs_up = jnp.concatenate([d_up, t_up], 0)
    total = lax.dot_general(lhs_gate, weights[0], contract, preferred_element_type=jnp.float32)
    total = total + lax.dot_general(
        lhs_up, weights[1], contract, preferred_element_type=jnp.float32
    )
    return (total[:count], total[count:])


def slot_targets(route_ids, expert_count, capacity):
    flat = route_ids.reshape(-1)
    count = flat.shape[0]
    onehot = (flat[:, None] == jnp.arange(expert_count, dtype=jnp.int32)[None, :]).astype(
        jnp.float32
    )
    lower = (jnp.arange(count)[:, None] > jnp.arange(count)[None, :]).astype(jnp.float32)
    before = jnp.dot(lower, onehot, precision=lax.Precision.HIGHEST)
    rank = jnp.sum(before * onehot, axis=1).astype(jnp.int32)
    return flat * capacity + rank


def capacity(tok_dev, half, expert_count):
    return min(2 * ((2 * tok_dev * half + 3 * expert_count - 1) // (3 * expert_count)), tok_dev)


def rms_terms(xf, probe):
    scale = lax.rsqrt(jnp.mean(xf * xf, axis=1, keepdims=True) + EPS)
    along = jnp.mean(xf * probe, axis=1, keepdims=True)
    return scale, along


def pack_kernel(expert_count, *refs):
    sources, pack, held, sems = (refs[:6], refs[6], refs[7:13], refs[13])
    copies = [
        pltpu.make_async_copy(source, target, sems.at[n])
        for n, (source, target) in enumerate(zip(sources, held))
    ]
    for copy in copies:
        copy.start()
    for copy in copies:
        copy.wait()
    tokens, gain, signs, cotangent, routes, gates = held
    width = tokens.shape[1]
    xf = tokens[...].astype(jnp.float32)
    probe = (2 * signs[...] - 1).astype(jnp.float32)
    scale, along = rms_terms(xf, probe)
    pack[:, :width] = (xf * scale * gain[...]).astype(jnp.bfloat16)
    tangent = gain[...] * (scale * probe - scale**3 * xf * along)
    pack[:, width : 2 * width] = tangent.astype(jnp.bfloat16)
    pack[:, 2 * width : 3 * width] = cotangent[...]
    tok_dev, lanes = (tokens.shape[0], pack.shape[1] - 3 * width)
    lane = lax.broadcasted_iota(jnp.int32, (lanes, tok_dev), 0)
    expert = lax.rem(lane, expert_count)
    gate = jnp.zeros(lane.shape, jnp.float32)
    for group in range(routes.shape[0]):
        for slot in range(routes.shape[1]):
            named = routes[group, slot : slot + 1, :] == expert
            gate = gate + jnp.where(named, gates[group, slot : slot + 1, :], 0.0)
    high = gate.astype(jnp.bfloat16).astype(jnp.float32)
    tail = jnp.where(lane < expert_count, high, gate - high)
    tail = jnp.where(lane < 2 * expert_count, tail, 0.0).astype(jnp.bfloat16)
    turned = lax.dot_general(
        identity(tok_dev).astype(jnp.bfloat16),
        tail,
        (((1,), (1,)), ((), ())),
        preferred_element_type=jnp.float32,
    )
    pack[:, 3 * width :] = turned.astype(jnp.bfloat16)


def identity(size):
    rows = lax.broadcasted_iota(jnp.int32, (size, size), 0)
    return (rows == lax.broadcasted_iota(jnp.int32, (size, size), 1)).astype(jnp.float32)


def packed(tokens, norm_gain, probe_signs, cotangent, routes, gates, expert_count):
    tok_dev, width = tokens.shape
    tail = -(-2 * expert_count // 128) * 128
    token_minor = (0, 2, 1)
    operands = (
        tokens,
        norm_gain.reshape(1, width),
        probe_signs,
        cotangent,
        jnp.transpose(routes, token_minor),
        jnp.transpose(gates, token_minor),
    )
    return pl.pallas_call(
        functools.partial(pack_kernel, expert_count),
        out_shape=jax.ShapeDtypeStruct((tok_dev, 3 * width + tail), jnp.bfloat16),
        in_specs=[pl.BlockSpec(memory_space=pl.ANY)] * 6,
        out_specs=pl.BlockSpec(memory_space=pltpu.VMEM),
        scratch_shapes=[pltpu.VMEM(array.shape, array.dtype) for array in operands]
        + [pltpu.SemaphoreType.DMA((6,))],
        compiler_params=pltpu.CompilerParams(vmem_limit_bytes=VMEM),
        cost_estimate=pl.CostEstimate(
            flops=20 * tok_dev * width, bytes_accessed=14 * tok_dev * width, transcendentals=0
        ),
    )(*(pltpu.with_memory_space_constraint(array, pltpu.HBM) for array in operands))


def join_kernel(own, other, held, sems):
    half = own.shape[2]
    copies = [
        pltpu.make_async_copy(
            source.at[part], held.at[part, :, pl.ds(h * half, half)], sems.at[h, part]
        )
        for h, source in enumerate((own, other))
        for part in range(3)
    ]
    for copy in copies:
        copy.start()
    for copy in copies:
        copy.wait()


def joined(own, other):
    parts, width, half = own.shape
    return pl.pallas_call(
        join_kernel,
        out_shape=pltpu.VMEM((parts, width, 2 * half), own.dtype),
        in_specs=[pl.BlockSpec(memory_space=pl.ANY)] * 2,
        out_specs=pl.BlockSpec(memory_space=pltpu.VMEM),
        scratch_shapes=[pltpu.SemaphoreType.DMA((2, parts))],
        compiler_params=pltpu.CompilerParams(vmem_limit_bytes=VMEM),
        cost_estimate=pl.CostEstimate(
            flops=0, bytes_accessed=8 * parts * width * half, transcendentals=0
        ),
    )(pltpu.with_memory_space_constraint(own, pltpu.HBM), other)


def expert_kernel(count, expert_count, *refs):
    packs, held, outs = (refs[:count], refs[count], refs[count + 1 : 2 * count + 1])
    both, cotan, acc = refs[2 * count + 1 :]
    tok_dev = packs[0].shape[0]
    _, width, hidden = held.shape
    rows = count * tok_dev

    def stacked(start, size):
        return jnp.concatenate([p[:, start : start + size].astype(jnp.float32) for p in packs], 0)

    both[:rows, :] = stacked(0, width).astype(jnp.bfloat16)
    both[rows:, :] = stacked(width, width).astype(jnp.bfloat16)
    cotan[...] = stacked(2 * width, width).astype(jnp.bfloat16)
    tail = stacked(3 * width, packs[0].shape[1] - 3 * width)
    mine = lax.axis_index("expert") // 2
    lane = lax.broadcasted_iota(jnp.int32, tail.shape, 1)
    picked = (lane == mine) | (lane == mine + expert_count)
    gate_row = jnp.sum(jnp.where(picked, tail, 0.0), axis=1, keepdims=True)

    def weights(part, start, size):
        return held[part, :, start : start + size]

    block = 256 if hidden % 256 == 0 else 128
    contract = (((1,), (1,)), ((), ()))
    for start in range(0, hidden, block):
        pre_gate = jnp.dot(
            both[...], weights(0, start, block), preferred_element_type=jnp.float32
        )
        pre_up = jnp.dot(both[...], weights(1, start, block), preferred_element_type=jnp.float32)
        back = jnp.dot(cotan[...], weights(2, start, block), preferred_element_type=jnp.float32)
        gate, gate_t = (pre_gate[:rows], pre_gate[rows:])
        up, up_t = (pre_up[:rows], pre_up[rows:])
        sig = jax.nn.sigmoid(gate)
        act = gate * sig
        slope = sig * (1.0 + gate * (1.0 - sig))
        bend = sig * (1.0 - sig) * (2.0 + gate * (1.0 - 2.0 * sig))
        d_gate = (back * slope * up).astype(jnp.bfloat16)
        d_up = (back * act).astype(jnp.bfloat16)
        t_gate = (back * (bend * gate_t * up + slope * up_t)).astype(jnp.bfloat16)
        t_up = (back * slope * gate_t).astype(jnp.bfloat16)
        total = lax.dot_general(
            jnp.concatenate([d_gate, t_gate], 0),
            weights(0, start, block),
            contract,
            preferred_element_type=jnp.float32,
        )
        total = total + lax.dot_general(
            jnp.concatenate([d_up, t_up], 0),
            weights(1, start, block),
            contract,
            preferred_element_type=jnp.float32,
        )
        acc[...] = total if start == 0 else acc[...] + total
    for n in range(count):
        part = slice(n * tok_dev, (n + 1) * tok_dev)
        later = slice(rows + n * tok_dev, rows + (n + 1) * tok_dev)
        outs[n][:, :width] = (acc[part] * gate_row[part]).astype(outs[n].dtype)
        outs[n][:, width:] = (acc[later] * gate_row[part]).astype(outs[n].dtype)


def experts(packs, kinds, held, expert_count):
    count = len(packs)
    tok_dev = packs[0].shape[0]
    _, width, hidden = held.shape
    rows = count * tok_dev
    whole = pl.BlockSpec(memory_space=pltpu.VMEM)
    return pl.pallas_call(
        functools.partial(expert_kernel, count, expert_count),
        out_shape=[jax.ShapeDtypeStruct((tok_dev, 2 * width), kind) for kind in kinds],
        in_specs=[whole] * (count + 1),
        out_specs=[whole] * count,
        scratch_shapes=[
            pltpu.VMEM((2 * rows, width), jnp.bfloat16),
            pltpu.VMEM((rows, width), jnp.bfloat16),
            pltpu.VMEM((2 * rows, width), jnp.float32),
        ],
        compiler_params=pltpu.CompilerParams(vmem_limit_bytes=VMEM),
        cost_estimate=pl.CostEstimate(
            flops=2 * 9 * rows * width * hidden,
            bytes_accessed=6 * width * hidden,
            transcendentals=rows * hidden,
        ),
    )(*packs, pltpu.with_memory_space_constraint(held, pltpu.VMEM))


def finish_kernel(tokens, gain, signs, here, there, forward, backward, hvp, quad):
    width = tokens.shape[1]
    xf = tokens[...].astype(jnp.float32)
    probe = (2 * signs[...] - 1).astype(jnp.float32)
    scale, along = rms_terms(xf, probe)
    slope_r = -(scale**3) * along
    rows = here[...]
    for part in (there, forward, backward):
        rows = rows + part[...].astype(jnp.float32)
    lifted = gain[...] * rows[:, :width]
    lifted_t = gain[...] * rows[:, width:]
    first = jnp.mean(xf * lifted, axis=1, keepdims=True)
    second = jnp.mean(xf * lifted_t, axis=1, keepdims=True)
    third = jnp.mean(probe * lifted, axis=1, keepdims=True)
    whole = (
        scale * lifted_t
        + slope_r * lifted
        - 3.0 * scale**2 * slope_r * first * xf
        - scale**3 * first * probe
        - scale**3 * (second + third) * xf
    )
    hvp[...] = whole
    column = jnp.mean(probe * whole, axis=1, keepdims=True)
    tok_dev = column.shape[0]
    quad[...] = jnp.sum(identity(tok_dev) * column, axis=0, keepdims=True)


def moved(rows, turns, flip_x=False, flip_core=False):
    count = lax.axis_size("expert")
    pairs = [
        (i, (i + 4 * turns) % count ^ (2 * flip_x) ^ (1 * flip_core)) for i in range(count)
    ]
    return lax.ppermute(rows, "expert", pairs)


def dense_local(tokens, norm_gain, probe_signs, cotangent, routes, gates, weights):
    tok_dev, width = tokens.shape
    n_exp = lax.axis_size("expert")
    expert_count = n_exp // 2
    pack = packed(tokens, norm_gain, probe_signs, cotangent, routes, gates, expert_count)
    held = joined(weights, moved(weights, 0, flip_core=True))
    same, across = {0: pack}, {}
    same[1] = moved(pack, 1)
    across[0] = moved(pack, 0, flip_x=True)
    same[1] = lax.optimization_barrier((same[1], across[0], held))[0]
    same[2] = moved(same[1], 1)
    across[1] = moved(same[1], 0, flip_x=True)
    same[3] = moved(lax.optimization_barrier((pack, same[1]))[0], -1)
    across[2] = moved(same[2], 0, flip_x=True)
    across[3] = moved(same[3], 0, flip_x=True)
    wide, sent = (jnp.float32, jnp.bfloat16)
    here, there = {}, {}
    here[0], here[1], here[2], here[3], there[0], there[1], there[2] = experts(
        [same[0], same[1], same[2], same[3], across[0], across[1], across[2]],
        [wide, wide, wide, sent, wide, sent, sent],
        held,
        expert_count,
    )
    last = lax.optimization_barrier((across[3], here[1]))[0]
    (there[3],) = experts([last], [sent], held, expert_count)

    def total(*parts):
        return sum(part.astype(jnp.float32) for part in parts).astype(jnp.bfloat16)

    backward = moved(here[3], 1)
    forward = moved(total(here[2], moved(there[2], 0, flip_x=True)), -1)
    forward = moved(total(here[1], moved(there[1], 0, flip_x=True), forward), -1)
    beside = moved(total(there[0], moved(there[3], 1)), 0, flip_x=True)
    hvp, quad = pl.pallas_call(
        finish_kernel,
        out_shape=[
            jax.ShapeDtypeStruct((tok_dev, width), jnp.float32),
            jax.ShapeDtypeStruct((1, tok_dev), jnp.float32),
        ],
        compiler_params=pltpu.CompilerParams(vmem_limit_bytes=VMEM),
        cost_estimate=pl.CostEstimate(
            flops=40 * tok_dev * width, bytes_accessed=26 * tok_dev * width, transcendentals=0
        ),
    )(tokens, norm_gain.reshape(1, width), probe_signs, here[0], beside, forward, backward)
    return (hvp, quad.reshape(tok_dev))


def routed_rows(normed, normed_t, cotangent, routes, gates, weights):
    tok_dev, width = normed.shape
    groups_here = routes.shape[0]
    half = routes.shape[2]
    n_exp = lax.axis_size("expert")
    expert_count = n_exp // 2
    cap = capacity(tok_dev, half, expert_count)
    buffer_rows = expert_count * cap
    stack_z, stack_t, stack_c, stack_w = ([], [], [], [])
    for group in range(groups_here):
        target = slot_targets(routes[group], expert_count, cap)
        place = (jnp.arange(buffer_rows, dtype=jnp.int32)[:, None] == target[None, :]).reshape(
            buffer_rows, tok_dev, half
        )
        place_tok = jnp.sum(place.astype(jnp.float32), axis=2).astype(jnp.bfloat16)
        stack_w.append(jnp.sum(place.astype(jnp.float32) * gates[group][None, :, :], axis=2))
        stack_z.append(
            jnp.dot(place_tok, normed, preferred_element_type=jnp.float32).astype(jnp.bfloat16)
        )
        stack_t.append(
            jnp.dot(place_tok, normed_t, preferred_element_type=jnp.float32).astype(jnp.bfloat16)
        )
        stack_c.append(
            jnp.dot(place_tok, cotangent, preferred_element_type=jnp.float32).astype(jnp.bfloat16)
        )
    rows_z = jnp.stack(stack_z, 0)
    rows_t = jnp.stack(stack_t, 0)
    rows_c = jnp.stack(stack_c, 0)
    weighted = jnp.stack(stack_w, 0)

    def arrange(rows):
        shaped = rows.reshape(groups_here, expert_count, 1, cap, width)
        shaped = jnp.broadcast_to(shaped, (groups_here, expert_count, 2, cap, width))
        return jnp.transpose(shaped, (1, 2, 0, 3, 4)).reshape(n_exp, groups_here * cap, width)

    send_z, send_t, send_c = (arrange(rows_z), arrange(rows_t), arrange(rows_c))
    got_z = lax.all_to_all(send_z, "expert", split_axis=0, concat_axis=0, tiled=True)
    got_t = lax.all_to_all(send_t, "expert", split_axis=0, concat_axis=0, tiled=True)
    got_c = lax.all_to_all(send_c, "expert", split_axis=0, concat_axis=0, tiled=True)
    sources, items, cols = got_z.shape
    g_rows, t_rows = expert_terms(
        weights, got_z.reshape(-1, cols), got_t.reshape(-1, cols), got_c.reshape(-1, cols)
    )
    g_rows = g_rows.reshape(sources, items, cols)
    t_rows = t_rows.reshape(sources, items, cols)
    back_g = lax.all_to_all(g_rows, "expert", split_axis=0, concat_axis=0, tiled=True)
    back_t = lax.all_to_all(t_rows, "expert", split_axis=0, concat_axis=0, tiled=True)

    def restore(rows):
        shaped = jnp.sum(rows.reshape(expert_count, 2, groups_here, cap, width), axis=1)
        return jnp.transpose(shaped, (1, 0, 2, 3)).reshape(groups_here, buffer_rows, width)

    back_g = restore(back_g)
    back_t = restore(back_t)
    contract = (((0, 1), (0, 1)), ((), ()))
    grad_z = lax.dot_general(weighted, back_g, contract, precision=lax.Precision.HIGHEST)
    tan_z = lax.dot_general(weighted, back_t, contract, precision=lax.Precision.HIGHEST)
    return (grad_z, tan_z)


def local(tokens, norm_gain, probe_signs, cotangent, routes, gates, expert_weights):
    cap = capacity(tokens.shape[0], routes.shape[2], lax.axis_size("expert") // 2)
    layout = (lax.axis_size("expert"), lax.axis_size("node"))
    if layout == (16, 1) and routes.shape[0] * cap >= tokens.shape[0]:
        return dense_local(
            tokens, norm_gain, probe_signs, cotangent, routes, gates, expert_weights
        )
    xf = tokens.astype(jnp.float32)
    probe = (2 * probe_signs - 1).astype(jnp.float32)
    tok_dev, width = xf.shape
    scale = lax.rsqrt(jnp.mean(xf * xf, axis=1, keepdims=True) + EPS)
    along = jnp.mean(xf * probe, axis=1, keepdims=True)
    normed = (xf * scale * norm_gain).astype(jnp.bfloat16)
    normed_t = (norm_gain * (scale * probe - scale**3 * xf * along)).astype(jnp.bfloat16)
    own_half = lax.all_gather(expert_weights, "node", axis=2, tiled=True)
    grad_z, tan_z = routed_rows(normed, normed_t, cotangent, routes, gates, own_half)
    share = width // lax.axis_size("node")
    start = lax.axis_index("node") * share
    slope_r = -(scale**3) * along
    grad_z, tan_z = lax.psum((grad_z, tan_z), "node")
    lifted = norm_gain * grad_z
    lifted_t = norm_gain * tan_z
    first = jnp.mean(xf * lifted, axis=1, keepdims=True)
    second = jnp.mean(xf * lifted_t, axis=1, keepdims=True)
    third = jnp.mean(probe * lifted, axis=1, keepdims=True)
    whole_hvp = (
        scale * lifted_t
        + slope_r * lifted
        - 3.0 * scale**2 * slope_r * first * xf
        - scale**3 * first * probe
        - scale**3 * (second + third) * xf
    )
    quad = jnp.mean(probe * whole_hvp, axis=1)
    hvp = lax.dynamic_slice_in_dim(whole_hvp, start, share, 1)
    return (hvp, quad)


def solution(mesh):
    placed = (
        P(("groups", "expert"), None),
        P(),
        P(("groups", "expert"), None),
        P(("groups", "expert"), None),
        P("node", ("groups", "expert"), None),
        P("node", ("groups", "expert"), None),
        P(None, None, ("expert", "node")),
    )
    return jax.shard_map(
        local,
        mesh=mesh,
        in_specs=placed,
        out_specs=(P(("groups", "expert"), "node"), P(("groups", "expert"))),
        check_vma=False,
    )
```

```python
import functools

import jax
import jax.numpy as jnp
from jax import lax
from jax.experimental import pallas as pl
from jax.experimental.pallas import tpu as pltpu
from jax.sharding import PartitionSpec as P

EPS = 1e-06
VMEM = 24 * 1024 * 1024


def expert_terms(weights, rows, rows_t, cotan):
    count = rows.shape[0]
    both = jnp.concatenate([rows, rows_t], 0)
    pre_gate = jnp.dot(both, weights[0], preferred_element_type=jnp.float32)
    pre_up = jnp.dot(both, weights[1], preferred_element_type=jnp.float32)
    gate, gate_t = (pre_gate[:count], pre_gate[count:])
    up, up_t = (pre_up[:count], pre_up[count:])
    back = jnp.dot(cotan, weights[2], preferred_element_type=jnp.float32)
    sig = jax.nn.sigmoid(gate)
    act = gate * sig
    slope = sig * (1.0 + gate * (1.0 - sig))
    bend = sig * (1.0 - sig) * (2.0 + gate * (1.0 - 2.0 * sig))
    d_gate = (back * slope * up).astype(jnp.bfloat16)
    d_up = (back * act).astype(jnp.bfloat16)
    t_gate = (back * (bend * gate_t * up + slope * up_t)).astype(jnp.bfloat16)
    t_up = (back * slope * gate_t).astype(jnp.bfloat16)
    contract = (((1,), (1,)), ((), ()))
    lhs_gate = jnp.concatenate([d_gate, t_gate], 0)
    lhs_up = jnp.concatenate([d_up, t_up], 0)
    total = lax.dot_general(lhs_gate, weights[0], contract, preferred_element_type=jnp.float32)
    total = total + lax.dot_general(
        lhs_up, weights[1], contract, preferred_element_type=jnp.float32
    )
    return (total[:count], total[count:])


def slot_targets(route_ids, expert_count, capacity):
    flat = route_ids.reshape(-1)
    count = flat.shape[0]
    onehot = (flat[:, None] == jnp.arange(expert_count, dtype=jnp.int32)[None, :]).astype(
        jnp.float32
    )
    lower = (jnp.arange(count)[:, None] > jnp.arange(count)[None, :]).astype(jnp.float32)
    before = jnp.dot(lower, onehot, precision=lax.Precision.HIGHEST)
    rank = jnp.sum(before * onehot, axis=1).astype(jnp.int32)
    return flat * capacity + rank


def capacity(tok_dev, half, expert_count):
    return min(2 * ((2 * tok_dev * half + 3 * expert_count - 1) // (3 * expert_count)), tok_dev)


def rms_terms(xf, probe):
    scale = lax.rsqrt(jnp.mean(xf * xf, axis=1, keepdims=True) + EPS)
    along = jnp.mean(xf * probe, axis=1, keepdims=True)
    return scale, along


def pack_kernel(expert_count, *refs):
    sources, pack, held, sems = (refs[:6], refs[6], refs[7:13], refs[13])
    copies = [
        pltpu.make_async_copy(source, target, sems.at[n])
        for n, (source, target) in enumerate(zip(sources, held))
    ]
    for copy in copies:
        copy.start()
    for copy in copies:
        copy.wait()
    tokens, gain, signs, cotangent, routes, gates = held
    width = tokens.shape[1]
    xf = tokens[...].astype(jnp.float32)
    probe = (2 * signs[...] - 1).astype(jnp.float32)
    scale, along = rms_terms(xf, probe)
    pack[:, :width] = (xf * scale * gain[...]).astype(jnp.bfloat16)
    tangent = gain[...] * (scale * probe - scale**3 * xf * along)
    pack[:, width : 2 * width] = tangent.astype(jnp.bfloat16)
    pack[:, 2 * width : 3 * width] = cotangent[...]
    tok_dev, lanes = (tokens.shape[0], pack.shape[1] - 3 * width)
    lane = lax.broadcasted_iota(jnp.int32, (lanes, tok_dev), 0)
    expert = lax.rem(lane, expert_count)
    gate = jnp.zeros(lane.shape, jnp.float32)
    for group in range(routes.shape[0]):
        for slot in range(routes.shape[1]):
            named = routes[group, slot : slot + 1, :] == expert
            gate = gate + jnp.where(named, gates[group, slot : slot + 1, :], 0.0)
    high = gate.astype(jnp.bfloat16).astype(jnp.float32)
    tail = jnp.where(lane < expert_count, high, gate - high)
    tail = jnp.where(lane < 2 * expert_count, tail, 0.0).astype(jnp.bfloat16)
    turned = lax.dot_general(
        identity(tok_dev).astype(jnp.bfloat16),
        tail,
        (((1,), (1,)), ((), ())),
        preferred_element_type=jnp.float32,
    )
    lane = lax.broadcasted_iota(jnp.int32, (tok_dev, lanes), 1)
    place = 2 * expert_count
    for number in (scale, -(scale**3) * along):
        for _ in range(3):
            addend = number.astype(jnp.bfloat16).astype(jnp.float32)
            turned = jnp.where(lane == place, addend, turned)
            number = number - addend
            place += 1
    pack[:, 3 * width :] = turned.astype(jnp.bfloat16)


def identity(size):
    rows = lax.broadcasted_iota(jnp.int32, (size, size), 0)
    return (rows == lax.broadcasted_iota(jnp.int32, (size, size), 1)).astype(jnp.float32)


def packed(tokens, norm_gain, probe_signs, cotangent, routes, gates, expert_count):
    tok_dev, width = tokens.shape
    tail = -(-(2 * expert_count + 6) // 128) * 128
    token_minor = (0, 2, 1)
    operands = (
        tokens,
        norm_gain.reshape(1, width),
        probe_signs,
        cotangent,
        jnp.transpose(routes, token_minor),
        jnp.transpose(gates, token_minor),
    )
    return pl.pallas_call(
        functools.partial(pack_kernel, expert_count),
        out_shape=jax.ShapeDtypeStruct((tok_dev, 3 * width + tail), jnp.bfloat16),
        in_specs=[pl.BlockSpec(memory_space=pl.ANY)] * 6,
        out_specs=pl.BlockSpec(memory_space=pltpu.VMEM),
        scratch_shapes=[pltpu.VMEM(array.shape, array.dtype) for array in operands]
        + [pltpu.SemaphoreType.DMA((6,))],
        compiler_params=pltpu.CompilerParams(vmem_limit_bytes=VMEM),
        cost_estimate=pl.CostEstimate(
            flops=20 * tok_dev * width, bytes_accessed=14 * tok_dev * width, transcendentals=0
        ),
    )(*(pltpu.with_memory_space_constraint(array, pltpu.HBM) for array in operands))


def join_kernel(own, other, held, sems):
    half = own.shape[2]
    copies = [
        pltpu.make_async_copy(
            source.at[part], held.at[part, :, pl.ds(h * half, half)], sems.at[h, part]
        )
        for h, source in enumerate((own, other))
        for part in range(3)
    ]
    for copy in copies:
        copy.start()
    for copy in copies:
        copy.wait()


def joined(own, other):
    parts, width, half = own.shape
    return pl.pallas_call(
        join_kernel,
        out_shape=pltpu.VMEM((parts, width, 2 * half), own.dtype),
        in_specs=[pl.BlockSpec(memory_space=pl.ANY)] * 2,
        out_specs=pl.BlockSpec(memory_space=pltpu.VMEM),
        scratch_shapes=[pltpu.SemaphoreType.DMA((2, parts))],
        compiler_params=pltpu.CompilerParams(vmem_limit_bytes=VMEM),
        cost_estimate=pl.CostEstimate(
            flops=0, bytes_accessed=8 * parts * width * half, transcendentals=0
        ),
    )(pltpu.with_memory_space_constraint(own, pltpu.HBM), other)


def expert_kernel(count, expert_count, *refs):
    packs, held, outs = (refs[:count], refs[count], refs[count + 1 : 2 * count + 1])
    both, cotan, acc = refs[2 * count + 1 :]
    tok_dev = packs[0].shape[0]
    _, width, hidden = held.shape
    rows = count * tok_dev

    def stacked(start, size):
        return jnp.concatenate([p[:, start : start + size].astype(jnp.float32) for p in packs], 0)

    both[:rows, :] = stacked(0, width).astype(jnp.bfloat16)
    both[rows:, :] = stacked(width, width).astype(jnp.bfloat16)
    cotan[...] = stacked(2 * width, width).astype(jnp.bfloat16)
    tail = stacked(3 * width, packs[0].shape[1] - 3 * width)
    mine = lax.axis_index("expert") // 2
    lane = lax.broadcasted_iota(jnp.int32, tail.shape, 1)
    after = 2 * expert_count

    def picked(lanes):
        return jnp.sum(jnp.where(lanes, tail, 0.0), axis=1, keepdims=True)

    gate_row = picked((lane == mine) | (lane == mine + expert_count))
    scale_row = picked((lane >= after) & (lane < after + 3))
    slope_row = picked((lane >= after + 3) & (lane < after + 6))

    def weights(part, start, size):
        return held[part, :, start : start + size]

    block = 256 if hidden % 256 == 0 else 128
    contract = (((1,), (1,)), ((), ()))
    for start in range(0, hidden, block):
        pre_gate = jnp.dot(
            both[...], weights(0, start, block), preferred_element_type=jnp.float32
        )
        pre_up = jnp.dot(both[...], weights(1, start, block), preferred_element_type=jnp.float32)
        back = jnp.dot(cotan[...], weights(2, start, block), preferred_element_type=jnp.float32)
        gate, gate_t = (pre_gate[:rows], pre_gate[rows:])
        up, up_t = (pre_up[:rows], pre_up[rows:])
        sig = jax.nn.sigmoid(gate)
        act = gate * sig
        slope = sig * (1.0 + gate * (1.0 - sig))
        bend = sig * (1.0 - sig) * (2.0 + gate * (1.0 - 2.0 * sig))
        d_gate = (back * slope * up).astype(jnp.bfloat16)
        d_up = (back * act).astype(jnp.bfloat16)
        t_gate = (back * (bend * gate_t * up + slope * up_t)).astype(jnp.bfloat16)
        t_up = (back * slope * gate_t).astype(jnp.bfloat16)
        total = lax.dot_general(
            jnp.concatenate([d_gate, t_gate], 0),
            weights(0, start, block),
            contract,
            preferred_element_type=jnp.float32,
        )
        total = total + lax.dot_general(
            jnp.concatenate([d_up, t_up], 0),
            weights(1, start, block),
            contract,
            preferred_element_type=jnp.float32,
        )
        acc[...] = total if start == 0 else acc[...] + total
    for n in range(count):
        part = slice(n * tok_dev, (n + 1) * tok_dev)
        later = slice(rows + n * tok_dev, rows + (n + 1) * tok_dev)
        grad, tan = (acc[part] * gate_row[part], acc[later] * gate_row[part])
        scale, slope_r = (scale_row[part], slope_row[part])
        normed = packs[n][:, :width].astype(jnp.float32)
        normed_t = packs[n][:, width : 2 * width].astype(jnp.float32)
        outs[n][:, :width] = (scale * tan + slope_r * grad).astype(outs[n].dtype)
        first = jnp.mean(normed * grad, axis=1, keepdims=True)
        second = jnp.mean(normed * tan + normed_t * grad, axis=1, keepdims=True)
        second = (second - slope_r / scale * first) / scale
        lane = lax.broadcasted_iota(jnp.int32, (tok_dev, outs[n].shape[1] - width), 1)
        sums = jnp.where(lane == 0, first / scale, jnp.where(lane == 1, second, 0.0))
        outs[n][:, width:] = sums.astype(outs[n].dtype)


def experts(packs, kinds, held, expert_count):
    count = len(packs)
    tok_dev = packs[0].shape[0]
    _, width, hidden = held.shape
    rows = count * tok_dev
    whole = pl.BlockSpec(memory_space=pltpu.VMEM)
    return pl.pallas_call(
        functools.partial(expert_kernel, count, expert_count),
        out_shape=[jax.ShapeDtypeStruct((tok_dev, width + 128), kind) for kind in kinds],
        in_specs=[whole] * (count + 1),
        out_specs=[whole] * count,
        scratch_shapes=[
            pltpu.VMEM((2 * rows, width), jnp.bfloat16),
            pltpu.VMEM((rows, width), jnp.bfloat16),
            pltpu.VMEM((2 * rows, width), jnp.float32),
        ],
        compiler_params=pltpu.CompilerParams(vmem_limit_bytes=VMEM),
        cost_estimate=pl.CostEstimate(
            flops=2 * 9 * rows * width * hidden,
            bytes_accessed=6 * width * hidden,
            transcendentals=rows * hidden,
        ),
    )(*packs, pltpu.with_memory_space_constraint(held, pltpu.VMEM))


def finish_kernel(tokens, gain, signs, here, there, forward, backward, hvp, quad):
    width = tokens.shape[1]
    xf = tokens[...].astype(jnp.float32)
    probe = (2 * signs[...] - 1).astype(jnp.float32)
    scale, along = rms_terms(xf, probe)
    slope_r = -(scale**3) * along
    rows = here[...]
    for part in (there, forward, backward):
        rows = rows + part[...].astype(jnp.float32)
    first = rows[:, width : width + 1]
    second = rows[:, width + 1 : width + 2]
    whole = (
        gain[...] * rows[:, :width]
        - 3.0 * scale**2 * slope_r * first * xf
        - scale**3 * first * probe
        - scale**3 * second * xf
    )
    hvp[...] = whole
    column = jnp.mean(probe * whole, axis=1, keepdims=True)
    tok_dev = column.shape[0]
    quad[...] = jnp.sum(identity(tok_dev) * column, axis=0, keepdims=True)


def moved(rows, turns, flip_x=False, flip_core=False):
    count = lax.axis_size("expert")
    pairs = [
        (i, (i + 4 * turns) % count ^ (2 * flip_x) ^ (1 * flip_core)) for i in range(count)
    ]
    return lax.ppermute(rows, "expert", pairs)


def dense_local(tokens, norm_gain, probe_signs, cotangent, routes, gates, weights):
    tok_dev, width = tokens.shape
    n_exp = lax.axis_size("expert")
    expert_count = n_exp // 2
    pack = packed(tokens, norm_gain, probe_signs, cotangent, routes, gates, expert_count)
    held = joined(weights, moved(weights, 0, flip_core=True))
    same, across = {0: pack}, {}
    same[1] = moved(pack, 1)
    across[0] = moved(pack, 0, flip_x=True)
    same[1] = lax.optimization_barrier((same[1], across[0], held))[0]
    same[2] = moved(same[1], 1)
    across[1] = moved(same[1], 0, flip_x=True)
    same[3] = moved(lax.optimization_barrier((pack, same[1]))[0], -1)
    across[2] = moved(same[2], 0, flip_x=True)
    across[3] = moved(lax.optimization_barrier((across[0], same[2]))[0], -1)
    wide, sent = (jnp.float32, jnp.bfloat16)
    here, there = {}, {}
    here[0], here[1], here[2], here[3], there[0], there[1], there[2] = experts(
        [same[0], same[1], same[2], same[3], across[0], across[1], across[2]],
        [wide, wide, wide, wide, sent, sent, sent],
        held,
        expert_count,
    )
    last = lax.optimization_barrier((across[3], here[1]))[0]
    (there[3],) = experts([last], [sent], held, expert_count)

    def total(*parts):
        return sum(part.astype(jnp.float32) for part in parts).astype(jnp.bfloat16)

    beside = {k: moved(there[k], 0, flip_x=True) for k in (2, 1, 3, 0)}
    backward = moved(total(here[3], beside[3]), 1)
    forward = moved(total(here[2], beside[2]), -1)
    forward = moved(total(here[1], beside[1], forward), -1)
    hvp, quad = pl.pallas_call(
        finish_kernel,
        out_shape=[
            jax.ShapeDtypeStruct((tok_dev, width), jnp.float32),
            jax.ShapeDtypeStruct((1, tok_dev), jnp.float32),
        ],
        compiler_params=pltpu.CompilerParams(vmem_limit_bytes=VMEM),
        cost_estimate=pl.CostEstimate(
            flops=40 * tok_dev * width, bytes_accessed=26 * tok_dev * width, transcendentals=0
        ),
    )(tokens, norm_gain.reshape(1, width), probe_signs, here[0], beside[0], forward, backward)
    return (hvp, quad.reshape(tok_dev))


def routed_rows(normed, normed_t, cotangent, routes, gates, weights):
    tok_dev, width = normed.shape
    groups_here = routes.shape[0]
    half = routes.shape[2]
    n_exp = lax.axis_size("expert")
    expert_count = n_exp // 2
    cap = capacity(tok_dev, half, expert_count)
    buffer_rows = expert_count * cap
    stack_z, stack_t, stack_c, stack_w = ([], [], [], [])
    for group in range(groups_here):
        target = slot_targets(routes[group], expert_count, cap)
        place = (jnp.arange(buffer_rows, dtype=jnp.int32)[:, None] == target[None, :]).reshape(
            buffer_rows, tok_dev, half
        )
        place_tok = jnp.sum(place.astype(jnp.float32), axis=2).astype(jnp.bfloat16)
        stack_w.append(jnp.sum(place.astype(jnp.float32) * gates[group][None, :, :], axis=2))
        stack_z.append(
            jnp.dot(place_tok, normed, preferred_element_type=jnp.float32).astype(jnp.bfloat16)
        )
        stack_t.append(
            jnp.dot(place_tok, normed_t, preferred_element_type=jnp.float32).astype(jnp.bfloat16)
        )
        stack_c.append(
            jnp.dot(place_tok, cotangent, preferred_element_type=jnp.float32).astype(jnp.bfloat16)
        )
    rows_z = jnp.stack(stack_z, 0)
    rows_t = jnp.stack(stack_t, 0)
    rows_c = jnp.stack(stack_c, 0)
    weighted = jnp.stack(stack_w, 0)

    def arrange(rows):
        shaped = rows.reshape(groups_here, expert_count, 1, cap, width)
        shaped = jnp.broadcast_to(shaped, (groups_here, expert_count, 2, cap, width))
        return jnp.transpose(shaped, (1, 2, 0, 3, 4)).reshape(n_exp, groups_here * cap, width)

    send_z, send_t, send_c = (arrange(rows_z), arrange(rows_t), arrange(rows_c))
    got_z = lax.all_to_all(send_z, "expert", split_axis=0, concat_axis=0, tiled=True)
    got_t = lax.all_to_all(send_t, "expert", split_axis=0, concat_axis=0, tiled=True)
    got_c = lax.all_to_all(send_c, "expert", split_axis=0, concat_axis=0, tiled=True)
    sources, items, cols = got_z.shape
    g_rows, t_rows = expert_terms(
        weights, got_z.reshape(-1, cols), got_t.reshape(-1, cols), got_c.reshape(-1, cols)
    )
    g_rows = g_rows.reshape(sources, items, cols)
    t_rows = t_rows.reshape(sources, items, cols)
    back_g = lax.all_to_all(g_rows, "expert", split_axis=0, concat_axis=0, tiled=True)
    back_t = lax.all_to_all(t_rows, "expert", split_axis=0, concat_axis=0, tiled=True)

    def restore(rows):
        shaped = jnp.sum(rows.reshape(expert_count, 2, groups_here, cap, width), axis=1)
        return jnp.transpose(shaped, (1, 0, 2, 3)).reshape(groups_here, buffer_rows, width)

    back_g = restore(back_g)
    back_t = restore(back_t)
    contract = (((0, 1), (0, 1)), ((), ()))
    grad_z = lax.dot_general(weighted, back_g, contract, precision=lax.Precision.HIGHEST)
    tan_z = lax.dot_general(weighted, back_t, contract, precision=lax.Precision.HIGHEST)
    return (grad_z, tan_z)


def local(tokens, norm_gain, probe_signs, cotangent, routes, gates, expert_weights):
    cap = capacity(tokens.shape[0], routes.shape[2], lax.axis_size("expert") // 2)
    layout = (lax.axis_size("expert"), lax.axis_size("node"))
    if layout == (16, 1) and routes.shape[0] * cap >= tokens.shape[0]:
        return dense_local(
            tokens, norm_gain, probe_signs, cotangent, routes, gates, expert_weights
        )
    xf = tokens.astype(jnp.float32)
    probe = (2 * probe_signs - 1).astype(jnp.float32)
    tok_dev, width = xf.shape
    scale = lax.rsqrt(jnp.mean(xf * xf, axis=1, keepdims=True) + EPS)
    along = jnp.mean(xf * probe, axis=1, keepdims=True)
    normed = (xf * scale * norm_gain).astype(jnp.bfloat16)
    normed_t = (norm_gain * (scale * probe - scale**3 * xf * along)).astype(jnp.bfloat16)
    own_half = lax.all_gather(expert_weights, "node", axis=2, tiled=True)
    grad_z, tan_z = routed_rows(normed, normed_t, cotangent, routes, gates, own_half)
    share = width // lax.axis_size("node")
    start = lax.axis_index("node") * share
    slope_r = -(scale**3) * along
    grad_z, tan_z = lax.psum((grad_z, tan_z), "node")
    lifted = norm_gain * grad_z
    lifted_t = norm_gain * tan_z
    first = jnp.mean(xf * lifted, axis=1, keepdims=True)
    second = jnp.mean(xf * lifted_t, axis=1, keepdims=True)
    third = jnp.mean(probe * lifted, axis=1, keepdims=True)
    whole_hvp = (
        scale * lifted_t
        + slope_r * lifted
        - 3.0 * scale**2 * slope_r * first * xf
        - scale**3 * first * probe
        - scale**3 * (second + third) * xf
    )
    quad = jnp.mean(probe * whole_hvp, axis=1)
    hvp = lax.dynamic_slice_in_dim(whole_hvp, start, share, 1)
    return (hvp, quad)


def solution(mesh):
    placed = (
        P(("groups", "expert"), None),
        P(),
        P(("groups", "expert"), None),
        P(("groups", "expert"), None),
        P("node", ("groups", "expert"), None),
        P("node", ("groups", "expert"), None),
        P(None, None, ("expert", "node")),
    )
    return jax.shard_map(
        local,
        mesh=mesh,
        in_specs=placed,
        out_specs=(P(("groups", "expert"), "node"), P(("groups", "expert"))),
        check_vma=False,
    )
```

```python
import functools

import jax
import jax.numpy as jnp
from jax import lax
from jax.experimental import pallas as pl
from jax.experimental.pallas import tpu as pltpu
from jax.sharding import PartitionSpec as P

EPS = 1e-06
VMEM = 24 * 1024 * 1024


def expert_terms(weights, rows, rows_t, cotan):
    count = rows.shape[0]
    both = jnp.concatenate([rows, rows_t], 0)
    pre_gate = jnp.dot(both, weights[0], preferred_element_type=jnp.float32)
    pre_up = jnp.dot(both, weights[1], preferred_element_type=jnp.float32)
    gate, gate_t = (pre_gate[:count], pre_gate[count:])
    up, up_t = (pre_up[:count], pre_up[count:])
    back = jnp.dot(cotan, weights[2], preferred_element_type=jnp.float32)
    sig = jax.nn.sigmoid(gate)
    act = gate * sig
    slope = sig * (1.0 + gate * (1.0 - sig))
    bend = sig * (1.0 - sig) * (2.0 + gate * (1.0 - 2.0 * sig))
    d_gate = (back * slope * up).astype(jnp.bfloat16)
    d_up = (back * act).astype(jnp.bfloat16)
    t_gate = (back * (bend * gate_t * up + slope * up_t)).astype(jnp.bfloat16)
    t_up = (back * slope * gate_t).astype(jnp.bfloat16)
    contract = (((1,), (1,)), ((), ()))
    lhs_gate = jnp.concatenate([d_gate, t_gate], 0)
    lhs_up = jnp.concatenate([d_up, t_up], 0)
    total = lax.dot_general(lhs_gate, weights[0], contract, preferred_element_type=jnp.float32)
    total = total + lax.dot_general(
        lhs_up, weights[1], contract, preferred_element_type=jnp.float32
    )
    return (total[:count], total[count:])


def slot_targets(route_ids, expert_count, capacity):
    flat = route_ids.reshape(-1)
    count = flat.shape[0]
    onehot = (flat[:, None] == jnp.arange(expert_count, dtype=jnp.int32)[None, :]).astype(
        jnp.float32
    )
    lower = (jnp.arange(count)[:, None] > jnp.arange(count)[None, :]).astype(jnp.float32)
    before = jnp.dot(lower, onehot, precision=lax.Precision.HIGHEST)
    rank = jnp.sum(before * onehot, axis=1).astype(jnp.int32)
    return flat * capacity + rank


def capacity(tok_dev, half, expert_count):
    return min(2 * ((2 * tok_dev * half + 3 * expert_count - 1) // (3 * expert_count)), tok_dev)


def rms_terms(xf, probe):
    scale = lax.rsqrt(jnp.mean(xf * xf, axis=1, keepdims=True) + EPS)
    along = jnp.mean(xf * probe, axis=1, keepdims=True)
    return scale, along


def pack_kernel(expert_count, *refs):
    sources, pack, held, sems = (refs[:6], refs[6], refs[7:13], refs[13])
    copies = [
        pltpu.make_async_copy(source, target, sems.at[n])
        for n, (source, target) in enumerate(zip(sources, held))
    ]
    for copy in copies:
        copy.start()
    for copy in copies:
        copy.wait()
    tokens, gain, signs, cotangent, routes, gates = held
    width = tokens.shape[1]
    xf = tokens[...].astype(jnp.float32)
    probe = (2 * signs[...] - 1).astype(jnp.float32)
    scale, along = rms_terms(xf, probe)
    pack[:, :width] = (xf * scale * gain[...]).astype(jnp.bfloat16)
    tangent = gain[...] * (scale * probe - scale**3 * xf * along)
    pack[:, width : 2 * width] = tangent.astype(jnp.bfloat16)
    pack[:, 2 * width : 3 * width] = cotangent[...]
    tok_dev, lanes = (tokens.shape[0], pack.shape[1] - 3 * width)
    lane = lax.broadcasted_iota(jnp.int32, (lanes, tok_dev), 0)
    expert = lax.rem(lane, expert_count)
    gate = jnp.zeros(lane.shape, jnp.float32)
    for group in range(routes.shape[0]):
        for slot in range(routes.shape[1]):
            named = routes[group, slot : slot + 1, :] == expert
            gate = gate + jnp.where(named, gates[group, slot : slot + 1, :], 0.0)
    high = gate.astype(jnp.bfloat16).astype(jnp.float32)
    tail = jnp.where(lane < expert_count, high, gate - high)
    tail = jnp.where(lane < 2 * expert_count, tail, 0.0).astype(jnp.bfloat16)
    turned = lax.dot_general(
        identity(tok_dev).astype(jnp.bfloat16),
        tail,
        (((1,), (1,)), ((), ())),
        preferred_element_type=jnp.float32,
    )
    lane = lax.broadcasted_iota(jnp.int32, (tok_dev, lanes), 1)
    place = 2 * expert_count
    for number in (scale, -(scale**3) * along):
        for _ in range(3):
            addend = number.astype(jnp.bfloat16).astype(jnp.float32)
            turned = jnp.where(lane == place, addend, turned)
            number = number - addend
            place += 1
    pack[:, 3 * width :] = turned.astype(jnp.bfloat16)


def identity(size):
    rows = lax.broadcasted_iota(jnp.int32, (size, size), 0)
    return (rows == lax.broadcasted_iota(jnp.int32, (size, size), 1)).astype(jnp.float32)


def packed(tokens, norm_gain, probe_signs, cotangent, routes, gates, expert_count):
    tok_dev, width = tokens.shape
    tail = -(-(2 * expert_count + 6) // 128) * 128
    token_minor = (0, 2, 1)
    operands = (
        tokens,
        norm_gain.reshape(1, width),
        probe_signs,
        cotangent,
        jnp.transpose(routes, token_minor),
        jnp.transpose(gates, token_minor),
    )
    return pl.pallas_call(
        functools.partial(pack_kernel, expert_count),
        out_shape=jax.ShapeDtypeStruct((tok_dev, 3 * width + tail), jnp.bfloat16),
        in_specs=[pl.BlockSpec(memory_space=pl.ANY)] * 6,
        out_specs=pl.BlockSpec(memory_space=pltpu.VMEM),
        scratch_shapes=[pltpu.VMEM(array.shape, array.dtype) for array in operands]
        + [pltpu.SemaphoreType.DMA((6,))],
        compiler_params=pltpu.CompilerParams(vmem_limit_bytes=VMEM),
        cost_estimate=pl.CostEstimate(
            flops=20 * tok_dev * width, bytes_accessed=14 * tok_dev * width, transcendentals=0
        ),
    )(*(pltpu.with_memory_space_constraint(array, pltpu.HBM) for array in operands))


def join_kernel(own, other, held, sems):
    half = own.shape[2]
    copies = [
        pltpu.make_async_copy(
            source.at[part], held.at[part, :, pl.ds(h * half, half)], sems.at[h, part]
        )
        for h, source in enumerate((own, other))
        for part in range(3)
    ]
    for copy in copies:
        copy.start()
    for copy in copies:
        copy.wait()


def joined(own, other):
    parts, width, half = own.shape
    return pl.pallas_call(
        join_kernel,
        out_shape=pltpu.VMEM((parts, width, 2 * half), own.dtype),
        in_specs=[pl.BlockSpec(memory_space=pl.ANY)] * 2,
        out_specs=pl.BlockSpec(memory_space=pltpu.VMEM),
        scratch_shapes=[pltpu.SemaphoreType.DMA((2, parts))],
        compiler_params=pltpu.CompilerParams(vmem_limit_bytes=VMEM),
        cost_estimate=pl.CostEstimate(
            flops=0, bytes_accessed=8 * parts * width * half, transcendentals=0
        ),
    )(pltpu.with_memory_space_constraint(own, pltpu.HBM), other)


def expert_kernel(count, expert_count, *refs):
    packs, held, outs = (refs[:count], refs[count], refs[count + 1 : 2 * count + 1])
    both, cotan, acc = refs[2 * count + 1 :]
    tok_dev = packs[0].shape[0]
    _, width, hidden = held.shape
    rows = count * tok_dev

    def stacked(start, size):
        return jnp.concatenate([p[:, start : start + size].astype(jnp.float32) for p in packs], 0)

    both[:rows, :] = stacked(0, width).astype(jnp.bfloat16)
    both[rows:, :] = stacked(width, width).astype(jnp.bfloat16)
    cotan[...] = stacked(2 * width, width).astype(jnp.bfloat16)
    tail = stacked(3 * width, packs[0].shape[1] - 3 * width)
    mine = lax.axis_index("expert") // 2
    lane = lax.broadcasted_iota(jnp.int32, tail.shape, 1)
    after = 2 * expert_count

    def picked(lanes):
        return jnp.sum(jnp.where(lanes, tail, 0.0), axis=1, keepdims=True)

    gate_row = picked((lane == mine) | (lane == mine + expert_count))
    scale_row = picked((lane >= after) & (lane < after + 3))
    slope_row = picked((lane >= after + 3) & (lane < after + 6))

    def weights(part, start, size):
        return held[part, :, start : start + size]

    block = 256 if hidden % 256 == 0 else 128
    contract = (((1,), (1,)), ((), ()))
    for start in range(0, hidden, block):
        pre_gate = jnp.dot(
            both[...], weights(0, start, block), preferred_element_type=jnp.float32
        )
        pre_up = jnp.dot(both[...], weights(1, start, block), preferred_element_type=jnp.float32)
        back = jnp.dot(cotan[...], weights(2, start, block), preferred_element_type=jnp.float32)
        gate, gate_t = (pre_gate[:rows], pre_gate[rows:])
        up, up_t = (pre_up[:rows], pre_up[rows:])
        sig = jax.nn.sigmoid(gate)
        act = gate * sig
        slope = sig * (1.0 + gate * (1.0 - sig))
        bend = sig * (1.0 - sig) * (2.0 + gate * (1.0 - 2.0 * sig))
        d_gate = (back * slope * up).astype(jnp.bfloat16)
        d_up = (back * act).astype(jnp.bfloat16)
        t_gate = (back * (bend * gate_t * up + slope * up_t)).astype(jnp.bfloat16)
        t_up = (back * slope * gate_t).astype(jnp.bfloat16)
        total = lax.dot_general(
            jnp.concatenate([d_gate, t_gate], 0),
            weights(0, start, block),
            contract,
            preferred_element_type=jnp.float32,
        )
        total = total + lax.dot_general(
            jnp.concatenate([d_up, t_up], 0),
            weights(1, start, block),
            contract,
            preferred_element_type=jnp.float32,
        )
        acc[...] = total if start == 0 else acc[...] + total
    for n in range(count):
        part = slice(n * tok_dev, (n + 1) * tok_dev)
        later = slice(rows + n * tok_dev, rows + (n + 1) * tok_dev)
        grad, tan = (acc[part] * gate_row[part], acc[later] * gate_row[part])
        scale, slope_r = (scale_row[part], slope_row[part])
        normed = packs[n][:, :width].astype(jnp.float32)
        normed_t = packs[n][:, width : 2 * width].astype(jnp.float32)
        outs[n][:, :width] = (scale * tan + slope_r * grad).astype(outs[n].dtype)
        first = jnp.mean(normed * grad, axis=1, keepdims=True)
        second = jnp.mean(normed * tan + normed_t * grad, axis=1, keepdims=True)
        second = (second - slope_r / scale * first) / scale
        lane = lax.broadcasted_iota(jnp.int32, (tok_dev, outs[n].shape[1] - width), 1)
        sums = jnp.where(lane == 0, first / scale, jnp.where(lane == 1, second, 0.0))
        outs[n][:, width:] = sums.astype(outs[n].dtype)


def experts(packs, kinds, held, expert_count):
    count = len(packs)
    tok_dev = packs[0].shape[0]
    _, width, hidden = held.shape
    rows = count * tok_dev
    whole = pl.BlockSpec(memory_space=pltpu.VMEM)
    return pl.pallas_call(
        functools.partial(expert_kernel, count, expert_count),
        out_shape=[jax.ShapeDtypeStruct((tok_dev, width + 128), kind) for kind in kinds],
        in_specs=[whole] * (count + 1),
        out_specs=[whole] * count,
        scratch_shapes=[
            pltpu.VMEM((2 * rows, width), jnp.bfloat16),
            pltpu.VMEM((rows, width), jnp.bfloat16),
            pltpu.VMEM((2 * rows, width), jnp.float32),
        ],
        compiler_params=pltpu.CompilerParams(vmem_limit_bytes=VMEM),
        cost_estimate=pl.CostEstimate(
            flops=2 * 9 * rows * width * hidden,
            bytes_accessed=6 * width * hidden,
            transcendentals=rows * hidden,
        ),
    )(*packs, pltpu.with_memory_space_constraint(held, pltpu.VMEM))


def finish_kernel(tokens, gain, signs, *refs):
    arrived, hvp, quad = (refs[:-2], refs[-2], refs[-1])
    width = tokens.shape[1]
    xf = tokens[...].astype(jnp.float32)
    probe = (2 * signs[...] - 1).astype(jnp.float32)
    scale, along = rms_terms(xf, probe)
    slope_r = -(scale**3) * along
    rows = sum(part[...].astype(jnp.float32) for part in arrived)
    first = rows[:, width : width + 1]
    second = rows[:, width + 1 : width + 2]
    whole = (
        gain[...] * rows[:, :width]
        - 3.0 * scale**2 * slope_r * first * xf
        - scale**3 * first * probe
        - scale**3 * second * xf
    )
    hvp[...] = whole
    column = jnp.mean(probe * whole, axis=1, keepdims=True)
    tok_dev = column.shape[0]
    quad[...] = jnp.sum(identity(tok_dev) * column, axis=0, keepdims=True)


def moved(rows, turns, flip_x=False, flip_core=False):
    count = lax.axis_size("expert")
    pairs = [
        (i, (i + 4 * turns) % count ^ (2 * flip_x) ^ (1 * flip_core)) for i in range(count)
    ]
    return lax.ppermute(rows, "expert", pairs)


def dense_local(tokens, norm_gain, probe_signs, cotangent, routes, gates, weights):
    tok_dev, width = tokens.shape
    n_exp = lax.axis_size("expert")
    expert_count = n_exp // 2
    pack = packed(tokens, norm_gain, probe_signs, cotangent, routes, gates, expert_count)
    held = joined(weights, moved(weights, 0, flip_core=True))
    same, across = {0: pack}, {}
    same[1] = moved(pack, 1)
    across[0] = moved(pack, 0, flip_x=True)
    same[1] = lax.optimization_barrier((same[1], across[0], held))[0]
    same[2] = moved(same[1], 1)
    across[1] = moved(same[1], 0, flip_x=True)
    same[3] = moved(lax.optimization_barrier((pack, same[1]))[0], -1)
    across[2] = moved(same[2], 0, flip_x=True)
    across[3] = moved(lax.optimization_barrier((across[0], same[2]))[0], -1)
    wide, sent = (jnp.float32, jnp.bfloat16)
    here, there = {}, {}
    here[0], here[1], there[0], there[1] = experts(
        [same[0], same[1], across[0], across[1]], [wide, wide, sent, sent], held, expert_count
    )
    far = lax.optimization_barrier((across[2], here[1]))[0]
    here[2], here[3], there[2] = experts(
        [same[2], same[3], far], [wide, sent, sent], held, expert_count
    )
    last = lax.optimization_barrier((across[3], here[2]))[0]
    (there[3],) = experts([last], [sent], held, expert_count)

    def flipped(rows):
        return moved(rows, 0, flip_x=True)

    def total(*parts):
        return sum(part.astype(jnp.float32) for part in parts).astype(jnp.bfloat16)

    arrived = [
        here[0],
        flipped(there[0]),
        moved(total(here[1], flipped(there[1])), -1),
        moved(total(here[2], flipped(there[2])), 2),
        moved(here[3], 1),
        moved(there[3], 1, flip_x=True),
    ]
    hvp, quad = pl.pallas_call(
        finish_kernel,
        out_shape=[
            jax.ShapeDtypeStruct((tok_dev, width), jnp.float32),
            jax.ShapeDtypeStruct((1, tok_dev), jnp.float32),
        ],
        compiler_params=pltpu.CompilerParams(vmem_limit_bytes=VMEM),
        cost_estimate=pl.CostEstimate(
            flops=40 * tok_dev * width, bytes_accessed=26 * tok_dev * width, transcendentals=0
        ),
    )(tokens, norm_gain.reshape(1, width), probe_signs, *arrived)
    return (hvp, quad.reshape(tok_dev))


def routed_rows(normed, normed_t, cotangent, routes, gates, weights):
    tok_dev, width = normed.shape
    groups_here = routes.shape[0]
    half = routes.shape[2]
    n_exp = lax.axis_size("expert")
    expert_count = n_exp // 2
    cap = capacity(tok_dev, half, expert_count)
    buffer_rows = expert_count * cap
    stack_z, stack_t, stack_c, stack_w = ([], [], [], [])
    for group in range(groups_here):
        target = slot_targets(routes[group], expert_count, cap)
        place = (jnp.arange(buffer_rows, dtype=jnp.int32)[:, None] == target[None, :]).reshape(
            buffer_rows, tok_dev, half
        )
        place_tok = jnp.sum(place.astype(jnp.float32), axis=2).astype(jnp.bfloat16)
        stack_w.append(jnp.sum(place.astype(jnp.float32) * gates[group][None, :, :], axis=2))
        stack_z.append(
            jnp.dot(place_tok, normed, preferred_element_type=jnp.float32).astype(jnp.bfloat16)
        )
        stack_t.append(
            jnp.dot(place_tok, normed_t, preferred_element_type=jnp.float32).astype(jnp.bfloat16)
        )
        stack_c.append(
            jnp.dot(place_tok, cotangent, preferred_element_type=jnp.float32).astype(jnp.bfloat16)
        )
    rows_z = jnp.stack(stack_z, 0)
    rows_t = jnp.stack(stack_t, 0)
    rows_c = jnp.stack(stack_c, 0)
    weighted = jnp.stack(stack_w, 0)

    def arrange(rows):
        shaped = rows.reshape(groups_here, expert_count, 1, cap, width)
        shaped = jnp.broadcast_to(shaped, (groups_here, expert_count, 2, cap, width))
        return jnp.transpose(shaped, (1, 2, 0, 3, 4)).reshape(n_exp, groups_here * cap, width)

    send_z, send_t, send_c = (arrange(rows_z), arrange(rows_t), arrange(rows_c))
    got_z = lax.all_to_all(send_z, "expert", split_axis=0, concat_axis=0, tiled=True)
    got_t = lax.all_to_all(send_t, "expert", split_axis=0, concat_axis=0, tiled=True)
    got_c = lax.all_to_all(send_c, "expert", split_axis=0, concat_axis=0, tiled=True)
    sources, items, cols = got_z.shape
    g_rows, t_rows = expert_terms(
        weights, got_z.reshape(-1, cols), got_t.reshape(-1, cols), got_c.reshape(-1, cols)
    )
    g_rows = g_rows.reshape(sources, items, cols)
    t_rows = t_rows.reshape(sources, items, cols)
    back_g = lax.all_to_all(g_rows, "expert", split_axis=0, concat_axis=0, tiled=True)
    back_t = lax.all_to_all(t_rows, "expert", split_axis=0, concat_axis=0, tiled=True)

    def restore(rows):
        shaped = jnp.sum(rows.reshape(expert_count, 2, groups_here, cap, width), axis=1)
        return jnp.transpose(shaped, (1, 0, 2, 3)).reshape(groups_here, buffer_rows, width)

    back_g = restore(back_g)
    back_t = restore(back_t)
    contract = (((0, 1), (0, 1)), ((), ()))
    grad_z = lax.dot_general(weighted, back_g, contract, precision=lax.Precision.HIGHEST)
    tan_z = lax.dot_general(weighted, back_t, contract, precision=lax.Precision.HIGHEST)
    return (grad_z, tan_z)


def local(tokens, norm_gain, probe_signs, cotangent, routes, gates, expert_weights):
    cap = capacity(tokens.shape[0], routes.shape[2], lax.axis_size("expert") // 2)
    layout = (lax.axis_size("expert"), lax.axis_size("node"))
    if layout == (16, 1) and routes.shape[0] * cap >= tokens.shape[0]:
        return dense_local(
            tokens, norm_gain, probe_signs, cotangent, routes, gates, expert_weights
        )
    xf = tokens.astype(jnp.float32)
    probe = (2 * probe_signs - 1).astype(jnp.float32)
    tok_dev, width = xf.shape
    scale = lax.rsqrt(jnp.mean(xf * xf, axis=1, keepdims=True) + EPS)
    along = jnp.mean(xf * probe, axis=1, keepdims=True)
    normed = (xf * scale * norm_gain).astype(jnp.bfloat16)
    normed_t = (norm_gain * (scale * probe - scale**3 * xf * along)).astype(jnp.bfloat16)
    own_half = lax.all_gather(expert_weights, "node", axis=2, tiled=True)
    grad_z, tan_z = routed_rows(normed, normed_t, cotangent, routes, gates, own_half)
    share = width // lax.axis_size("node")
    start = lax.axis_index("node") * share
    slope_r = -(scale**3) * along
    grad_z, tan_z = lax.psum((grad_z, tan_z), "node")
    lifted = norm_gain * grad_z
    lifted_t = norm_gain * tan_z
    first = jnp.mean(xf * lifted, axis=1, keepdims=True)
    second = jnp.mean(xf * lifted_t, axis=1, keepdims=True)
    third = jnp.mean(probe * lifted, axis=1, keepdims=True)
    whole_hvp = (
        scale * lifted_t
        + slope_r * lifted
        - 3.0 * scale**2 * slope_r * first * xf
        - scale**3 * first * probe
        - scale**3 * (second + third) * xf
    )
    quad = jnp.mean(probe * whole_hvp, axis=1)
    hvp = lax.dynamic_slice_in_dim(whole_hvp, start, share, 1)
    return (hvp, quad)


def solution(mesh):
    placed = (
        P(("groups", "expert"), None),
        P(),
        P(("groups", "expert"), None),
        P(("groups", "expert"), None),
        P("node", ("groups", "expert"), None),
        P("node", ("groups", "expert"), None),
        P(None, None, ("expert", "node")),
    )
    return jax.shard_map(
        local,
        mesh=mesh,
        in_specs=placed,
        out_specs=(P(("groups", "expert"), "node"), P(("groups", "expert"))),
        check_vma=False,
    )
```

```python
import functools

import jax
import jax.numpy as jnp
from jax import lax
from jax.experimental import pallas as pl
from jax.experimental.pallas import tpu as pltpu
from jax.sharding import PartitionSpec as P

EPS = 1e-06
VMEM = 24 * 1024 * 1024


def expert_terms(weights, rows, rows_t, cotan):
    count = rows.shape[0]
    both = jnp.concatenate([rows, rows_t], 0)
    pre_gate = jnp.dot(both, weights[0], preferred_element_type=jnp.float32)
    pre_up = jnp.dot(both, weights[1], preferred_element_type=jnp.float32)
    gate, gate_t = (pre_gate[:count], pre_gate[count:])
    up, up_t = (pre_up[:count], pre_up[count:])
    back = jnp.dot(cotan, weights[2], preferred_element_type=jnp.float32)
    sig = jax.nn.sigmoid(gate)
    act = gate * sig
    slope = sig * (1.0 + gate * (1.0 - sig))
    bend = sig * (1.0 - sig) * (2.0 + gate * (1.0 - 2.0 * sig))
    d_gate = (back * slope * up).astype(jnp.bfloat16)
    d_up = (back * act).astype(jnp.bfloat16)
    t_gate = (back * (bend * gate_t * up + slope * up_t)).astype(jnp.bfloat16)
    t_up = (back * slope * gate_t).astype(jnp.bfloat16)
    contract = (((1,), (1,)), ((), ()))
    lhs_gate = jnp.concatenate([d_gate, t_gate], 0)
    lhs_up = jnp.concatenate([d_up, t_up], 0)
    total = lax.dot_general(lhs_gate, weights[0], contract, preferred_element_type=jnp.float32)
    total = total + lax.dot_general(
        lhs_up, weights[1], contract, preferred_element_type=jnp.float32
    )
    return (total[:count], total[count:])


def slot_targets(route_ids, expert_count, capacity):
    flat = route_ids.reshape(-1)
    count = flat.shape[0]
    onehot = (flat[:, None] == jnp.arange(expert_count, dtype=jnp.int32)[None, :]).astype(
        jnp.float32
    )
    lower = (jnp.arange(count)[:, None] > jnp.arange(count)[None, :]).astype(jnp.float32)
    before = jnp.dot(lower, onehot, precision=lax.Precision.HIGHEST)
    rank = jnp.sum(before * onehot, axis=1).astype(jnp.int32)
    return flat * capacity + rank


def capacity(tok_dev, half, expert_count):
    return min(2 * ((2 * tok_dev * half + 3 * expert_count - 1) // (3 * expert_count)), tok_dev)


def rms_terms(xf, probe):
    scale = lax.rsqrt(jnp.mean(xf * xf, axis=1, keepdims=True) + EPS)
    along = jnp.mean(xf * probe, axis=1, keepdims=True)
    return scale, along


def pack_kernel(expert_count, *refs):
    sources, pack, held, sems = (refs[:6], refs[6], refs[7:13], refs[13])
    copies = [
        pltpu.make_async_copy(source, target, sems.at[n])
        for n, (source, target) in enumerate(zip(sources, held))
    ]
    for copy in copies:
        copy.start()
    for copy in copies:
        copy.wait()
    tokens, gain, signs, cotangent, routes, gates = held
    width = tokens.shape[1]
    xf = tokens[...].astype(jnp.float32)
    probe = (2 * signs[...] - 1).astype(jnp.float32)
    scale, along = rms_terms(xf, probe)
    pack[:, :width] = (xf * scale * gain[...]).astype(jnp.bfloat16)
    tangent = gain[...] * (scale * probe - scale**3 * xf * along)
    pack[:, width : 2 * width] = tangent.astype(jnp.bfloat16)
    pack[:, 2 * width : 3 * width] = cotangent[...]
    tok_dev, lanes = (tokens.shape[0], pack.shape[1] - 3 * width)
    lane = lax.broadcasted_iota(jnp.int32, (lanes, tok_dev), 0)
    expert = lax.rem(lane, expert_count)
    gate = jnp.zeros(lane.shape, jnp.float32)
    for group in range(routes.shape[0]):
        for slot in range(routes.shape[1]):
            named = routes[group, slot : slot + 1, :] == expert
            gate = gate + jnp.where(named, gates[group, slot : slot + 1, :], 0.0)
    high = gate.astype(jnp.bfloat16).astype(jnp.float32)
    tail = jnp.where(lane < expert_count, high, gate - high)
    tail = jnp.where(lane < 2 * expert_count, tail, 0.0).astype(jnp.bfloat16)
    turned = lax.dot_general(
        identity(tok_dev).astype(jnp.bfloat16),
        tail,
        (((1,), (1,)), ((), ())),
        preferred_element_type=jnp.float32,
    )
    lane = lax.broadcasted_iota(jnp.int32, (tok_dev, lanes), 1)
    place = 2 * expert_count
    for number in (scale, -(scale**3) * along):
        for _ in range(3):
            addend = number.astype(jnp.bfloat16).astype(jnp.float32)
            turned = jnp.where(lane == place, addend, turned)
            number = number - addend
            place += 1
    pack[:, 3 * width :] = turned.astype(jnp.bfloat16)


def identity(size):
    rows = lax.broadcasted_iota(jnp.int32, (size, size), 0)
    return (rows == lax.broadcasted_iota(jnp.int32, (size, size), 1)).astype(jnp.float32)


def packed(tokens, norm_gain, probe_signs, cotangent, routes, gates, expert_count):
    tok_dev, width = tokens.shape
    tail = -(-(2 * expert_count + 6) // 128) * 128
    token_minor = (0, 2, 1)
    operands = (
        tokens,
        norm_gain.reshape(1, width),
        probe_signs,
        cotangent,
        jnp.transpose(routes, token_minor),
        jnp.transpose(gates, token_minor),
    )
    return pl.pallas_call(
        functools.partial(pack_kernel, expert_count),
        out_shape=jax.ShapeDtypeStruct((tok_dev, 3 * width + tail), jnp.bfloat16),
        in_specs=[pl.BlockSpec(memory_space=pl.ANY)] * 6,
        out_specs=pl.BlockSpec(memory_space=pltpu.VMEM),
        scratch_shapes=[pltpu.VMEM(array.shape, array.dtype) for array in operands]
        + [pltpu.SemaphoreType.DMA((6,))],
        compiler_params=pltpu.CompilerParams(vmem_limit_bytes=VMEM),
        cost_estimate=pl.CostEstimate(
            flops=20 * tok_dev * width, bytes_accessed=14 * tok_dev * width, transcendentals=0
        ),
    )(*(pltpu.with_memory_space_constraint(array, pltpu.HBM) for array in operands))


def join_kernel(own, other, held, sems):
    half = own.shape[2]
    copies = [
        pltpu.make_async_copy(
            source.at[part], held.at[part, :, pl.ds(h * half, half)], sems.at[h, part]
        )
        for h, source in enumerate((own, other))
        for part in range(3)
    ]
    for copy in copies:
        copy.start()
    for copy in copies:
        copy.wait()


def joined(own, other):
    parts, width, half = own.shape
    return pl.pallas_call(
        join_kernel,
        out_shape=pltpu.VMEM((parts, width, 2 * half), own.dtype),
        in_specs=[pl.BlockSpec(memory_space=pl.ANY)] * 2,
        out_specs=pl.BlockSpec(memory_space=pltpu.VMEM),
        scratch_shapes=[pltpu.SemaphoreType.DMA((2, parts))],
        compiler_params=pltpu.CompilerParams(vmem_limit_bytes=VMEM),
        cost_estimate=pl.CostEstimate(
            flops=0, bytes_accessed=8 * parts * width * half, transcendentals=0
        ),
    )(pltpu.with_memory_space_constraint(own, pltpu.HBM), other)


def expert_kernel(count, expert_count, *refs):
    packs, held, outs = (refs[:count], refs[count], refs[count + 1 : 2 * count + 1])
    both, cotan, acc = refs[2 * count + 1 :]
    tok_dev = packs[0].shape[0]
    _, width, hidden = held.shape
    rows = count * tok_dev

    def stacked(start, size):
        return jnp.concatenate([p[:, start : start + size].astype(jnp.float32) for p in packs], 0)

    both[:rows, :] = stacked(0, width).astype(jnp.bfloat16)
    both[rows:, :] = stacked(width, width).astype(jnp.bfloat16)
    cotan[...] = stacked(2 * width, width).astype(jnp.bfloat16)
    tail = stacked(3 * width, packs[0].shape[1] - 3 * width)
    mine = lax.axis_index("expert") // 2
    lane = lax.broadcasted_iota(jnp.int32, tail.shape, 1)
    after = 2 * expert_count

    def picked(lanes):
        return jnp.sum(jnp.where(lanes, tail, 0.0), axis=1, keepdims=True)

    gate_row = picked((lane == mine) | (lane == mine + expert_count))
    scale_row = picked((lane >= after) & (lane < after + 3))
    slope_row = picked((lane >= after + 3) & (lane < after + 6))

    def weights(part, start, size):
        return held[part, :, start : start + size]

    block = 256 if hidden % 256 == 0 else 128
    contract = (((1,), (1,)), ((), ()))
    for start in range(0, hidden, block):
        pre_gate = jnp.dot(
            both[...], weights(0, start, block), preferred_element_type=jnp.float32
        )
        pre_up = jnp.dot(both[...], weights(1, start, block), preferred_element_type=jnp.float32)
        back = jnp.dot(cotan[...], weights(2, start, block), preferred_element_type=jnp.float32)
        gate, gate_t = (pre_gate[:rows], pre_gate[rows:])
        up, up_t = (pre_up[:rows], pre_up[rows:])
        sig = jax.nn.sigmoid(gate)
        act = gate * sig
        slope = sig * (1.0 + gate * (1.0 - sig))
        bend = sig * (1.0 - sig) * (2.0 + gate * (1.0 - 2.0 * sig))
        d_gate = (back * slope * up).astype(jnp.bfloat16)
        d_up = (back * act).astype(jnp.bfloat16)
        t_gate = (back * (bend * gate_t * up + slope * up_t)).astype(jnp.bfloat16)
        t_up = (back * slope * gate_t).astype(jnp.bfloat16)
        total = lax.dot_general(
            jnp.concatenate([d_gate, t_gate], 0),
            weights(0, start, block),
            contract,
            preferred_element_type=jnp.float32,
        )
        total = total + lax.dot_general(
            jnp.concatenate([d_up, t_up], 0),
            weights(1, start, block),
            contract,
            preferred_element_type=jnp.float32,
        )
        acc[...] = total if start == 0 else acc[...] + total
    for n in range(count):
        part = slice(n * tok_dev, (n + 1) * tok_dev)
        later = slice(rows + n * tok_dev, rows + (n + 1) * tok_dev)
        grad, tan = (acc[part] * gate_row[part], acc[later] * gate_row[part])
        scale, slope_r = (scale_row[part], slope_row[part])
        normed = packs[n][:, :width].astype(jnp.float32)
        normed_t = packs[n][:, width : 2 * width].astype(jnp.float32)
        outs[n][:, :width] = (scale * tan + slope_r * grad).astype(outs[n].dtype)
        first = jnp.mean(normed * grad, axis=1, keepdims=True)
        second = jnp.mean(normed * tan + normed_t * grad, axis=1, keepdims=True)
        second = (second - slope_r / scale * first) / scale
        lane = lax.broadcasted_iota(jnp.int32, (tok_dev, outs[n].shape[1] - width), 1)
        sums = jnp.where(lane == 0, first / scale, jnp.where(lane == 1, second, 0.0))
        outs[n][:, width:] = sums.astype(outs[n].dtype)


def experts(packs, kinds, held, expert_count):
    count = len(packs)
    tok_dev = packs[0].shape[0]
    _, width, hidden = held.shape
    rows = count * tok_dev
    whole = pl.BlockSpec(memory_space=pltpu.VMEM)
    return pl.pallas_call(
        functools.partial(expert_kernel, count, expert_count),
        out_shape=[jax.ShapeDtypeStruct((tok_dev, width + 128), kind) for kind in kinds],
        in_specs=[whole] * (count + 1),
        out_specs=[whole] * count,
        scratch_shapes=[
            pltpu.VMEM((2 * rows, width), jnp.bfloat16),
            pltpu.VMEM((rows, width), jnp.bfloat16),
            pltpu.VMEM((2 * rows, width), jnp.float32),
        ],
        compiler_params=pltpu.CompilerParams(vmem_limit_bytes=VMEM),
        cost_estimate=pl.CostEstimate(
            flops=2 * 9 * rows * width * hidden,
            bytes_accessed=6 * width * hidden,
            transcendentals=rows * hidden,
        ),
    )(*packs, pltpu.with_memory_space_constraint(held, pltpu.VMEM))


def finish_kernel(tokens, gain, signs, *refs):
    arrived, hvp, quad = (refs[:-2], refs[-2], refs[-1])
    width = tokens.shape[1]
    xf = tokens[...].astype(jnp.float32)
    probe = (2 * signs[...] - 1).astype(jnp.float32)
    scale, along = rms_terms(xf, probe)
    slope_r = -(scale**3) * along
    rows = sum(part[...].astype(jnp.float32) for part in arrived)
    first = rows[:, width : width + 1]
    second = rows[:, width + 1 : width + 2]
    whole = (
        gain[...] * rows[:, :width]
        - 3.0 * scale**2 * slope_r * first * xf
        - scale**3 * first * probe
        - scale**3 * second * xf
    )
    hvp[...] = whole
    column = jnp.mean(probe * whole, axis=1, keepdims=True)
    tok_dev = column.shape[0]
    quad[...] = jnp.sum(identity(tok_dev) * column, axis=0, keepdims=True)


def moved(rows, turns, flip_x=False, flip_core=False):
    count = lax.axis_size("expert")
    pairs = [
        (i, (i + 4 * turns) % count ^ (2 * flip_x) ^ (1 * flip_core)) for i in range(count)
    ]
    return lax.ppermute(rows, "expert", pairs)


def dense_local(tokens, norm_gain, probe_signs, cotangent, routes, gates, weights):
    tok_dev, width = tokens.shape
    n_exp = lax.axis_size("expert")
    expert_count = n_exp // 2
    pack = packed(tokens, norm_gain, probe_signs, cotangent, routes, gates, expert_count)
    held = joined(weights, moved(weights, 0, flip_core=True))
    same, across = {0: pack}, {}
    same[1] = moved(pack, 1)
    across[0] = moved(pack, 0, flip_x=True)
    same[1] = lax.optimization_barrier((same[1], across[0], held))[0]
    same[3] = moved(pack, -1)
    same[2] = moved(same[1], 1)
    across[1] = moved(same[1], 0, flip_x=True)
    across[3] = moved(same[3], 0, flip_x=True)
    across[2] = moved(across[1], 1)
    wide, sent = (jnp.float32, jnp.bfloat16)
    here, there = {}, {}
    here[0], here[1], here[2], here[3], there[0], there[1] = experts(
        [same[0], same[1], same[2], same[3], across[0], across[1]],
        [wide, wide, sent, sent, sent, sent],
        held,
        expert_count,
    )
    late = lax.optimization_barrier((across[2], across[3], here[1]))[:2]
    there[2], there[3] = experts(late, [sent, sent], held, expert_count)

    def flipped(rows):
        return moved(rows, 0, flip_x=True)

    def total(*parts):
        return sum(part.astype(jnp.float32) for part in parts).astype(jnp.bfloat16)

    beside = flipped(there[1])
    kept = lax.optimization_barrier((here[1], there[2]))[0]
    arrived = [
        here[0],
        flipped(there[0]),
        moved(here[2], 2),
        moved(here[3], 1),
        moved(there[2], 2, flip_x=True),
        moved(there[3], 1, flip_x=True),
        moved(total(kept, beside), -1),
    ]
    hvp, quad = pl.pallas_call(
        finish_kernel,
        out_shape=[
            jax.ShapeDtypeStruct((tok_dev, width), jnp.float32),
            jax.ShapeDtypeStruct((1, tok_dev), jnp.float32),
        ],
        compiler_params=pltpu.CompilerParams(vmem_limit_bytes=VMEM),
        cost_estimate=pl.CostEstimate(
            flops=40 * tok_dev * width, bytes_accessed=26 * tok_dev * width, transcendentals=0
        ),
    )(tokens, norm_gain.reshape(1, width), probe_signs, *arrived)
    return (hvp, quad.reshape(tok_dev))


def routed_rows(normed, normed_t, cotangent, routes, gates, weights):
    tok_dev, width = normed.shape
    groups_here = routes.shape[0]
    half = routes.shape[2]
    n_exp = lax.axis_size("expert")
    expert_count = n_exp // 2
    cap = capacity(tok_dev, half, expert_count)
    buffer_rows = expert_count * cap
    stack_z, stack_t, stack_c, stack_w = ([], [], [], [])
    for group in range(groups_here):
        target = slot_targets(routes[group], expert_count, cap)
        place = (jnp.arange(buffer_rows, dtype=jnp.int32)[:, None] == target[None, :]).reshape(
            buffer_rows, tok_dev, half
        )
        place_tok = jnp.sum(place.astype(jnp.float32), axis=2).astype(jnp.bfloat16)
        stack_w.append(jnp.sum(place.astype(jnp.float32) * gates[group][None, :, :], axis=2))
        stack_z.append(
            jnp.dot(place_tok, normed, preferred_element_type=jnp.float32).astype(jnp.bfloat16)
        )
        stack_t.append(
            jnp.dot(place_tok, normed_t, preferred_element_type=jnp.float32).astype(jnp.bfloat16)
        )
        stack_c.append(
            jnp.dot(place_tok, cotangent, preferred_element_type=jnp.float32).astype(jnp.bfloat16)
        )
    rows_z = jnp.stack(stack_z, 0)
    rows_t = jnp.stack(stack_t, 0)
    rows_c = jnp.stack(stack_c, 0)
    weighted = jnp.stack(stack_w, 0)

    def arrange(rows):
        shaped = rows.reshape(groups_here, expert_count, 1, cap, width)
        shaped = jnp.broadcast_to(shaped, (groups_here, expert_count, 2, cap, width))
        return jnp.transpose(shaped, (1, 2, 0, 3, 4)).reshape(n_exp, groups_here * cap, width)

    send_z, send_t, send_c = (arrange(rows_z), arrange(rows_t), arrange(rows_c))
    got_z = lax.all_to_all(send_z, "expert", split_axis=0, concat_axis=0, tiled=True)
    got_t = lax.all_to_all(send_t, "expert", split_axis=0, concat_axis=0, tiled=True)
    got_c = lax.all_to_all(send_c, "expert", split_axis=0, concat_axis=0, tiled=True)
    sources, items, cols = got_z.shape
    g_rows, t_rows = expert_terms(
        weights, got_z.reshape(-1, cols), got_t.reshape(-1, cols), got_c.reshape(-1, cols)
    )
    g_rows = g_rows.reshape(sources, items, cols)
    t_rows = t_rows.reshape(sources, items, cols)
    back_g = lax.all_to_all(g_rows, "expert", split_axis=0, concat_axis=0, tiled=True)
    back_t = lax.all_to_all(t_rows, "expert", split_axis=0, concat_axis=0, tiled=True)

    def restore(rows):
        shaped = jnp.sum(rows.reshape(expert_count, 2, groups_here, cap, width), axis=1)
        return jnp.transpose(shaped, (1, 0, 2, 3)).reshape(groups_here, buffer_rows, width)

    back_g = restore(back_g)
    back_t = restore(back_t)
    contract = (((0, 1), (0, 1)), ((), ()))
    grad_z = lax.dot_general(weighted, back_g, contract, precision=lax.Precision.HIGHEST)
    tan_z = lax.dot_general(weighted, back_t, contract, precision=lax.Precision.HIGHEST)
    return (grad_z, tan_z)


def local(tokens, norm_gain, probe_signs, cotangent, routes, gates, expert_weights):
    cap = capacity(tokens.shape[0], routes.shape[2], lax.axis_size("expert") // 2)
    layout = (lax.axis_size("expert"), lax.axis_size("node"))
    if layout == (16, 1) and routes.shape[0] * cap >= tokens.shape[0]:
        return dense_local(
            tokens, norm_gain, probe_signs, cotangent, routes, gates, expert_weights
        )
    xf = tokens.astype(jnp.float32)
    probe = (2 * probe_signs - 1).astype(jnp.float32)
    tok_dev, width = xf.shape
    scale = lax.rsqrt(jnp.mean(xf * xf, axis=1, keepdims=True) + EPS)
    along = jnp.mean(xf * probe, axis=1, keepdims=True)
    normed = (xf * scale * norm_gain).astype(jnp.bfloat16)
    normed_t = (norm_gain * (scale * probe - scale**3 * xf * along)).astype(jnp.bfloat16)
    own_half = lax.all_gather(expert_weights, "node", axis=2, tiled=True)
    grad_z, tan_z = routed_rows(normed, normed_t, cotangent, routes, gates, own_half)
    share = width // lax.axis_size("node")
    start = lax.axis_index("node") * share
    slope_r = -(scale**3) * along
    grad_z, tan_z = lax.psum((grad_z, tan_z), "node")
    lifted = norm_gain * grad_z
    lifted_t = norm_gain * tan_z
    first = jnp.mean(xf * lifted, axis=1, keepdims=True)
    second = jnp.mean(xf * lifted_t, axis=1, keepdims=True)
    third = jnp.mean(probe * lifted, axis=1, keepdims=True)
    whole_hvp = (
        scale * lifted_t
        + slope_r * lifted
        - 3.0 * scale**2 * slope_r * first * xf
        - scale**3 * first * probe
        - scale**3 * (second + third) * xf
    )
    quad = jnp.mean(probe * whole_hvp, axis=1)
    hvp = lax.dynamic_slice_in_dim(whole_hvp, start, share, 1)
    return (hvp, quad)


def solution(mesh):
    placed = (
        P(("groups", "expert"), None),
        P(),
        P(("groups", "expert"), None),
        P(("groups", "expert"), None),
        P("node", ("groups", "expert"), None),
        P("node", ("groups", "expert"), None),
        P(None, None, ("expert", "node")),
    )
    return jax.shard_map(
        local,
        mesh=mesh,
        in_specs=placed,
        out_specs=(P(("groups", "expert"), "node"), P(("groups", "expert"))),
        check_vma=False,
    )
```

```python
import functools

import jax
import jax.numpy as jnp
from jax import lax
from jax.experimental import pallas as pl
from jax.experimental.pallas import tpu as pltpu
from jax.sharding import PartitionSpec as P

EPS = 1e-06
VMEM = 24 * 1024 * 1024


def expert_terms(weights, rows, rows_t, cotan):
    count = rows.shape[0]
    both = jnp.concatenate([rows, rows_t], 0)
    pre_gate = jnp.dot(both, weights[0], preferred_element_type=jnp.float32)
    pre_up = jnp.dot(both, weights[1], preferred_element_type=jnp.float32)
    gate, gate_t = (pre_gate[:count], pre_gate[count:])
    up, up_t = (pre_up[:count], pre_up[count:])
    back = jnp.dot(cotan, weights[2], preferred_element_type=jnp.float32)
    sig = jax.nn.sigmoid(gate)
    act = gate * sig
    slope = sig * (1.0 + gate * (1.0 - sig))
    bend = sig * (1.0 - sig) * (2.0 + gate * (1.0 - 2.0 * sig))
    d_gate = (back * slope * up).astype(jnp.bfloat16)
    d_up = (back * act).astype(jnp.bfloat16)
    t_gate = (back * (bend * gate_t * up + slope * up_t)).astype(jnp.bfloat16)
    t_up = (back * slope * gate_t).astype(jnp.bfloat16)
    contract = (((1,), (1,)), ((), ()))
    lhs_gate = jnp.concatenate([d_gate, t_gate], 0)
    lhs_up = jnp.concatenate([d_up, t_up], 0)
    total = lax.dot_general(lhs_gate, weights[0], contract, preferred_element_type=jnp.float32)
    total = total + lax.dot_general(
        lhs_up, weights[1], contract, preferred_element_type=jnp.float32
    )
    return (total[:count], total[count:])


def slot_targets(route_ids, expert_count, capacity):
    flat = route_ids.reshape(-1)
    count = flat.shape[0]
    onehot = (flat[:, None] == jnp.arange(expert_count, dtype=jnp.int32)[None, :]).astype(
        jnp.float32
    )
    lower = (jnp.arange(count)[:, None] > jnp.arange(count)[None, :]).astype(jnp.float32)
    before = jnp.dot(lower, onehot, precision=lax.Precision.HIGHEST)
    rank = jnp.sum(before * onehot, axis=1).astype(jnp.int32)
    return flat * capacity + rank


def capacity(tok_dev, half, expert_count):
    return min(2 * ((2 * tok_dev * half + 3 * expert_count - 1) // (3 * expert_count)), tok_dev)


def rms_terms(xf, probe):
    scale = lax.rsqrt(jnp.mean(xf * xf, axis=1, keepdims=True) + EPS)
    along = jnp.mean(xf * probe, axis=1, keepdims=True)
    return scale, along


def pack_kernel(expert_count, *refs):
    sources, pack, held, sems = (refs[:6], refs[6], refs[7:13], refs[13])
    copies = [
        pltpu.make_async_copy(source, target, sems.at[n])
        for n, (source, target) in enumerate(zip(sources, held))
    ]
    for copy in copies:
        copy.start()
    for copy in copies:
        copy.wait()
    tokens, gain, signs, cotangent, routes, gates = held
    width = tokens.shape[1]
    xf = tokens[...].astype(jnp.float32)
    probe = (2 * signs[...] - 1).astype(jnp.float32)
    scale, along = rms_terms(xf, probe)
    pack[:, :width] = (xf * scale * gain[...]).astype(jnp.bfloat16)
    tangent = gain[...] * (scale * probe - scale**3 * xf * along)
    pack[:, width : 2 * width] = tangent.astype(jnp.bfloat16)
    pack[:, 2 * width : 3 * width] = cotangent[...]
    tok_dev, lanes = (tokens.shape[0], pack.shape[1] - 3 * width)
    lane = lax.broadcasted_iota(jnp.int32, (lanes, tok_dev), 0)
    expert = lax.rem(lane, expert_count)
    gate = jnp.zeros(lane.shape, jnp.float32)
    for group in range(routes.shape[0]):
        for slot in range(routes.shape[1]):
            named = routes[group, slot : slot + 1, :] == expert
            gate = gate + jnp.where(named, gates[group, slot : slot + 1, :], 0.0)
    high = gate.astype(jnp.bfloat16).astype(jnp.float32)
    tail = jnp.where(lane < expert_count, high, gate - high)
    tail = jnp.where(lane < 2 * expert_count, tail, 0.0).astype(jnp.bfloat16)
    turned = lax.dot_general(
        identity(tok_dev).astype(jnp.bfloat16),
        tail,
        (((1,), (1,)), ((), ())),
        preferred_element_type=jnp.float32,
    )
    lane = lax.broadcasted_iota(jnp.int32, (tok_dev, lanes), 1)
    place = 2 * expert_count
    for number in (scale, -(scale**3) * along):
        for _ in range(3):
            addend = number.astype(jnp.bfloat16).astype(jnp.float32)
            turned = jnp.where(lane == place, addend, turned)
            number = number - addend
            place += 1
    pack[:, 3 * width :] = turned.astype(jnp.bfloat16)


def identity(size):
    rows = lax.broadcasted_iota(jnp.int32, (size, size), 0)
    return (rows == lax.broadcasted_iota(jnp.int32, (size, size), 1)).astype(jnp.float32)


def packed(tokens, norm_gain, probe_signs, cotangent, routes, gates, expert_count):
    tok_dev, width = tokens.shape
    tail = -(-(2 * expert_count + 6) // 128) * 128
    token_minor = (0, 2, 1)
    operands = (
        tokens,
        norm_gain.reshape(1, width),
        probe_signs,
        cotangent,
        jnp.transpose(routes, token_minor),
        jnp.transpose(gates, token_minor),
    )
    return pl.pallas_call(
        functools.partial(pack_kernel, expert_count),
        out_shape=jax.ShapeDtypeStruct((tok_dev, 3 * width + tail), jnp.bfloat16),
        in_specs=[pl.BlockSpec(memory_space=pl.ANY)] * 6,
        out_specs=pl.BlockSpec(memory_space=pltpu.VMEM),
        scratch_shapes=[pltpu.VMEM(array.shape, array.dtype) for array in operands]
        + [pltpu.SemaphoreType.DMA((6,))],
        compiler_params=pltpu.CompilerParams(vmem_limit_bytes=VMEM),
        cost_estimate=pl.CostEstimate(
            flops=20 * tok_dev * width, bytes_accessed=14 * tok_dev * width, transcendentals=0
        ),
    )(*(pltpu.with_memory_space_constraint(array, pltpu.HBM) for array in operands))


def join_kernel(own, other, held, sems):
    half = own.shape[2]
    copies = [
        pltpu.make_async_copy(
            source.at[part], held.at[part, :, pl.ds(h * half, half)], sems.at[h, part]
        )
        for h, source in enumerate((own, other))
        for part in range(3)
    ]
    for copy in copies:
        copy.start()
    for copy in copies:
        copy.wait()


def joined(own, other):
    parts, width, half = own.shape
    return pl.pallas_call(
        join_kernel,
        out_shape=pltpu.VMEM((parts, width, 2 * half), own.dtype),
        in_specs=[pl.BlockSpec(memory_space=pl.ANY)] * 2,
        out_specs=pl.BlockSpec(memory_space=pltpu.VMEM),
        scratch_shapes=[pltpu.SemaphoreType.DMA((2, parts))],
        compiler_params=pltpu.CompilerParams(vmem_limit_bytes=VMEM),
        cost_estimate=pl.CostEstimate(
            flops=0, bytes_accessed=8 * parts * width * half, transcendentals=0
        ),
    )(pltpu.with_memory_space_constraint(own, pltpu.HBM), other)


def expert_kernel(expert_count, gathered, held, *refs):
    count, tok_dev, lanes = gathered.shape
    outs, both, cotan, acc = (refs[:count], *refs[count:])
    _, width, hidden = held.shape
    turns = count // 2
    place = lax.axis_index("expert") // 2
    places = [
        lax.rem(place // 2 + turns - k, turns) * 2 + (lax.rem(place, 2) + flip) % 2
        for flip in range(2)
        for k in range(turns)
    ]
    rows = count * tok_dev

    def stacked(start, size):
        return jnp.concatenate(
            [gathered[place, :, start : start + size].astype(jnp.float32) for place in places], 0
        )

    both[:rows, :] = stacked(0, width).astype(jnp.bfloat16)
    both[rows:, :] = stacked(width, width).astype(jnp.bfloat16)
    cotan[...] = stacked(2 * width, width).astype(jnp.bfloat16)
    tail = stacked(3 * width, lanes - 3 * width)
    mine = lax.axis_index("expert") // 2
    lane = lax.broadcasted_iota(jnp.int32, tail.shape, 1)
    after = 2 * expert_count

    def picked(lanes):
        return jnp.sum(jnp.where(lanes, tail, 0.0), axis=1, keepdims=True)

    gate_row = picked((lane == mine) | (lane == mine + expert_count))
    scale_row = picked((lane >= after) & (lane < after + 3))
    slope_row = picked((lane >= after + 3) & (lane < after + 6))

    def weights(part, start, size):
        return held[part, :, start : start + size]

    block = 256 if hidden % 256 == 0 else 128
    contract = (((1,), (1,)), ((), ()))
    for start in range(0, hidden, block):
        pre_gate = jnp.dot(
            both[...], weights(0, start, block), preferred_element_type=jnp.float32
        )
        pre_up = jnp.dot(both[...], weights(1, start, block), preferred_element_type=jnp.float32)
        back = jnp.dot(cotan[...], weights(2, start, block), preferred_element_type=jnp.float32)
        gate, gate_t = (pre_gate[:rows], pre_gate[rows:])
        up, up_t = (pre_up[:rows], pre_up[rows:])
        sig = jax.nn.sigmoid(gate)
        act = gate * sig
        slope = sig * (1.0 + gate * (1.0 - sig))
        bend = sig * (1.0 - sig) * (2.0 + gate * (1.0 - 2.0 * sig))
        d_gate = (back * slope * up).astype(jnp.bfloat16)
        d_up = (back * act).astype(jnp.bfloat16)
        t_gate = (back * (bend * gate_t * up + slope * up_t)).astype(jnp.bfloat16)
        t_up = (back * slope * gate_t).astype(jnp.bfloat16)
        total = lax.dot_general(
            jnp.concatenate([d_gate, t_gate], 0),
            weights(0, start, block),
            contract,
            preferred_element_type=jnp.float32,
        )
        total = total + lax.dot_general(
            jnp.concatenate([d_up, t_up], 0),
            weights(1, start, block),
            contract,
            preferred_element_type=jnp.float32,
        )
        acc[...] = total if start == 0 else acc[...] + total
    for n in range(count):
        part = slice(n * tok_dev, (n + 1) * tok_dev)
        later = slice(rows + n * tok_dev, rows + (n + 1) * tok_dev)
        grad, tan = (acc[part] * gate_row[part], acc[later] * gate_row[part])
        scale, slope_r = (scale_row[part], slope_row[part])
        normed = gathered[places[n], :, :width].astype(jnp.float32)
        normed_t = gathered[places[n], :, width : 2 * width].astype(jnp.float32)
        outs[n][:, :width] = (scale * tan + slope_r * grad).astype(outs[n].dtype)
        first = jnp.mean(normed * grad, axis=1, keepdims=True)
        second = jnp.mean(normed * tan + normed_t * grad, axis=1, keepdims=True)
        second = (second - slope_r / scale * first) / scale
        lane = lax.broadcasted_iota(jnp.int32, (tok_dev, outs[n].shape[1] - width), 1)
        sums = jnp.where(lane == 0, first / scale, jnp.where(lane == 1, second, 0.0))
        outs[n][:, width:] = sums.astype(outs[n].dtype)


def experts(gathered, kinds, held, expert_count):
    count, tok_dev, _ = gathered.shape
    _, width, hidden = held.shape
    rows = count * tok_dev
    whole = pl.BlockSpec(memory_space=pltpu.VMEM)
    return pl.pallas_call(
        functools.partial(expert_kernel, expert_count),
        out_shape=[jax.ShapeDtypeStruct((tok_dev, width + 128), kind) for kind in kinds],
        in_specs=[whole] * 2,
        out_specs=[whole] * count,
        scratch_shapes=[
            pltpu.VMEM((2 * rows, width), jnp.bfloat16),
            pltpu.VMEM((rows, width), jnp.bfloat16),
            pltpu.VMEM((2 * rows, width), jnp.float32),
        ],
        compiler_params=pltpu.CompilerParams(vmem_limit_bytes=VMEM),
        cost_estimate=pl.CostEstimate(
            flops=2 * 9 * rows * width * hidden,
            bytes_accessed=6 * width * hidden,
            transcendentals=rows * hidden,
        ),
    )(gathered, pltpu.with_memory_space_constraint(held, pltpu.VMEM))


def finish_kernel(tokens, gain, signs, *refs):
    arrived, hvp, quad = (refs[:-2], refs[-2], refs[-1])
    width = tokens.shape[1]
    xf = tokens[...].astype(jnp.float32)
    probe = (2 * signs[...] - 1).astype(jnp.float32)
    scale, along = rms_terms(xf, probe)
    slope_r = -(scale**3) * along
    rows = sum(part[...].astype(jnp.float32) for part in arrived)
    first = rows[:, width : width + 1]
    second = rows[:, width + 1 : width + 2]
    whole = (
        gain[...] * rows[:, :width]
        - 3.0 * scale**2 * slope_r * first * xf
        - scale**3 * first * probe
        - scale**3 * second * xf
    )
    hvp[...] = whole
    column = jnp.mean(probe * whole, axis=1, keepdims=True)
    tok_dev = column.shape[0]
    quad[...] = jnp.sum(identity(tok_dev) * column, axis=0, keepdims=True)


def moved(rows, turns, flip_x=False, flip_core=False):
    count = lax.axis_size("expert")
    pairs = [
        (i, (i + 4 * turns) % count ^ (2 * flip_x) ^ (1 * flip_core)) for i in range(count)
    ]
    return lax.ppermute(rows, "expert", pairs)


def dense_local(tokens, norm_gain, probe_signs, cotangent, routes, gates, weights):
    tok_dev, width = tokens.shape
    n_exp = lax.axis_size("expert")
    expert_count = n_exp // 2
    pack = packed(tokens, norm_gain, probe_signs, cotangent, routes, gates, expert_count)
    held = joined(weights, moved(weights, 0, flip_core=True))
    parity = [list(range(core, n_exp, 2)) for core in range(2)]
    gathered = lax.all_gather(pack, "expert", axis_index_groups=parity)
    wide, sent = (jnp.float32, jnp.bfloat16)
    results = experts(gathered, [wide] * 4 + [sent] * 4, held, expert_count)
    here, there = (results[:4], results[4:])

    def total(*parts):
        return sum(part.astype(jnp.float32) for part in parts).astype(jnp.bfloat16)

    beside = {k: moved(there[k], 0, flip_x=True) for k in (2, 1, 3, 0)}
    forward = moved(total(here[2], beside[2]), -1)
    arrived = [
        here[0],
        beside[0],
        moved(total(here[1], beside[1], forward), -1),
        moved(total(here[3], beside[3]), 1),
    ]
    hvp, quad = pl.pallas_call(
        finish_kernel,
        out_shape=[
            jax.ShapeDtypeStruct((tok_dev, width), jnp.float32),
            jax.ShapeDtypeStruct((1, tok_dev), jnp.float32),
        ],
        compiler_params=pltpu.CompilerParams(vmem_limit_bytes=VMEM),
        cost_estimate=pl.CostEstimate(
            flops=40 * tok_dev * width, bytes_accessed=26 * tok_dev * width, transcendentals=0
        ),
    )(tokens, norm_gain.reshape(1, width), probe_signs, *arrived)
    return (hvp, quad.reshape(tok_dev))


def routed_rows(normed, normed_t, cotangent, routes, gates, weights):
    tok_dev, width = normed.shape
    groups_here = routes.shape[0]
    half = routes.shape[2]
    n_exp = lax.axis_size("expert")
    expert_count = n_exp // 2
    cap = capacity(tok_dev, half, expert_count)
    buffer_rows = expert_count * cap
    stack_z, stack_t, stack_c, stack_w = ([], [], [], [])
    for group in range(groups_here):
        target = slot_targets(routes[group], expert_count, cap)
        place = (jnp.arange(buffer_rows, dtype=jnp.int32)[:, None] == target[None, :]).reshape(
            buffer_rows, tok_dev, half
        )
        place_tok = jnp.sum(place.astype(jnp.float32), axis=2).astype(jnp.bfloat16)
        stack_w.append(jnp.sum(place.astype(jnp.float32) * gates[group][None, :, :], axis=2))
        stack_z.append(
            jnp.dot(place_tok, normed, preferred_element_type=jnp.float32).astype(jnp.bfloat16)
        )
        stack_t.append(
            jnp.dot(place_tok, normed_t, preferred_element_type=jnp.float32).astype(jnp.bfloat16)
        )
        stack_c.append(
            jnp.dot(place_tok, cotangent, preferred_element_type=jnp.float32).astype(jnp.bfloat16)
        )
    rows_z = jnp.stack(stack_z, 0)
    rows_t = jnp.stack(stack_t, 0)
    rows_c = jnp.stack(stack_c, 0)
    weighted = jnp.stack(stack_w, 0)

    def arrange(rows):
        shaped = rows.reshape(groups_here, expert_count, 1, cap, width)
        shaped = jnp.broadcast_to(shaped, (groups_here, expert_count, 2, cap, width))
        return jnp.transpose(shaped, (1, 2, 0, 3, 4)).reshape(n_exp, groups_here * cap, width)

    send_z, send_t, send_c = (arrange(rows_z), arrange(rows_t), arrange(rows_c))
    got_z = lax.all_to_all(send_z, "expert", split_axis=0, concat_axis=0, tiled=True)
    got_t = lax.all_to_all(send_t, "expert", split_axis=0, concat_axis=0, tiled=True)
    got_c = lax.all_to_all(send_c, "expert", split_axis=0, concat_axis=0, tiled=True)
    sources, items, cols = got_z.shape
    g_rows, t_rows = expert_terms(
        weights, got_z.reshape(-1, cols), got_t.reshape(-1, cols), got_c.reshape(-1, cols)
    )
    g_rows = g_rows.reshape(sources, items, cols)
    t_rows = t_rows.reshape(sources, items, cols)
    back_g = lax.all_to_all(g_rows, "expert", split_axis=0, concat_axis=0, tiled=True)
    back_t = lax.all_to_all(t_rows, "expert", split_axis=0, concat_axis=0, tiled=True)

    def restore(rows):
        shaped = jnp.sum(rows.reshape(expert_count, 2, groups_here, cap, width), axis=1)
        return jnp.transpose(shaped, (1, 0, 2, 3)).reshape(groups_here, buffer_rows, width)

    back_g = restore(back_g)
    back_t = restore(back_t)
    contract = (((0, 1), (0, 1)), ((), ()))
    grad_z = lax.dot_general(weighted, back_g, contract, precision=lax.Precision.HIGHEST)
    tan_z = lax.dot_general(weighted, back_t, contract, precision=lax.Precision.HIGHEST)
    return (grad_z, tan_z)


def local(tokens, norm_gain, probe_signs, cotangent, routes, gates, expert_weights):
    cap = capacity(tokens.shape[0], routes.shape[2], lax.axis_size("expert") // 2)
    layout = (lax.axis_size("expert"), lax.axis_size("node"))
    if layout == (16, 1) and routes.shape[0] * cap >= tokens.shape[0]:
        return dense_local(
            tokens, norm_gain, probe_signs, cotangent, routes, gates, expert_weights
        )
    xf = tokens.astype(jnp.float32)
    probe = (2 * probe_signs - 1).astype(jnp.float32)
    tok_dev, width = xf.shape
    scale = lax.rsqrt(jnp.mean(xf * xf, axis=1, keepdims=True) + EPS)
    along = jnp.mean(xf * probe, axis=1, keepdims=True)
    normed = (xf * scale * norm_gain).astype(jnp.bfloat16)
    normed_t = (norm_gain * (scale * probe - scale**3 * xf * along)).astype(jnp.bfloat16)
    own_half = lax.all_gather(expert_weights, "node", axis=2, tiled=True)
    grad_z, tan_z = routed_rows(normed, normed_t, cotangent, routes, gates, own_half)
    share = width // lax.axis_size("node")
    start = lax.axis_index("node") * share
    slope_r = -(scale**3) * along
    grad_z, tan_z = lax.psum((grad_z, tan_z), "node")
    lifted = norm_gain * grad_z
    lifted_t = norm_gain * tan_z
    first = jnp.mean(xf * lifted, axis=1, keepdims=True)
    second = jnp.mean(xf * lifted_t, axis=1, keepdims=True)
    third = jnp.mean(probe * lifted, axis=1, keepdims=True)
    whole_hvp = (
        scale * lifted_t
        + slope_r * lifted
        - 3.0 * scale**2 * slope_r * first * xf
        - scale**3 * first * probe
        - scale**3 * (second + third) * xf
    )
    quad = jnp.mean(probe * whole_hvp, axis=1)
    hvp = lax.dynamic_slice_in_dim(whole_hvp, start, share, 1)
    return (hvp, quad)


def solution(mesh):
    placed = (
        P(("groups", "expert"), None),
        P(),
        P(("groups", "expert"), None),
        P(("groups", "expert"), None),
        P("node", ("groups", "expert"), None),
        P("node", ("groups", "expert"), None),
        P(None, None, ("expert", "node")),
    )
    return jax.shard_map(
        local,
        mesh=mesh,
        in_specs=placed,
        out_specs=(P(("groups", "expert"), "node"), P(("groups", "expert"))),
        check_vma=False,
    )
```

```python
import functools

import jax
import jax.numpy as jnp
from jax import lax
from jax.experimental import pallas as pl
from jax.experimental.pallas import tpu as pltpu
from jax.sharding import PartitionSpec as P

EPS = 1e-06
VMEM = 24 * 1024 * 1024


def expert_terms(weights, rows, rows_t, cotan):
    count = rows.shape[0]
    both = jnp.concatenate([rows, rows_t], 0)
    pre_gate = jnp.dot(both, weights[0], preferred_element_type=jnp.float32)
    pre_up = jnp.dot(both, weights[1], preferred_element_type=jnp.float32)
    gate, gate_t = (pre_gate[:count], pre_gate[count:])
    up, up_t = (pre_up[:count], pre_up[count:])
    back = jnp.dot(cotan, weights[2], preferred_element_type=jnp.float32)
    sig = jax.nn.sigmoid(gate)
    act = gate * sig
    slope = sig * (1.0 + gate * (1.0 - sig))
    bend = sig * (1.0 - sig) * (2.0 + gate * (1.0 - 2.0 * sig))
    d_gate = (back * slope * up).astype(jnp.bfloat16)
    d_up = (back * act).astype(jnp.bfloat16)
    t_gate = (back * (bend * gate_t * up + slope * up_t)).astype(jnp.bfloat16)
    t_up = (back * slope * gate_t).astype(jnp.bfloat16)
    contract = (((1,), (1,)), ((), ()))
    lhs_gate = jnp.concatenate([d_gate, t_gate], 0)
    lhs_up = jnp.concatenate([d_up, t_up], 0)
    total = lax.dot_general(lhs_gate, weights[0], contract, preferred_element_type=jnp.float32)
    total = total + lax.dot_general(
        lhs_up, weights[1], contract, preferred_element_type=jnp.float32
    )
    return (total[:count], total[count:])


def slot_targets(route_ids, expert_count, capacity):
    flat = route_ids.reshape(-1)
    count = flat.shape[0]
    onehot = (flat[:, None] == jnp.arange(expert_count, dtype=jnp.int32)[None, :]).astype(
        jnp.float32
    )
    lower = (jnp.arange(count)[:, None] > jnp.arange(count)[None, :]).astype(jnp.float32)
    before = jnp.dot(lower, onehot, precision=lax.Precision.HIGHEST)
    rank = jnp.sum(before * onehot, axis=1).astype(jnp.int32)
    return flat * capacity + rank


def capacity(tok_dev, half, expert_count):
    return min(2 * ((2 * tok_dev * half + 3 * expert_count - 1) // (3 * expert_count)), tok_dev)


def rms_terms(xf, probe):
    scale = lax.rsqrt(jnp.mean(xf * xf, axis=1, keepdims=True) + EPS)
    along = jnp.mean(xf * probe, axis=1, keepdims=True)
    return scale, along


def pack_kernel(expert_count, *refs):
    sources, pack, held, sems = (refs[:6], refs[6], refs[7:13], refs[13])
    copies = [
        pltpu.make_async_copy(source, target, sems.at[n])
        for n, (source, target) in enumerate(zip(sources, held))
    ]
    for copy in copies:
        copy.start()
    for copy in copies:
        copy.wait()
    tokens, gain, signs, cotangent, routes, gates = held
    width = tokens.shape[1]
    xf = tokens[...].astype(jnp.float32)
    probe = (2 * signs[...] - 1).astype(jnp.float32)
    scale, along = rms_terms(xf, probe)
    pack[:, :width] = (xf * scale * gain[...]).astype(jnp.bfloat16)
    tangent = gain[...] * (scale * probe - scale**3 * xf * along)
    pack[:, width : 2 * width] = tangent.astype(jnp.bfloat16)
    pack[:, 2 * width : 3 * width] = cotangent[...]
    tok_dev, lanes = (tokens.shape[0], pack.shape[1] - 3 * width)
    lane = lax.broadcasted_iota(jnp.int32, (lanes, tok_dev), 0)
    expert = lax.rem(lane, expert_count)
    gate = jnp.zeros(lane.shape, jnp.float32)
    for group in range(routes.shape[0]):
        for slot in range(routes.shape[1]):
            named = routes[group, slot : slot + 1, :] == expert
            gate = gate + jnp.where(named, gates[group, slot : slot + 1, :], 0.0)
    high = gate.astype(jnp.bfloat16).astype(jnp.float32)
    tail = jnp.where(lane < expert_count, high, gate - high)
    tail = jnp.where(lane < 2 * expert_count, tail, 0.0).astype(jnp.bfloat16)
    turned = lax.dot_general(
        identity(tok_dev).astype(jnp.bfloat16),
        tail,
        (((1,), (1,)), ((), ())),
        preferred_element_type=jnp.float32,
    )
    lane = lax.broadcasted_iota(jnp.int32, (tok_dev, lanes), 1)
    place = 2 * expert_count
    for number in (scale, -(scale**3) * along):
        for _ in range(3):
            addend = number.astype(jnp.bfloat16).astype(jnp.float32)
            turned = jnp.where(lane == place, addend, turned)
            number = number - addend
            place += 1
    pack[:, 3 * width :] = turned.astype(jnp.bfloat16)


def identity(size):
    rows = lax.broadcasted_iota(jnp.int32, (size, size), 0)
    return (rows == lax.broadcasted_iota(jnp.int32, (size, size), 1)).astype(jnp.float32)


def packed(tokens, norm_gain, probe_signs, cotangent, routes, gates, expert_count):
    tok_dev, width = tokens.shape
    tail = -(-(2 * expert_count + 6) // 128) * 128
    token_minor = (0, 2, 1)
    operands = (
        tokens,
        norm_gain.reshape(1, width),
        probe_signs,
        cotangent,
        jnp.transpose(routes, token_minor),
        jnp.transpose(gates, token_minor),
    )
    return pl.pallas_call(
        functools.partial(pack_kernel, expert_count),
        out_shape=jax.ShapeDtypeStruct((tok_dev, 3 * width + tail), jnp.bfloat16),
        in_specs=[pl.BlockSpec(memory_space=pl.ANY)] * 6,
        out_specs=pl.BlockSpec(memory_space=pltpu.VMEM),
        scratch_shapes=[pltpu.VMEM(array.shape, array.dtype) for array in operands]
        + [pltpu.SemaphoreType.DMA((6,))],
        compiler_params=pltpu.CompilerParams(vmem_limit_bytes=VMEM),
        cost_estimate=pl.CostEstimate(
            flops=20 * tok_dev * width, bytes_accessed=14 * tok_dev * width, transcendentals=0
        ),
    )(*(pltpu.with_memory_space_constraint(array, pltpu.HBM) for array in operands))


def join_kernel(own, other, held, sems):
    half = own.shape[2]
    copies = [
        pltpu.make_async_copy(
            source.at[part], held.at[part, :, pl.ds(h * half, half)], sems.at[h, part]
        )
        for h, source in enumerate((own, other))
        for part in range(3)
    ]
    for copy in copies:
        copy.start()
    for copy in copies:
        copy.wait()


def joined(own, other):
    parts, width, half = own.shape
    return pl.pallas_call(
        join_kernel,
        out_shape=pltpu.VMEM((parts, width, 2 * half), own.dtype),
        in_specs=[pl.BlockSpec(memory_space=pl.ANY)] * 2,
        out_specs=pl.BlockSpec(memory_space=pltpu.VMEM),
        scratch_shapes=[pltpu.SemaphoreType.DMA((2, parts))],
        compiler_params=pltpu.CompilerParams(vmem_limit_bytes=VMEM),
        cost_estimate=pl.CostEstimate(
            flops=0, bytes_accessed=8 * parts * width * half, transcendentals=0
        ),
    )(pltpu.with_memory_space_constraint(own, pltpu.HBM), other)


def expert_kernel(count, expert_count, *refs):
    packs, held, outs = (refs[:count], refs[count], refs[count + 1 : 2 * count + 1])
    both, cotan, acc = refs[2 * count + 1 :]
    tok_dev = packs[0].shape[0]
    _, width, hidden = held.shape
    rows = count * tok_dev

    def stacked(start, size):
        return jnp.concatenate([p[:, start : start + size].astype(jnp.float32) for p in packs], 0)

    both[:rows, :] = stacked(0, width).astype(jnp.bfloat16)
    both[rows:, :] = stacked(width, width).astype(jnp.bfloat16)
    cotan[...] = stacked(2 * width, width).astype(jnp.bfloat16)
    tail = stacked(3 * width, packs[0].shape[1] - 3 * width)
    mine = lax.axis_index("expert") // 2
    lane = lax.broadcasted_iota(jnp.int32, tail.shape, 1)
    after = 2 * expert_count

    def picked(lanes):
        return jnp.sum(jnp.where(lanes, tail, 0.0), axis=1, keepdims=True)

    gate_row = picked((lane == mine) | (lane == mine + expert_count))
    scale_row = picked((lane >= after) & (lane < after + 3))
    slope_row = picked((lane >= after + 3) & (lane < after + 6))

    def weights(part, start, size):
        return held[part, :, start : start + size]

    block = 256 if hidden % 256 == 0 else 128
    contract = (((1,), (1,)), ((), ()))
    for start in range(0, hidden, block):
        pre_gate = jnp.dot(
            both[...], weights(0, start, block), preferred_element_type=jnp.float32
        )
        pre_up = jnp.dot(both[...], weights(1, start, block), preferred_element_type=jnp.float32)
        back = jnp.dot(cotan[...], weights(2, start, block), preferred_element_type=jnp.float32)
        gate, gate_t = (pre_gate[:rows], pre_gate[rows:])
        up, up_t = (pre_up[:rows], pre_up[rows:])
        sig = jax.nn.sigmoid(gate)
        act = gate * sig
        slope = sig * (1.0 + gate * (1.0 - sig))
        bend = sig * (1.0 - sig) * (2.0 + gate * (1.0 - 2.0 * sig))
        d_gate = (back * slope * up).astype(jnp.bfloat16)
        d_up = (back * act).astype(jnp.bfloat16)
        t_gate = (back * (bend * gate_t * up + slope * up_t)).astype(jnp.bfloat16)
        t_up = (back * slope * gate_t).astype(jnp.bfloat16)
        total = lax.dot_general(
            jnp.concatenate([d_gate, t_gate], 0),
            weights(0, start, block),
            contract,
            preferred_element_type=jnp.float32,
        )
        total = total + lax.dot_general(
            jnp.concatenate([d_up, t_up], 0),
            weights(1, start, block),
            contract,
            preferred_element_type=jnp.float32,
        )
        acc[...] = total if start == 0 else acc[...] + total
    for n in range(count):
        part = slice(n * tok_dev, (n + 1) * tok_dev)
        later = slice(rows + n * tok_dev, rows + (n + 1) * tok_dev)
        grad, tan = (acc[part] * gate_row[part], acc[later] * gate_row[part])
        scale, slope_r = (scale_row[part], slope_row[part])
        normed = packs[n][:, :width].astype(jnp.float32)
        normed_t = packs[n][:, width : 2 * width].astype(jnp.float32)
        outs[n][:, :width] = (scale * tan + slope_r * grad).astype(outs[n].dtype)
        first = jnp.mean(normed * grad, axis=1, keepdims=True)
        second = jnp.mean(normed * tan + normed_t * grad, axis=1, keepdims=True)
        second = (second - slope_r / scale * first) / scale
        lane = lax.broadcasted_iota(jnp.int32, (tok_dev, outs[n].shape[1] - width), 1)
        sums = jnp.where(lane == 0, first / scale, jnp.where(lane == 1, second, 0.0))
        outs[n][:, width:] = sums.astype(outs[n].dtype)


def experts(packs, kinds, held, expert_count):
    count = len(packs)
    tok_dev = packs[0].shape[0]
    _, width, hidden = held.shape
    rows = count * tok_dev
    whole = pl.BlockSpec(memory_space=pltpu.VMEM)
    return pl.pallas_call(
        functools.partial(expert_kernel, count, expert_count),
        out_shape=[jax.ShapeDtypeStruct((tok_dev, width + 128), kind) for kind in kinds],
        in_specs=[whole] * (count + 1),
        out_specs=[whole] * count,
        scratch_shapes=[
            pltpu.VMEM((2 * rows, width), jnp.bfloat16),
            pltpu.VMEM((rows, width), jnp.bfloat16),
            pltpu.VMEM((2 * rows, width), jnp.float32),
        ],
        compiler_params=pltpu.CompilerParams(vmem_limit_bytes=VMEM),
        cost_estimate=pl.CostEstimate(
            flops=2 * 9 * rows * width * hidden,
            bytes_accessed=6 * width * hidden,
            transcendentals=rows * hidden,
        ),
    )(*packs, pltpu.with_memory_space_constraint(held, pltpu.VMEM))


def finish_kernel(tokens, gain, signs, *refs):
    arrived, hvp, quad = (refs[:-2], refs[-2], refs[-1])
    width = tokens.shape[1]
    xf = tokens[...].astype(jnp.float32)
    probe = (2 * signs[...] - 1).astype(jnp.float32)
    scale, along = rms_terms(xf, probe)
    slope_r = -(scale**3) * along
    rows = sum(part[...].astype(jnp.float32) for part in arrived)
    first = rows[:, width : width + 1]
    second = rows[:, width + 1 : width + 2]
    whole = (
        gain[...] * rows[:, :width]
        - 3.0 * scale**2 * slope_r * first * xf
        - scale**3 * first * probe
        - scale**3 * second * xf
    )
    hvp[...] = whole
    column = jnp.mean(probe * whole, axis=1, keepdims=True)
    tok_dev = column.shape[0]
    quad[...] = jnp.sum(identity(tok_dev) * column, axis=0, keepdims=True)


def moved(rows, turns, flip_x=False, flip_core=False):
    count = lax.axis_size("expert")
    pairs = [
        (i, (i + 4 * turns) % count ^ (2 * flip_x) ^ (1 * flip_core)) for i in range(count)
    ]
    return lax.ppermute(rows, "expert", pairs)


def dense_local(tokens, norm_gain, probe_signs, cotangent, routes, gates, weights):
    tok_dev, width = tokens.shape
    n_exp = lax.axis_size("expert")
    expert_count = n_exp // 2
    pack = packed(tokens, norm_gain, probe_signs, cotangent, routes, gates, expert_count)
    held = joined(weights, moved(weights, 0, flip_core=True))
    same, across = {0: pack}, {}
    same[1] = moved(pack, 1)
    across[0] = moved(pack, 0, flip_x=True)
    same[1] = lax.optimization_barrier((same[1], across[0]))[0]
    same[3] = moved(pack, -1)
    same[2] = moved(same[1], 1)
    across[1] = moved(same[1], 0, flip_x=True)
    same[3] = lax.optimization_barrier((same[3], held))[0]
    across[3] = moved(same[3], 0, flip_x=True)
    across[2] = moved(same[2], 0, flip_x=True)
    wide, sent = (jnp.float32, jnp.bfloat16)
    here, there = {}, {}
    here[0], here[1], here[2], here[3], there[0], there[1] = experts(
        [same[0], same[1], same[2], same[3], across[0], across[1]],
        [wide, wide, sent, sent, sent, sent],
        held,
        expert_count,
    )
    late = lax.optimization_barrier((across[2], across[3], here[1]))[:2]
    there[2], there[3] = experts(late, [sent, sent], held, expert_count)

    def flipped(rows):
        return moved(rows, 0, flip_x=True)

    def total(*parts):
        return sum(part.astype(jnp.float32) for part in parts).astype(jnp.bfloat16)

    beside = flipped(there[1])
    kept = lax.optimization_barrier((here[1], there[2]))[0]
    arrived = [
        here[0],
        flipped(there[0]),
        moved(here[2], 2),
        moved(here[3], 1),
        moved(there[2], 2, flip_x=True),
        moved(there[3], 1, flip_x=True),
        moved(total(kept, beside), -1),
    ]
    hvp, quad = pl.pallas_call(
        finish_kernel,
        out_shape=[
            jax.ShapeDtypeStruct((tok_dev, width), jnp.float32),
            jax.ShapeDtypeStruct((1, tok_dev), jnp.float32),
        ],
        compiler_params=pltpu.CompilerParams(vmem_limit_bytes=VMEM),
        cost_estimate=pl.CostEstimate(
            flops=40 * tok_dev * width, bytes_accessed=26 * tok_dev * width, transcendentals=0
        ),
    )(tokens, norm_gain.reshape(1, width), probe_signs, *arrived)
    return (hvp, quad.reshape(tok_dev))


def routed_rows(normed, normed_t, cotangent, routes, gates, weights):
    tok_dev, width = normed.shape
    groups_here = routes.shape[0]
    half = routes.shape[2]
    n_exp = lax.axis_size("expert")
    expert_count = n_exp // 2
    cap = capacity(tok_dev, half, expert_count)
    buffer_rows = expert_count * cap
    stack_z, stack_t, stack_c, stack_w = ([], [], [], [])
    for group in range(groups_here):
        target = slot_targets(routes[group], expert_count, cap)
        place = (jnp.arange(buffer_rows, dtype=jnp.int32)[:, None] == target[None, :]).reshape(
            buffer_rows, tok_dev, half
        )
        place_tok = jnp.sum(place.astype(jnp.float32), axis=2).astype(jnp.bfloat16)
        stack_w.append(jnp.sum(place.astype(jnp.float32) * gates[group][None, :, :], axis=2))
        stack_z.append(
            jnp.dot(place_tok, normed, preferred_element_type=jnp.float32).astype(jnp.bfloat16)
        )
        stack_t.append(
            jnp.dot(place_tok, normed_t, preferred_element_type=jnp.float32).astype(jnp.bfloat16)
        )
        stack_c.append(
            jnp.dot(place_tok, cotangent, preferred_element_type=jnp.float32).astype(jnp.bfloat16)
        )
    rows_z = jnp.stack(stack_z, 0)
    rows_t = jnp.stack(stack_t, 0)
    rows_c = jnp.stack(stack_c, 0)
    weighted = jnp.stack(stack_w, 0)

    def arrange(rows):
        shaped = rows.reshape(groups_here, expert_count, 1, cap, width)
        shaped = jnp.broadcast_to(shaped, (groups_here, expert_count, 2, cap, width))
        return jnp.transpose(shaped, (1, 2, 0, 3, 4)).reshape(n_exp, groups_here * cap, width)

    send_z, send_t, send_c = (arrange(rows_z), arrange(rows_t), arrange(rows_c))
    got_z = lax.all_to_all(send_z, "expert", split_axis=0, concat_axis=0, tiled=True)
    got_t = lax.all_to_all(send_t, "expert", split_axis=0, concat_axis=0, tiled=True)
    got_c = lax.all_to_all(send_c, "expert", split_axis=0, concat_axis=0, tiled=True)
    sources, items, cols = got_z.shape
    g_rows, t_rows = expert_terms(
        weights, got_z.reshape(-1, cols), got_t.reshape(-1, cols), got_c.reshape(-1, cols)
    )
    g_rows = g_rows.reshape(sources, items, cols)
    t_rows = t_rows.reshape(sources, items, cols)
    back_g = lax.all_to_all(g_rows, "expert", split_axis=0, concat_axis=0, tiled=True)
    back_t = lax.all_to_all(t_rows, "expert", split_axis=0, concat_axis=0, tiled=True)

    def restore(rows):
        shaped = jnp.sum(rows.reshape(expert_count, 2, groups_here, cap, width), axis=1)
        return jnp.transpose(shaped, (1, 0, 2, 3)).reshape(groups_here, buffer_rows, width)

    back_g = restore(back_g)
    back_t = restore(back_t)
    contract = (((0, 1), (0, 1)), ((), ()))
    grad_z = lax.dot_general(weighted, back_g, contract, precision=lax.Precision.HIGHEST)
    tan_z = lax.dot_general(weighted, back_t, contract, precision=lax.Precision.HIGHEST)
    return (grad_z, tan_z)


def local(tokens, norm_gain, probe_signs, cotangent, routes, gates, expert_weights):
    cap = capacity(tokens.shape[0], routes.shape[2], lax.axis_size("expert") // 2)
    layout = (lax.axis_size("expert"), lax.axis_size("node"))
    if layout == (16, 1) and routes.shape[0] * cap >= tokens.shape[0]:
        return dense_local(
            tokens, norm_gain, probe_signs, cotangent, routes, gates, expert_weights
        )
    xf = tokens.astype(jnp.float32)
    probe = (2 * probe_signs - 1).astype(jnp.float32)
    tok_dev, width = xf.shape
    scale = lax.rsqrt(jnp.mean(xf * xf, axis=1, keepdims=True) + EPS)
    along = jnp.mean(xf * probe, axis=1, keepdims=True)
    normed = (xf * scale * norm_gain).astype(jnp.bfloat16)
    normed_t = (norm_gain * (scale * probe - scale**3 * xf * along)).astype(jnp.bfloat16)
    own_half = lax.all_gather(expert_weights, "node", axis=2, tiled=True)
    grad_z, tan_z = routed_rows(normed, normed_t, cotangent, routes, gates, own_half)
    share = width // lax.axis_size("node")
    start = lax.axis_index("node") * share
    slope_r = -(scale**3) * along
    grad_z, tan_z = lax.psum((grad_z, tan_z), "node")
    lifted = norm_gain * grad_z
    lifted_t = norm_gain * tan_z
    first = jnp.mean(xf * lifted, axis=1, keepdims=True)
    second = jnp.mean(xf * lifted_t, axis=1, keepdims=True)
    third = jnp.mean(probe * lifted, axis=1, keepdims=True)
    whole_hvp = (
        scale * lifted_t
        + slope_r * lifted
        - 3.0 * scale**2 * slope_r * first * xf
        - scale**3 * first * probe
        - scale**3 * (second + third) * xf
    )
    quad = jnp.mean(probe * whole_hvp, axis=1)
    hvp = lax.dynamic_slice_in_dim(whole_hvp, start, share, 1)
    return (hvp, quad)


def solution(mesh):
    placed = (
        P(("groups", "expert"), None),
        P(),
        P(("groups", "expert"), None),
        P(("groups", "expert"), None),
        P("node", ("groups", "expert"), None),
        P("node", ("groups", "expert"), None),
        P(None, None, ("expert", "node")),
    )
    return jax.shard_map(
        local,
        mesh=mesh,
        in_specs=placed,
        out_specs=(P(("groups", "expert"), "node"), P(("groups", "expert"))),
        check_vma=False,
    )
```

```python
import functools

import jax
import jax.numpy as jnp
from jax import lax
from jax.experimental import pallas as pl
from jax.experimental.pallas import tpu as pltpu
from jax.sharding import PartitionSpec as P

EPS = 1e-06
VMEM = 24 * 1024 * 1024


def expert_terms(weights, rows, rows_t, cotan):
    count = rows.shape[0]
    both = jnp.concatenate([rows, rows_t], 0)
    pre_gate = jnp.dot(both, weights[0], preferred_element_type=jnp.float32)
    pre_up = jnp.dot(both, weights[1], preferred_element_type=jnp.float32)
    gate, gate_t = (pre_gate[:count], pre_gate[count:])
    up, up_t = (pre_up[:count], pre_up[count:])
    back = jnp.dot(cotan, weights[2], preferred_element_type=jnp.float32)
    sig = jax.nn.sigmoid(gate)
    act = gate * sig
    slope = sig * (1.0 + gate * (1.0 - sig))
    bend = sig * (1.0 - sig) * (2.0 + gate * (1.0 - 2.0 * sig))
    d_gate = (back * slope * up).astype(jnp.bfloat16)
    d_up = (back * act).astype(jnp.bfloat16)
    t_gate = (back * (bend * gate_t * up + slope * up_t)).astype(jnp.bfloat16)
    t_up = (back * slope * gate_t).astype(jnp.bfloat16)
    contract = (((1,), (1,)), ((), ()))
    lhs_gate = jnp.concatenate([d_gate, t_gate], 0)
    lhs_up = jnp.concatenate([d_up, t_up], 0)
    total = lax.dot_general(lhs_gate, weights[0], contract, preferred_element_type=jnp.float32)
    total = total + lax.dot_general(
        lhs_up, weights[1], contract, preferred_element_type=jnp.float32
    )
    return (total[:count], total[count:])


def slot_targets(route_ids, expert_count, capacity):
    flat = route_ids.reshape(-1)
    count = flat.shape[0]
    onehot = (flat[:, None] == jnp.arange(expert_count, dtype=jnp.int32)[None, :]).astype(
        jnp.float32
    )
    lower = (jnp.arange(count)[:, None] > jnp.arange(count)[None, :]).astype(jnp.float32)
    before = jnp.dot(lower, onehot, precision=lax.Precision.HIGHEST)
    rank = jnp.sum(before * onehot, axis=1).astype(jnp.int32)
    return flat * capacity + rank


def capacity(tok_dev, half, expert_count):
    return min(2 * ((2 * tok_dev * half + 3 * expert_count - 1) // (3 * expert_count)), tok_dev)


def rms_terms(xf, probe):
    scale = lax.rsqrt(jnp.mean(xf * xf, axis=1, keepdims=True) + EPS)
    along = jnp.mean(xf * probe, axis=1, keepdims=True)
    return scale, along


def pack_kernel(expert_count, *refs):
    sources, pack, held, sems = (refs[:6], refs[6], refs[7:13], refs[13])
    copies = [
        pltpu.make_async_copy(source, target, sems.at[n])
        for n, (source, target) in enumerate(zip(sources, held))
    ]
    for copy in copies:
        copy.start()
    for copy in copies:
        copy.wait()
    tokens, gain, signs, cotangent, routes, gates = held
    width = tokens.shape[1]
    xf = tokens[...].astype(jnp.float32)
    probe = (2 * signs[...] - 1).astype(jnp.float32)
    scale, along = rms_terms(xf, probe)
    pack[:, :width] = (xf * scale * gain[...]).astype(jnp.bfloat16)
    tangent = gain[...] * (scale * probe - scale**3 * xf * along)
    pack[:, width : 2 * width] = tangent.astype(jnp.bfloat16)
    pack[:, 2 * width : 3 * width] = cotangent[...]
    tok_dev, lanes = (tokens.shape[0], pack.shape[1] - 3 * width)
    lane = lax.broadcasted_iota(jnp.int32, (lanes, tok_dev), 0)
    expert = lax.rem(lane, expert_count)
    gate = jnp.zeros(lane.shape, jnp.float32)
    for group in range(routes.shape[0]):
        for slot in range(routes.shape[1]):
            named = routes[group, slot : slot + 1, :] == expert
            gate = gate + jnp.where(named, gates[group, slot : slot + 1, :], 0.0)
    high = gate.astype(jnp.bfloat16).astype(jnp.float32)
    tail = jnp.where(lane < expert_count, high, gate - high)
    tail = jnp.where(lane < 2 * expert_count, tail, 0.0).astype(jnp.bfloat16)
    turned = lax.dot_general(
        identity(tok_dev).astype(jnp.bfloat16),
        tail,
        (((1,), (1,)), ((), ())),
        preferred_element_type=jnp.float32,
    )
    lane = lax.broadcasted_iota(jnp.int32, (tok_dev, lanes), 1)
    place = 2 * expert_count
    for number in (scale, -(scale**3) * along):
        for _ in range(3):
            addend = number.astype(jnp.bfloat16).astype(jnp.float32)
            turned = jnp.where(lane == place, addend, turned)
            number = number - addend
            place += 1
    pack[:, 3 * width :] = turned.astype(jnp.bfloat16)


def identity(size):
    rows = lax.broadcasted_iota(jnp.int32, (size, size), 0)
    return (rows == lax.broadcasted_iota(jnp.int32, (size, size), 1)).astype(jnp.float32)


def packed(tokens, norm_gain, probe_signs, cotangent, routes, gates, expert_count):
    tok_dev, width = tokens.shape
    tail = -(-(2 * expert_count + 6) // 128) * 128
    token_minor = (0, 2, 1)
    operands = (
        tokens,
        norm_gain.reshape(1, width),
        probe_signs,
        cotangent,
        jnp.transpose(routes, token_minor),
        jnp.transpose(gates, token_minor),
    )
    return pl.pallas_call(
        functools.partial(pack_kernel, expert_count),
        out_shape=jax.ShapeDtypeStruct((tok_dev, 3 * width + tail), jnp.bfloat16),
        in_specs=[pl.BlockSpec(memory_space=pl.ANY)] * 6,
        out_specs=pl.BlockSpec(memory_space=pltpu.VMEM),
        scratch_shapes=[pltpu.VMEM(array.shape, array.dtype) for array in operands]
        + [pltpu.SemaphoreType.DMA((6,))],
        compiler_params=pltpu.CompilerParams(vmem_limit_bytes=VMEM),
        cost_estimate=pl.CostEstimate(
            flops=20 * tok_dev * width, bytes_accessed=14 * tok_dev * width, transcendentals=0
        ),
    )(*(pltpu.with_memory_space_constraint(array, pltpu.HBM) for array in operands))


def join_kernel(own, other, held, sems):
    half = own.shape[2]
    copies = [
        pltpu.make_async_copy(
            source.at[part], held.at[part, :, pl.ds(h * half, half)], sems.at[h, part]
        )
        for h, source in enumerate((own, other))
        for part in range(3)
    ]
    for copy in copies:
        copy.start()
    for copy in copies:
        copy.wait()


def joined(own, other):
    parts, width, half = own.shape
    return pl.pallas_call(
        join_kernel,
        out_shape=pltpu.VMEM((parts, width, 2 * half), own.dtype),
        in_specs=[pl.BlockSpec(memory_space=pl.ANY)] * 2,
        out_specs=pl.BlockSpec(memory_space=pltpu.VMEM),
        scratch_shapes=[pltpu.SemaphoreType.DMA((2, parts))],
        compiler_params=pltpu.CompilerParams(vmem_limit_bytes=VMEM),
        cost_estimate=pl.CostEstimate(
            flops=0, bytes_accessed=8 * parts * width * half, transcendentals=0
        ),
    )(pltpu.with_memory_space_constraint(own, pltpu.HBM), other)


def expert_kernel(count, expert_count, *refs):
    packs, held, outs = (refs[:count], refs[count], refs[count + 1 : 2 * count + 1])
    both, cotan, acc = refs[2 * count + 1 :]
    tok_dev = packs[0].shape[0]
    _, width, hidden = held.shape
    rows = count * tok_dev

    def stacked(start, size):
        return jnp.concatenate([p[:, start : start + size].astype(jnp.float32) for p in packs], 0)

    both[:rows, :] = stacked(0, width).astype(jnp.bfloat16)
    both[rows:, :] = stacked(width, width).astype(jnp.bfloat16)
    cotan[...] = stacked(2 * width, width).astype(jnp.bfloat16)
    tail = stacked(3 * width, packs[0].shape[1] - 3 * width)
    mine = lax.axis_index("expert") // 2
    lane = lax.broadcasted_iota(jnp.int32, tail.shape, 1)
    after = 2 * expert_count

    def picked(lanes):
        return jnp.sum(jnp.where(lanes, tail, 0.0), axis=1, keepdims=True)

    gate_row = picked((lane == mine) | (lane == mine + expert_count))
    scale_row = picked((lane >= after) & (lane < after + 3))
    slope_row = picked((lane >= after + 3) & (lane < after + 6))

    def weights(part, start, size):
        return held[part, :, start : start + size]

    block = 256 if hidden % 256 == 0 else 128
    contract = (((1,), (1,)), ((), ()))
    for start in range(0, hidden, block):
        pre_gate = jnp.dot(
            both[...], weights(0, start, block), preferred_element_type=jnp.float32
        )
        pre_up = jnp.dot(both[...], weights(1, start, block), preferred_element_type=jnp.float32)
        back = jnp.dot(cotan[...], weights(2, start, block), preferred_element_type=jnp.float32)
        gate, gate_t = (pre_gate[:rows], pre_gate[rows:])
        up, up_t = (pre_up[:rows], pre_up[rows:])
        sig = jax.nn.sigmoid(gate)
        act = gate * sig
        slope = sig * (1.0 + gate * (1.0 - sig))
        bend = sig * (1.0 - sig) * (2.0 + gate * (1.0 - 2.0 * sig))
        d_gate = (back * slope * up).astype(jnp.bfloat16)
        d_up = (back * act).astype(jnp.bfloat16)
        t_gate = (back * (bend * gate_t * up + slope * up_t)).astype(jnp.bfloat16)
        t_up = (back * slope * gate_t).astype(jnp.bfloat16)
        total = lax.dot_general(
            jnp.concatenate([d_gate, t_gate], 0),
            weights(0, start, block),
            contract,
            preferred_element_type=jnp.float32,
        )
        total = total + lax.dot_general(
            jnp.concatenate([d_up, t_up], 0),
            weights(1, start, block),
            contract,
            preferred_element_type=jnp.float32,
        )
        acc[...] = total if start == 0 else acc[...] + total
    for n in range(count):
        part = slice(n * tok_dev, (n + 1) * tok_dev)
        later = slice(rows + n * tok_dev, rows + (n + 1) * tok_dev)
        grad, tan = (acc[part] * gate_row[part], acc[later] * gate_row[part])
        scale, slope_r = (scale_row[part], slope_row[part])
        normed = packs[n][:, :width].astype(jnp.float32)
        normed_t = packs[n][:, width : 2 * width].astype(jnp.float32)
        outs[n][:, :width] = (scale * tan + slope_r * grad).astype(outs[n].dtype)
        first = jnp.mean(normed * grad, axis=1, keepdims=True)
        second = jnp.mean(normed * tan + normed_t * grad, axis=1, keepdims=True)
        second = (second - slope_r / scale * first) / scale
        lane = lax.broadcasted_iota(jnp.int32, (tok_dev, outs[n].shape[1] - width), 1)
        sums = jnp.where(lane == 0, first / scale, jnp.where(lane == 1, second, 0.0))
        outs[n][:, width:] = sums.astype(outs[n].dtype)


def experts(packs, kinds, held, expert_count):
    count = len(packs)
    tok_dev = packs[0].shape[0]
    _, width, hidden = held.shape
    rows = count * tok_dev
    whole = pl.BlockSpec(memory_space=pltpu.VMEM)
    return pl.pallas_call(
        functools.partial(expert_kernel, count, expert_count),
        out_shape=[jax.ShapeDtypeStruct((tok_dev, width + 128), kind) for kind in kinds],
        in_specs=[whole] * (count + 1),
        out_specs=[whole] * count,
        scratch_shapes=[
            pltpu.VMEM((2 * rows, width), jnp.bfloat16),
            pltpu.VMEM((rows, width), jnp.bfloat16),
            pltpu.VMEM((2 * rows, width), jnp.float32),
        ],
        compiler_params=pltpu.CompilerParams(vmem_limit_bytes=VMEM),
        cost_estimate=pl.CostEstimate(
            flops=2 * 9 * rows * width * hidden,
            bytes_accessed=6 * width * hidden,
            transcendentals=rows * hidden,
        ),
    )(*packs, pltpu.with_memory_space_constraint(held, pltpu.VMEM))


def finish_kernel(tokens, gain, signs, *refs):
    arrived, hvp, quad = (refs[:-2], refs[-2], refs[-1])
    width = tokens.shape[1]
    xf = tokens[...].astype(jnp.float32)
    probe = (2 * signs[...] - 1).astype(jnp.float32)
    scale, along = rms_terms(xf, probe)
    slope_r = -(scale**3) * along
    rows = sum(part[...].astype(jnp.float32) for part in arrived)
    first = rows[:, width : width + 1]
    second = rows[:, width + 1 : width + 2]
    whole = (
        gain[...] * rows[:, :width]
        - 3.0 * scale**2 * slope_r * first * xf
        - scale**3 * first * probe
        - scale**3 * second * xf
    )
    hvp[...] = whole
    column = jnp.mean(probe * whole, axis=1, keepdims=True)
    tok_dev = column.shape[0]
    quad[...] = jnp.sum(identity(tok_dev) * column, axis=0, keepdims=True)


def moved(rows, turns, flip_x=False, flip_core=False):
    count = lax.axis_size("expert")
    pairs = [
        (i, (i + 4 * turns) % count ^ (2 * flip_x) ^ (1 * flip_core)) for i in range(count)
    ]
    return lax.ppermute(rows, "expert", pairs)


def dense_local(tokens, norm_gain, probe_signs, cotangent, routes, gates, weights):
    tok_dev, width = tokens.shape
    n_exp = lax.axis_size("expert")
    expert_count = n_exp // 2
    pack = packed(tokens, norm_gain, probe_signs, cotangent, routes, gates, expert_count)
    held = joined(weights, moved(weights, 0, flip_core=True))
    same, across = {0: pack}, {}
    same[1] = moved(pack, 1)
    across[0] = moved(pack, 0, flip_x=True)
    same[1] = lax.optimization_barrier((same[1], across[0], held))[0]
    same[2] = moved(same[1], 1)
    across[1] = moved(same[1], 0, flip_x=True)
    across[2] = moved(same[2], 0, flip_x=True)
    same[3] = moved(lax.optimization_barrier((pack, same[2]))[0], -1)
    wide, sent = (jnp.float32, jnp.bfloat16)
    here, there = {}, {}
    here[0], here[1], here[2], there[0], there[1] = experts(
        [same[0], same[1], same[2], across[0], across[1]],
        [wide, wide, sent, sent, sent],
        held,
        expert_count,
    )
    near, far, _ = lax.optimization_barrier((same[3], across[2], here[1]))
    across[3] = moved(near, 0, flip_x=True)
    here[3], there[2] = experts([near, far], [sent, sent], held, expert_count)
    last = lax.optimization_barrier((across[3], there[2]))[0]
    (there[3],) = experts([last], [sent], held, expert_count)

    def flipped(rows):
        return moved(rows, 0, flip_x=True)

    def total(*parts):
        return sum(part.astype(jnp.float32) for part in parts).astype(jnp.bfloat16)

    beside, forward = (flipped(there[1]), moved(here[2], -1))
    kept = lax.optimization_barrier((here[1], there[3]))[0]
    arrived = [
        here[0],
        flipped(there[0]),
        moved(here[3], 1),
        moved(there[2], 2, flip_x=True),
        moved(there[3], 1, flip_x=True),
        moved(total(kept, beside, forward), -1),
    ]
    hvp, quad = pl.pallas_call(
        finish_kernel,
        out_shape=[
            jax.ShapeDtypeStruct((tok_dev, width), jnp.float32),
            jax.ShapeDtypeStruct((1, tok_dev), jnp.float32),
        ],
        compiler_params=pltpu.CompilerParams(vmem_limit_bytes=VMEM),
        cost_estimate=pl.CostEstimate(
            flops=40 * tok_dev * width, bytes_accessed=26 * tok_dev * width, transcendentals=0
        ),
    )(tokens, norm_gain.reshape(1, width), probe_signs, *arrived)
    return (hvp, quad.reshape(tok_dev))


def routed_rows(normed, normed_t, cotangent, routes, gates, weights):
    tok_dev, width = normed.shape
    groups_here = routes.shape[0]
    half = routes.shape[2]
    n_exp = lax.axis_size("expert")
    expert_count = n_exp // 2
    cap = capacity(tok_dev, half, expert_count)
    buffer_rows = expert_count * cap
    stack_z, stack_t, stack_c, stack_w = ([], [], [], [])
    for group in range(groups_here):
        target = slot_targets(routes[group], expert_count, cap)
        place = (jnp.arange(buffer_rows, dtype=jnp.int32)[:, None] == target[None, :]).reshape(
            buffer_rows, tok_dev, half
        )
        place_tok = jnp.sum(place.astype(jnp.float32), axis=2).astype(jnp.bfloat16)
        stack_w.append(jnp.sum(place.astype(jnp.float32) * gates[group][None, :, :], axis=2))
        stack_z.append(
            jnp.dot(place_tok, normed, preferred_element_type=jnp.float32).astype(jnp.bfloat16)
        )
        stack_t.append(
            jnp.dot(place_tok, normed_t, preferred_element_type=jnp.float32).astype(jnp.bfloat16)
        )
        stack_c.append(
            jnp.dot(place_tok, cotangent, preferred_element_type=jnp.float32).astype(jnp.bfloat16)
        )
    rows_z = jnp.stack(stack_z, 0)
    rows_t = jnp.stack(stack_t, 0)
    rows_c = jnp.stack(stack_c, 0)
    weighted = jnp.stack(stack_w, 0)

    def arrange(rows):
        shaped = rows.reshape(groups_here, expert_count, 1, cap, width)
        shaped = jnp.broadcast_to(shaped, (groups_here, expert_count, 2, cap, width))
        return jnp.transpose(shaped, (1, 2, 0, 3, 4)).reshape(n_exp, groups_here * cap, width)

    send_z, send_t, send_c = (arrange(rows_z), arrange(rows_t), arrange(rows_c))
    got_z = lax.all_to_all(send_z, "expert", split_axis=0, concat_axis=0, tiled=True)
    got_t = lax.all_to_all(send_t, "expert", split_axis=0, concat_axis=0, tiled=True)
    got_c = lax.all_to_all(send_c, "expert", split_axis=0, concat_axis=0, tiled=True)
    sources, items, cols = got_z.shape
    g_rows, t_rows = expert_terms(
        weights, got_z.reshape(-1, cols), got_t.reshape(-1, cols), got_c.reshape(-1, cols)
    )
    g_rows = g_rows.reshape(sources, items, cols)
    t_rows = t_rows.reshape(sources, items, cols)
    back_g = lax.all_to_all(g_rows, "expert", split_axis=0, concat_axis=0, tiled=True)
    back_t = lax.all_to_all(t_rows, "expert", split_axis=0, concat_axis=0, tiled=True)

    def restore(rows):
        shaped = jnp.sum(rows.reshape(expert_count, 2, groups_here, cap, width), axis=1)
        return jnp.transpose(shaped, (1, 0, 2, 3)).reshape(groups_here, buffer_rows, width)

    back_g = restore(back_g)
    back_t = restore(back_t)
    contract = (((0, 1), (0, 1)), ((), ()))
    grad_z = lax.dot_general(weighted, back_g, contract, precision=lax.Precision.HIGHEST)
    tan_z = lax.dot_general(weighted, back_t, contract, precision=lax.Precision.HIGHEST)
    return (grad_z, tan_z)


def local(tokens, norm_gain, probe_signs, cotangent, routes, gates, expert_weights):
    cap = capacity(tokens.shape[0], routes.shape[2], lax.axis_size("expert") // 2)
    layout = (lax.axis_size("expert"), lax.axis_size("node"))
    if layout == (16, 1) and routes.shape[0] * cap >= tokens.shape[0]:
        return dense_local(
            tokens, norm_gain, probe_signs, cotangent, routes, gates, expert_weights
        )
    xf = tokens.astype(jnp.float32)
    probe = (2 * probe_signs - 1).astype(jnp.float32)
    tok_dev, width = xf.shape
    scale = lax.rsqrt(jnp.mean(xf * xf, axis=1, keepdims=True) + EPS)
    along = jnp.mean(xf * probe, axis=1, keepdims=True)
    normed = (xf * scale * norm_gain).astype(jnp.bfloat16)
    normed_t = (norm_gain * (scale * probe - scale**3 * xf * along)).astype(jnp.bfloat16)
    own_half = lax.all_gather(expert_weights, "node", axis=2, tiled=True)
    grad_z, tan_z = routed_rows(normed, normed_t, cotangent, routes, gates, own_half)
    share = width // lax.axis_size("node")
    start = lax.axis_index("node") * share
    slope_r = -(scale**3) * along
    grad_z, tan_z = lax.psum((grad_z, tan_z), "node")
    lifted = norm_gain * grad_z
    lifted_t = norm_gain * tan_z
    first = jnp.mean(xf * lifted, axis=1, keepdims=True)
    second = jnp.mean(xf * lifted_t, axis=1, keepdims=True)
    third = jnp.mean(probe * lifted, axis=1, keepdims=True)
    whole_hvp = (
        scale * lifted_t
        + slope_r * lifted
        - 3.0 * scale**2 * slope_r * first * xf
        - scale**3 * first * probe
        - scale**3 * (second + third) * xf
    )
    quad = jnp.mean(probe * whole_hvp, axis=1)
    hvp = lax.dynamic_slice_in_dim(whole_hvp, start, share, 1)
    return (hvp, quad)


def solution(mesh):
    placed = (
        P(("groups", "expert"), None),
        P(),
        P(("groups", "expert"), None),
        P(("groups", "expert"), None),
        P("node", ("groups", "expert"), None),
        P("node", ("groups", "expert"), None),
        P(None, None, ("expert", "node")),
    )
    return jax.shard_map(
        local,
        mesh=mesh,
        in_specs=placed,
        out_specs=(P(("groups", "expert"), "node"), P(("groups", "expert"))),
        check_vma=False,
    )
```

```python
import functools

import jax
import jax.numpy as jnp
from jax import lax
from jax.experimental import pallas as pl
from jax.experimental.pallas import tpu as pltpu
from jax.sharding import PartitionSpec as P

EPS = 1e-06
VMEM = 24 * 1024 * 1024


def expert_terms(weights, rows, rows_t, cotan):
    count = rows.shape[0]
    both = jnp.concatenate([rows, rows_t], 0)
    pre_gate = jnp.dot(both, weights[0], preferred_element_type=jnp.float32)
    pre_up = jnp.dot(both, weights[1], preferred_element_type=jnp.float32)
    gate, gate_t = (pre_gate[:count], pre_gate[count:])
    up, up_t = (pre_up[:count], pre_up[count:])
    back = jnp.dot(cotan, weights[2], preferred_element_type=jnp.float32)
    sig = jax.nn.sigmoid(gate)
    act = gate * sig
    slope = sig * (1.0 + gate * (1.0 - sig))
    bend = sig * (1.0 - sig) * (2.0 + gate * (1.0 - 2.0 * sig))
    d_gate = (back * slope * up).astype(jnp.bfloat16)
    d_up = (back * act).astype(jnp.bfloat16)
    t_gate = (back * (bend * gate_t * up + slope * up_t)).astype(jnp.bfloat16)
    t_up = (back * slope * gate_t).astype(jnp.bfloat16)
    contract = (((1,), (1,)), ((), ()))
    lhs_gate = jnp.concatenate([d_gate, t_gate], 0)
    lhs_up = jnp.concatenate([d_up, t_up], 0)
    total = lax.dot_general(lhs_gate, weights[0], contract, preferred_element_type=jnp.float32)
    total = total + lax.dot_general(
        lhs_up, weights[1], contract, preferred_element_type=jnp.float32
    )
    return (total[:count], total[count:])


def slot_targets(route_ids, expert_count, capacity):
    flat = route_ids.reshape(-1)
    count = flat.shape[0]
    onehot = (flat[:, None] == jnp.arange(expert_count, dtype=jnp.int32)[None, :]).astype(
        jnp.float32
    )
    lower = (jnp.arange(count)[:, None] > jnp.arange(count)[None, :]).astype(jnp.float32)
    before = jnp.dot(lower, onehot, precision=lax.Precision.HIGHEST)
    rank = jnp.sum(before * onehot, axis=1).astype(jnp.int32)
    return flat * capacity + rank


def capacity(tok_dev, half, expert_count):
    return min(2 * ((2 * tok_dev * half + 3 * expert_count - 1) // (3 * expert_count)), tok_dev)


def rms_terms(xf, probe):
    scale = lax.rsqrt(jnp.mean(xf * xf, axis=1, keepdims=True) + EPS)
    along = jnp.mean(xf * probe, axis=1, keepdims=True)
    return scale, along


def pack_kernel(expert_count, *refs):
    sources, pack, held, sems = (refs[:6], refs[6], refs[7:13], refs[13])
    copies = [
        pltpu.make_async_copy(source, target, sems.at[n])
        for n, (source, target) in enumerate(zip(sources, held))
    ]
    for copy in copies:
        copy.start()
    for copy in copies:
        copy.wait()
    tokens, gain, signs, cotangent, routes, gates = held
    width = tokens.shape[1]
    xf = tokens[...].astype(jnp.float32)
    probe = (2 * signs[...] - 1).astype(jnp.float32)
    scale, along = rms_terms(xf, probe)
    pack[:, :width] = (xf * scale * gain[...]).astype(jnp.bfloat16)
    tangent = gain[...] * (scale * probe - scale**3 * xf * along)
    pack[:, width : 2 * width] = tangent.astype(jnp.bfloat16)
    pack[:, 2 * width : 3 * width] = cotangent[...]
    tok_dev, lanes = (tokens.shape[0], pack.shape[1] - 3 * width)
    lane = lax.broadcasted_iota(jnp.int32, (lanes, tok_dev), 0)
    expert = lax.rem(lane, expert_count)
    gate = jnp.zeros(lane.shape, jnp.float32)
    for group in range(routes.shape[0]):
        for slot in range(routes.shape[1]):
            named = routes[group, slot : slot + 1, :] == expert
            gate = gate + jnp.where(named, gates[group, slot : slot + 1, :], 0.0)
    high = gate.astype(jnp.bfloat16).astype(jnp.float32)
    tail = jnp.where(lane < expert_count, high, gate - high)
    tail = jnp.where(lane < 2 * expert_count, tail, 0.0).astype(jnp.bfloat16)
    turned = lax.dot_general(
        identity(tok_dev).astype(jnp.bfloat16),
        tail,
        (((1,), (1,)), ((), ())),
        preferred_element_type=jnp.float32,
    )
    lane = lax.broadcasted_iota(jnp.int32, (tok_dev, lanes), 1)
    place = 2 * expert_count
    for number in (scale, -(scale**3) * along):
        for _ in range(3):
            addend = number.astype(jnp.bfloat16).astype(jnp.float32)
            turned = jnp.where(lane == place, addend, turned)
            number = number - addend
            place += 1
    pack[:, 3 * width :] = turned.astype(jnp.bfloat16)


def identity(size):
    rows = lax.broadcasted_iota(jnp.int32, (size, size), 0)
    return (rows == lax.broadcasted_iota(jnp.int32, (size, size), 1)).astype(jnp.float32)


def packed(tokens, norm_gain, probe_signs, cotangent, routes, gates, expert_count):
    tok_dev, width = tokens.shape
    tail = -(-(2 * expert_count + 6) // 128) * 128
    token_minor = (0, 2, 1)
    operands = (
        tokens,
        norm_gain.reshape(1, width),
        probe_signs,
        cotangent,
        jnp.transpose(routes, token_minor),
        jnp.transpose(gates, token_minor),
    )
    return pl.pallas_call(
        functools.partial(pack_kernel, expert_count),
        out_shape=jax.ShapeDtypeStruct((tok_dev, 3 * width + tail), jnp.bfloat16),
        in_specs=[pl.BlockSpec(memory_space=pl.ANY)] * 6,
        out_specs=pl.BlockSpec(memory_space=pltpu.VMEM),
        scratch_shapes=[pltpu.VMEM(array.shape, array.dtype) for array in operands]
        + [pltpu.SemaphoreType.DMA((6,))],
        compiler_params=pltpu.CompilerParams(vmem_limit_bytes=VMEM),
        cost_estimate=pl.CostEstimate(
            flops=20 * tok_dev * width, bytes_accessed=14 * tok_dev * width, transcendentals=0
        ),
    )(*(pltpu.with_memory_space_constraint(array, pltpu.HBM) for array in operands))


def join_kernel(own, other, held, sems):
    half = own.shape[2]
    copies = [
        pltpu.make_async_copy(
            source.at[part], held.at[part, :, pl.ds(h * half, half)], sems.at[h, part]
        )
        for h, source in enumerate((own, other))
        for part in range(3)
    ]
    for copy in copies:
        copy.start()
    for copy in copies:
        copy.wait()


def joined(own, other):
    parts, width, half = own.shape
    return pl.pallas_call(
        join_kernel,
        out_shape=pltpu.VMEM((parts, width, 2 * half), own.dtype),
        in_specs=[pl.BlockSpec(memory_space=pl.ANY)] * 2,
        out_specs=pl.BlockSpec(memory_space=pltpu.VMEM),
        scratch_shapes=[pltpu.SemaphoreType.DMA((2, parts))],
        compiler_params=pltpu.CompilerParams(vmem_limit_bytes=VMEM),
        cost_estimate=pl.CostEstimate(
            flops=0, bytes_accessed=8 * parts * width * half, transcendentals=0
        ),
    )(pltpu.with_memory_space_constraint(own, pltpu.HBM), other)


def expert_kernel(count, expert_count, *refs):
    packs, held, outs = (refs[:count], refs[count], refs[count + 1 : -3])
    both, cotan, acc = refs[-3:]
    tok_dev = packs[0].shape[0]
    _, width, hidden = held.shape
    rows = count * tok_dev

    def stacked(start, size):
        return jnp.concatenate([p[:, start : start + size].astype(jnp.float32) for p in packs], 0)

    both[:rows, :] = stacked(0, width).astype(jnp.bfloat16)
    both[rows:, :] = stacked(width, width).astype(jnp.bfloat16)
    cotan[...] = stacked(2 * width, width).astype(jnp.bfloat16)
    tail = stacked(3 * width, packs[0].shape[1] - 3 * width)
    mine = lax.axis_index("expert") // 2
    lane = lax.broadcasted_iota(jnp.int32, tail.shape, 1)
    after = 2 * expert_count

    def picked(lanes):
        return jnp.sum(jnp.where(lanes, tail, 0.0), axis=1, keepdims=True)

    gate_row = picked((lane == mine) | (lane == mine + expert_count))
    scale_row = picked((lane >= after) & (lane < after + 3))
    slope_row = picked((lane >= after + 3) & (lane < after + 6))

    def weights(part, start, size):
        return held[part, :, start : start + size]

    block = 256 if hidden % 256 == 0 else 128
    contract = (((1,), (1,)), ((), ()))
    for start in range(0, hidden, block):
        pre_gate = jnp.dot(
            both[...], weights(0, start, block), preferred_element_type=jnp.float32
        )
        pre_up = jnp.dot(both[...], weights(1, start, block), preferred_element_type=jnp.float32)
        back = jnp.dot(cotan[...], weights(2, start, block), preferred_element_type=jnp.float32)
        gate, gate_t = (pre_gate[:rows], pre_gate[rows:])
        up, up_t = (pre_up[:rows], pre_up[rows:])
        sig = jax.nn.sigmoid(gate)
        act = gate * sig
        slope = sig * (1.0 + gate * (1.0 - sig))
        bend = sig * (1.0 - sig) * (2.0 + gate * (1.0 - 2.0 * sig))
        d_gate = (back * slope * up).astype(jnp.bfloat16)
        d_up = (back * act).astype(jnp.bfloat16)
        t_gate = (back * (bend * gate_t * up + slope * up_t)).astype(jnp.bfloat16)
        t_up = (back * slope * gate_t).astype(jnp.bfloat16)
        total = lax.dot_general(
            jnp.concatenate([d_gate, t_gate], 0),
            weights(0, start, block),
            contract,
            preferred_element_type=jnp.float32,
        )
        total = total + lax.dot_general(
            jnp.concatenate([d_up, t_up], 0),
            weights(1, start, block),
            contract,
            preferred_element_type=jnp.float32,
        )
        acc[...] = total if start == 0 else acc[...] + total
    homes = [out.at[:, pl.ds(at, width + 128)] for out in outs for at in range(0, out.shape[1], width + 128)]
    for n, home in enumerate(homes):
        part = slice(n * tok_dev, (n + 1) * tok_dev)
        later = slice(rows + n * tok_dev, rows + (n + 1) * tok_dev)
        grad, tan = (acc[part] * gate_row[part], acc[later] * gate_row[part])
        scale, slope_r = (scale_row[part], slope_row[part])
        normed = packs[n][:, :width].astype(jnp.float32)
        normed_t = packs[n][:, width : 2 * width].astype(jnp.float32)
        home[:, :width] = (scale * tan + slope_r * grad).astype(home.dtype)
        first = jnp.mean(normed * grad, axis=1, keepdims=True)
        second = jnp.mean(normed * tan + normed_t * grad, axis=1, keepdims=True)
        second = (second - slope_r / scale * first) / scale
        lane = lax.broadcasted_iota(jnp.int32, (tok_dev, 128), 1)
        sums = jnp.where(lane == 0, first / scale, jnp.where(lane == 1, second, 0.0))
        home[:, width:] = sums.astype(home.dtype)


def experts(packs, kinds, held, expert_count):
    count = len(packs)
    tok_dev = packs[0].shape[0]
    _, width, hidden = held.shape
    rows = count * tok_dev
    whole = pl.BlockSpec(memory_space=pltpu.VMEM)
    return pl.pallas_call(
        functools.partial(expert_kernel, count, expert_count),
        out_shape=[jax.ShapeDtypeStruct((tok_dev, n * (width + 128)), kind) for kind, n in kinds],
        in_specs=[whole] * (count + 1),
        out_specs=[whole] * len(kinds),
        scratch_shapes=[
            pltpu.VMEM((2 * rows, width), jnp.bfloat16),
            pltpu.VMEM((rows, width), jnp.bfloat16),
            pltpu.VMEM((2 * rows, width), jnp.float32),
        ],
        compiler_params=pltpu.CompilerParams(vmem_limit_bytes=VMEM),
        cost_estimate=pl.CostEstimate(
            flops=2 * 9 * rows * width * hidden,
            bytes_accessed=6 * width * hidden,
            transcendentals=rows * hidden,
        ),
    )(*packs, pltpu.with_memory_space_constraint(held, pltpu.VMEM))


def finish_kernel(tokens, gain, signs, *refs):
    arrived, hvp, quad = (refs[:-2], refs[-2], refs[-1])
    width = tokens.shape[1]
    xf = tokens[...].astype(jnp.float32)
    probe = (2 * signs[...] - 1).astype(jnp.float32)
    scale, along = rms_terms(xf, probe)
    slope_r = -(scale**3) * along
    lanes = arrived[0].shape[1]
    rows = sum(part[:, :lanes].astype(jnp.float32) for part in arrived)
    first = rows[:, width : width + 1]
    second = rows[:, width + 1 : width + 2]
    whole = (
        gain[...] * rows[:, :width]
        - 3.0 * scale**2 * slope_r * first * xf
        - scale**3 * first * probe
        - scale**3 * second * xf
    )
    hvp[...] = whole
    column = jnp.mean(probe * whole, axis=1, keepdims=True)
    tok_dev = column.shape[0]
    quad[...] = jnp.sum(identity(tok_dev) * column, axis=0, keepdims=True)


def moved(rows, turns, flip_x=False, flip_core=False):
    count = lax.axis_size("expert")
    pairs = [
        (i, (i + 4 * turns) % count ^ (2 * flip_x) ^ (1 * flip_core)) for i in range(count)
    ]
    return lax.ppermute(rows, "expert", pairs)


def dense_local(tokens, norm_gain, probe_signs, cotangent, routes, gates, weights):
    tok_dev, width = tokens.shape
    n_exp = lax.axis_size("expert")
    expert_count = n_exp // 2
    pack = packed(tokens, norm_gain, probe_signs, cotangent, routes, gates, expert_count)
    held = joined(weights, moved(weights, 0, flip_core=True))
    same, across = {0: pack}, {}
    same[1] = moved(pack, 1)
    across[0] = moved(pack, 0, flip_x=True)
    same[1] = lax.optimization_barrier((same[1], across[0], held))[0]
    same[3] = moved(lax.optimization_barrier((pack, same[1]))[0], -1)
    same[2] = moved(same[1], 1)
    across[1] = moved(same[1], 0, flip_x=True)
    across[3] = moved(same[3], 0, flip_x=True)
    across[2] = moved(same[2], 0, flip_x=True)
    wide, sent, pair = ((jnp.float32, 1), (jnp.bfloat16, 1), (jnp.bfloat16, 2))
    here = {}
    here[0], here[1], here[2], here[3], there = experts(
        [same[0], same[1], same[2], same[3], across[0], across[1]],
        [wide, wide, sent, sent, pair],
        held,
        expert_count,
    )
    late = lax.optimization_barrier((across[2], across[3], here[1]))[:2]
    far, last = experts(late, [sent, sent], held, expert_count)

    def total(*parts):
        return sum(part.astype(jnp.float32) for part in parts).astype(jnp.bfloat16)

    beside, forward = (moved(there, 0, flip_x=True), moved(here[2], -1))
    kept = lax.optimization_barrier((here[1], far))[0]
    arrived = [
        here[0],
        beside,
        moved(here[3], 1),
        moved(far, 2, flip_x=True),
        moved(last, 1, flip_x=True),
        moved(total(kept, beside[:, kept.shape[1] :], forward), -1),
    ]
    hvp, quad = pl.pallas_call(
        finish_kernel,
        out_shape=[
            jax.ShapeDtypeStruct((tok_dev, width), jnp.float32),
            jax.ShapeDtypeStruct((1, tok_dev), jnp.float32),
        ],
        compiler_params=pltpu.CompilerParams(vmem_limit_bytes=VMEM),
        cost_estimate=pl.CostEstimate(
            flops=40 * tok_dev * width, bytes_accessed=26 * tok_dev * width, transcendentals=0
        ),
    )(tokens, norm_gain.reshape(1, width), probe_signs, *arrived)
    return (hvp, quad.reshape(tok_dev))


def routed_rows(normed, normed_t, cotangent, routes, gates, weights):
    tok_dev, width = normed.shape
    groups_here = routes.shape[0]
    half = routes.shape[2]
    n_exp = lax.axis_size("expert")
    expert_count = n_exp // 2
    cap = capacity(tok_dev, half, expert_count)
    buffer_rows = expert_count * cap
    stack_z, stack_t, stack_c, stack_w = ([], [], [], [])
    for group in range(groups_here):
        target = slot_targets(routes[group], expert_count, cap)
        place = (jnp.arange(buffer_rows, dtype=jnp.int32)[:, None] == target[None, :]).reshape(
            buffer_rows, tok_dev, half
        )
        place_tok = jnp.sum(place.astype(jnp.float32), axis=2).astype(jnp.bfloat16)
        stack_w.append(jnp.sum(place.astype(jnp.float32) * gates[group][None, :, :], axis=2))
        stack_z.append(
            jnp.dot(place_tok, normed, preferred_element_type=jnp.float32).astype(jnp.bfloat16)
        )
        stack_t.append(
            jnp.dot(place_tok, normed_t, preferred_element_type=jnp.float32).astype(jnp.bfloat16)
        )
        stack_c.append(
            jnp.dot(place_tok, cotangent, preferred_element_type=jnp.float32).astype(jnp.bfloat16)
        )
    rows_z = jnp.stack(stack_z, 0)
    rows_t = jnp.stack(stack_t, 0)
    rows_c = jnp.stack(stack_c, 0)
    weighted = jnp.stack(stack_w, 0)

    def arrange(rows):
        shaped = rows.reshape(groups_here, expert_count, 1, cap, width)
        shaped = jnp.broadcast_to(shaped, (groups_here, expert_count, 2, cap, width))
        return jnp.transpose(shaped, (1, 2, 0, 3, 4)).reshape(n_exp, groups_here * cap, width)

    send_z, send_t, send_c = (arrange(rows_z), arrange(rows_t), arrange(rows_c))
    got_z = lax.all_to_all(send_z, "expert", split_axis=0, concat_axis=0, tiled=True)
    got_t = lax.all_to_all(send_t, "expert", split_axis=0, concat_axis=0, tiled=True)
    got_c = lax.all_to_all(send_c, "expert", split_axis=0, concat_axis=0, tiled=True)
    sources, items, cols = got_z.shape
    g_rows, t_rows = expert_terms(
        weights, got_z.reshape(-1, cols), got_t.reshape(-1, cols), got_c.reshape(-1, cols)
    )
    g_rows = g_rows.reshape(sources, items, cols)
    t_rows = t_rows.reshape(sources, items, cols)
    back_g = lax.all_to_all(g_rows, "expert", split_axis=0, concat_axis=0, tiled=True)
    back_t = lax.all_to_all(t_rows, "expert", split_axis=0, concat_axis=0, tiled=True)

    def restore(rows):
        shaped = jnp.sum(rows.reshape(expert_count, 2, groups_here, cap, width), axis=1)
        return jnp.transpose(shaped, (1, 0, 2, 3)).reshape(groups_here, buffer_rows, width)

    back_g = restore(back_g)
    back_t = restore(back_t)
    contract = (((0, 1), (0, 1)), ((), ()))
    grad_z = lax.dot_general(weighted, back_g, contract, precision=lax.Precision.HIGHEST)
    tan_z = lax.dot_general(weighted, back_t, contract, precision=lax.Precision.HIGHEST)
    return (grad_z, tan_z)


def local(tokens, norm_gain, probe_signs, cotangent, routes, gates, expert_weights):
    cap = capacity(tokens.shape[0], routes.shape[2], lax.axis_size("expert") // 2)
    layout = (lax.axis_size("expert"), lax.axis_size("node"))
    if layout == (16, 1) and routes.shape[0] * cap >= tokens.shape[0]:
        return dense_local(
            tokens, norm_gain, probe_signs, cotangent, routes, gates, expert_weights
        )
    xf = tokens.astype(jnp.float32)
    probe = (2 * probe_signs - 1).astype(jnp.float32)
    tok_dev, width = xf.shape
    scale = lax.rsqrt(jnp.mean(xf * xf, axis=1, keepdims=True) + EPS)
    along = jnp.mean(xf * probe, axis=1, keepdims=True)
    normed = (xf * scale * norm_gain).astype(jnp.bfloat16)
    normed_t = (norm_gain * (scale * probe - scale**3 * xf * along)).astype(jnp.bfloat16)
    own_half = lax.all_gather(expert_weights, "node", axis=2, tiled=True)
    grad_z, tan_z = routed_rows(normed, normed_t, cotangent, routes, gates, own_half)
    share = width // lax.axis_size("node")
    start = lax.axis_index("node") * share
    slope_r = -(scale**3) * along
    grad_z, tan_z = lax.psum((grad_z, tan_z), "node")
    lifted = norm_gain * grad_z
    lifted_t = norm_gain * tan_z
    first = jnp.mean(xf * lifted, axis=1, keepdims=True)
    second = jnp.mean(xf * lifted_t, axis=1, keepdims=True)
    third = jnp.mean(probe * lifted, axis=1, keepdims=True)
    whole_hvp = (
        scale * lifted_t
        + slope_r * lifted
        - 3.0 * scale**2 * slope_r * first * xf
        - scale**3 * first * probe
        - scale**3 * (second + third) * xf
    )
    quad = jnp.mean(probe * whole_hvp, axis=1)
    hvp = lax.dynamic_slice_in_dim(whole_hvp, start, share, 1)
    return (hvp, quad)


def solution(mesh):
    placed = (
        P(("groups", "expert"), None),
        P(),
        P(("groups", "expert"), None),
        P(("groups", "expert"), None),
        P("node", ("groups", "expert"), None),
        P("node", ("groups", "expert"), None),
        P(None, None, ("expert", "node")),
    )
    return jax.shard_map(
        local,
        mesh=mesh,
        in_specs=placed,
        out_specs=(P(("groups", "expert"), "node"), P(("groups", "expert"))),
        check_vma=False,
    )
```

```python
import functools

import jax
import jax.numpy as jnp
from jax import lax
from jax.experimental import pallas as pl
from jax.experimental.pallas import tpu as pltpu
from jax.sharding import PartitionSpec as P

EPS = 1e-06
VMEM = 24 * 1024 * 1024


def expert_terms(weights, rows, rows_t, cotan):
    count = rows.shape[0]
    both = jnp.concatenate([rows, rows_t], 0)
    pre_gate = jnp.dot(both, weights[0], preferred_element_type=jnp.float32)
    pre_up = jnp.dot(both, weights[1], preferred_element_type=jnp.float32)
    gate, gate_t = (pre_gate[:count], pre_gate[count:])
    up, up_t = (pre_up[:count], pre_up[count:])
    back = jnp.dot(cotan, weights[2], preferred_element_type=jnp.float32)
    sig = jax.nn.sigmoid(gate)
    act = gate * sig
    slope = sig * (1.0 + gate * (1.0 - sig))
    bend = sig * (1.0 - sig) * (2.0 + gate * (1.0 - 2.0 * sig))
    d_gate = (back * slope * up).astype(jnp.bfloat16)
    d_up = (back * act).astype(jnp.bfloat16)
    t_gate = (back * (bend * gate_t * up + slope * up_t)).astype(jnp.bfloat16)
    t_up = (back * slope * gate_t).astype(jnp.bfloat16)
    contract = (((1,), (1,)), ((), ()))
    lhs_gate = jnp.concatenate([d_gate, t_gate], 0)
    lhs_up = jnp.concatenate([d_up, t_up], 0)
    total = lax.dot_general(lhs_gate, weights[0], contract, preferred_element_type=jnp.float32)
    total = total + lax.dot_general(
        lhs_up, weights[1], contract, preferred_element_type=jnp.float32
    )
    return (total[:count], total[count:])


def slot_targets(route_ids, expert_count, capacity):
    flat = route_ids.reshape(-1)
    count = flat.shape[0]
    onehot = (flat[:, None] == jnp.arange(expert_count, dtype=jnp.int32)[None, :]).astype(
        jnp.float32
    )
    lower = (jnp.arange(count)[:, None] > jnp.arange(count)[None, :]).astype(jnp.float32)
    before = jnp.dot(lower, onehot, precision=lax.Precision.HIGHEST)
    rank = jnp.sum(before * onehot, axis=1).astype(jnp.int32)
    return flat * capacity + rank


def capacity(tok_dev, half, expert_count):
    return min(2 * ((2 * tok_dev * half + 3 * expert_count - 1) // (3 * expert_count)), tok_dev)


def rms_terms(xf, probe):
    scale = lax.rsqrt(jnp.mean(xf * xf, axis=1, keepdims=True) + EPS)
    along = jnp.mean(xf * probe, axis=1, keepdims=True)
    return scale, along


def pack_kernel(expert_count, *refs):
    sources, pack, held, sems = (refs[:6], refs[6], refs[7:13], refs[13])
    copies = [
        pltpu.make_async_copy(source, target, sems.at[n])
        for n, (source, target) in enumerate(zip(sources, held))
    ]
    for copy in copies:
        copy.start()
    for copy in copies:
        copy.wait()
    tokens, gain, signs, cotangent, routes, gates = held
    width = tokens.shape[1]
    xf = tokens[...].astype(jnp.float32)
    probe = (2 * signs[...] - 1).astype(jnp.float32)
    scale, along = rms_terms(xf, probe)
    pack[:, :width] = (xf * scale * gain[...]).astype(jnp.bfloat16)
    tangent = gain[...] * (scale * probe - scale**3 * xf * along)
    pack[:, width : 2 * width] = tangent.astype(jnp.bfloat16)
    pack[:, 2 * width : 3 * width] = cotangent[...]
    tok_dev, lanes = (tokens.shape[0], pack.shape[1] - 3 * width)
    lane = lax.broadcasted_iota(jnp.int32, (lanes, tok_dev), 0)
    expert = lax.rem(lane, expert_count)
    gate = jnp.zeros(lane.shape, jnp.float32)
    for group in range(routes.shape[0]):
        for slot in range(routes.shape[1]):
            named = routes[group, slot : slot + 1, :] == expert
            gate = gate + jnp.where(named, gates[group, slot : slot + 1, :], 0.0)
    high = gate.astype(jnp.bfloat16).astype(jnp.float32)
    tail = jnp.where(lane < expert_count, high, gate - high)
    tail = jnp.where(lane < 2 * expert_count, tail, 0.0).astype(jnp.bfloat16)
    turned = lax.dot_general(
        identity(tok_dev).astype(jnp.bfloat16),
        tail,
        (((1,), (1,)), ((), ())),
        preferred_element_type=jnp.float32,
    )
    lane = lax.broadcasted_iota(jnp.int32, (tok_dev, lanes), 1)
    place = 2 * expert_count
    for number in (scale, -(scale**3) * along):
        for _ in range(3):
            addend = number.astype(jnp.bfloat16).astype(jnp.float32)
            turned = jnp.where(lane == place, addend, turned)
            number = number - addend
            place += 1
    pack[:, 3 * width :] = turned.astype(jnp.bfloat16)


def identity(size):
    rows = lax.broadcasted_iota(jnp.int32, (size, size), 0)
    return (rows == lax.broadcasted_iota(jnp.int32, (size, size), 1)).astype(jnp.float32)


def packed(tokens, norm_gain, probe_signs, cotangent, routes, gates, expert_count):
    tok_dev, width = tokens.shape
    tail = -(-(2 * expert_count + 6) // 128) * 128
    token_minor = (0, 2, 1)
    operands = (
        tokens,
        norm_gain.reshape(1, width),
        probe_signs,
        cotangent,
        jnp.transpose(routes, token_minor),
        jnp.transpose(gates, token_minor),
    )
    return pl.pallas_call(
        functools.partial(pack_kernel, expert_count),
        out_shape=jax.ShapeDtypeStruct((tok_dev, 3 * width + tail), jnp.bfloat16),
        in_specs=[pl.BlockSpec(memory_space=pl.ANY)] * 6,
        out_specs=pl.BlockSpec(memory_space=pltpu.VMEM),
        scratch_shapes=[pltpu.VMEM(array.shape, array.dtype) for array in operands]
        + [pltpu.SemaphoreType.DMA((6,))],
        compiler_params=pltpu.CompilerParams(vmem_limit_bytes=VMEM),
        cost_estimate=pl.CostEstimate(
            flops=20 * tok_dev * width, bytes_accessed=14 * tok_dev * width, transcendentals=0
        ),
    )(*(pltpu.with_memory_space_constraint(array, pltpu.HBM) for array in operands))


def join_kernel(own, other, held, sems):
    half = own.shape[2]
    copies = [
        pltpu.make_async_copy(
            source.at[part], held.at[part, :, pl.ds(h * half, half)], sems.at[h, part]
        )
        for h, source in enumerate((own, other))
        for part in range(3)
    ]
    for copy in copies:
        copy.start()
    for copy in copies:
        copy.wait()


def joined(own, other):
    parts, width, half = own.shape
    return pl.pallas_call(
        join_kernel,
        out_shape=pltpu.VMEM((parts, width, 2 * half), own.dtype),
        in_specs=[pl.BlockSpec(memory_space=pl.ANY)] * 2,
        out_specs=pl.BlockSpec(memory_space=pltpu.VMEM),
        scratch_shapes=[pltpu.SemaphoreType.DMA((2, parts))],
        compiler_params=pltpu.CompilerParams(vmem_limit_bytes=VMEM),
        cost_estimate=pl.CostEstimate(
            flops=0, bytes_accessed=8 * parts * width * half, transcendentals=0
        ),
    )(pltpu.with_memory_space_constraint(own, pltpu.HBM), other)


def expert_kernel(count, expert_count, *refs):
    packs, held, outs = (refs[:count], refs[count], refs[count + 1 : -3])
    both, cotan, acc = refs[-3:]
    tok_dev = packs[0].shape[0]
    _, width, hidden = held.shape
    rows = count * tok_dev

    def stacked(start, size):
        return jnp.concatenate([p[:, start : start + size].astype(jnp.float32) for p in packs], 0)

    both[:rows, :] = stacked(0, width).astype(jnp.bfloat16)
    both[rows:, :] = stacked(width, width).astype(jnp.bfloat16)
    cotan[...] = stacked(2 * width, width).astype(jnp.bfloat16)
    tail = stacked(3 * width, packs[0].shape[1] - 3 * width)
    mine = lax.axis_index("expert") // 2
    lane = lax.broadcasted_iota(jnp.int32, tail.shape, 1)
    after = 2 * expert_count

    def picked(lanes):
        return jnp.sum(jnp.where(lanes, tail, 0.0), axis=1, keepdims=True)

    gate_row = picked((lane == mine) | (lane == mine + expert_count))
    scale_row = picked((lane >= after) & (lane < after + 3))
    slope_row = picked((lane >= after + 3) & (lane < after + 6))

    def weights(part, start, size):
        return held[part, :, start : start + size]

    block = 256 if hidden % 256 == 0 else 128
    contract = (((1,), (1,)), ((), ()))
    for start in range(0, hidden, block):
        pre_gate = jnp.dot(
            both[...], weights(0, start, block), preferred_element_type=jnp.float32
        )
        pre_up = jnp.dot(both[...], weights(1, start, block), preferred_element_type=jnp.float32)
        back = jnp.dot(cotan[...], weights(2, start, block), preferred_element_type=jnp.float32)
        gate, gate_t = (pre_gate[:rows], pre_gate[rows:])
        up, up_t = (pre_up[:rows], pre_up[rows:])
        sig = jax.nn.sigmoid(gate)
        act = gate * sig
        slope = sig * (1.0 + gate * (1.0 - sig))
        bend = sig * (1.0 - sig) * (2.0 + gate * (1.0 - 2.0 * sig))
        d_gate = (back * slope * up).astype(jnp.bfloat16)
        d_up = (back * act).astype(jnp.bfloat16)
        t_gate = (back * (bend * gate_t * up + slope * up_t)).astype(jnp.bfloat16)
        t_up = (back * slope * gate_t).astype(jnp.bfloat16)
        total = lax.dot_general(
            jnp.concatenate([d_gate, t_gate], 0),
            weights(0, start, block),
            contract,
            preferred_element_type=jnp.float32,
        )
        total = total + lax.dot_general(
            jnp.concatenate([d_up, t_up], 0),
            weights(1, start, block),
            contract,
            preferred_element_type=jnp.float32,
        )
        acc[...] = total if start == 0 else acc[...] + total
    homes = [out.at[:, pl.ds(at, width + 128)] for out in outs for at in range(0, out.shape[1], width + 128)]
    for n, home in enumerate(homes):
        part = slice(n * tok_dev, (n + 1) * tok_dev)
        later = slice(rows + n * tok_dev, rows + (n + 1) * tok_dev)
        grad, tan = (acc[part] * gate_row[part], acc[later] * gate_row[part])
        scale, slope_r = (scale_row[part], slope_row[part])
        normed = packs[n][:, :width].astype(jnp.float32)
        normed_t = packs[n][:, width : 2 * width].astype(jnp.float32)
        home[:, :width] = (scale * tan + slope_r * grad).astype(home.dtype)
        first = jnp.mean(normed * grad, axis=1, keepdims=True)
        second = jnp.mean(normed * tan + normed_t * grad, axis=1, keepdims=True)
        second = (second - slope_r / scale * first) / scale
        lane = lax.broadcasted_iota(jnp.int32, (tok_dev, 128), 1)
        sums = jnp.where(lane == 0, first / scale, jnp.where(lane == 1, second, 0.0))
        home[:, width:] = sums.astype(home.dtype)


def experts(packs, kinds, held, expert_count):
    count = len(packs)
    tok_dev = packs[0].shape[0]
    _, width, hidden = held.shape
    rows = count * tok_dev
    whole = pl.BlockSpec(memory_space=pltpu.VMEM)
    return pl.pallas_call(
        functools.partial(expert_kernel, count, expert_count),
        out_shape=[jax.ShapeDtypeStruct((tok_dev, n * (width + 128)), kind) for kind, n in kinds],
        in_specs=[whole] * (count + 1),
        out_specs=[whole] * len(kinds),
        scratch_shapes=[
            pltpu.VMEM((2 * rows, width), jnp.bfloat16),
            pltpu.VMEM((rows, width), jnp.bfloat16),
            pltpu.VMEM((2 * rows, width), jnp.float32),
        ],
        compiler_params=pltpu.CompilerParams(vmem_limit_bytes=VMEM),
        cost_estimate=pl.CostEstimate(
            flops=2 * 9 * rows * width * hidden,
            bytes_accessed=6 * width * hidden,
            transcendentals=rows * hidden,
        ),
    )(*packs, pltpu.with_memory_space_constraint(held, pltpu.VMEM))


def finish_kernel(tokens, gain, signs, *refs):
    arrived, hvp, quad = (refs[:-2], refs[-2], refs[-1])
    width = tokens.shape[1]
    xf = tokens[...].astype(jnp.float32)
    probe = (2 * signs[...] - 1).astype(jnp.float32)
    scale, along = rms_terms(xf, probe)
    slope_r = -(scale**3) * along
    lanes = arrived[0].shape[1]
    rows = sum(part[:, :lanes].astype(jnp.float32) for part in arrived)
    first = rows[:, width : width + 1]
    second = rows[:, width + 1 : width + 2]
    whole = (
        gain[...] * rows[:, :width]
        - 3.0 * scale**2 * slope_r * first * xf
        - scale**3 * first * probe
        - scale**3 * second * xf
    )
    hvp[...] = whole
    column = jnp.mean(probe * whole, axis=1, keepdims=True)
    tok_dev = column.shape[0]
    quad[...] = jnp.sum(identity(tok_dev) * column, axis=0, keepdims=True)


def moved(rows, turns, flip_x=False, flip_core=False):
    count = lax.axis_size("expert")
    pairs = [
        (i, (i + 4 * turns * (1 - 2 * (i % 2))) % count ^ (2 * flip_x) ^ (1 * flip_core))
        for i in range(count)
    ]
    return lax.ppermute(rows, "expert", pairs)


def dense_local(tokens, norm_gain, probe_signs, cotangent, routes, gates, weights):
    tok_dev, width = tokens.shape
    n_exp = lax.axis_size("expert")
    expert_count = n_exp // 2
    pack = packed(tokens, norm_gain, probe_signs, cotangent, routes, gates, expert_count)
    held = joined(weights, moved(weights, 0, flip_core=True))
    same, across = {0: pack}, {}
    same[1] = moved(pack, 1)
    across[0] = moved(pack, 0, flip_x=True)
    same[1] = lax.optimization_barrier((same[1], across[0], held))[0]
    same[3] = moved(lax.optimization_barrier((pack, same[1]))[0], -1)
    same[2] = moved(same[1], 1)
    across[1] = moved(same[1], 0, flip_x=True)
    across[3] = moved(same[3], 0, flip_x=True)
    across[2] = moved(same[2], 0, flip_x=True)
    wide, sent, pair = ((jnp.float32, 1), (jnp.bfloat16, 1), (jnp.bfloat16, 2))
    here = {}
    here[0], here[1], here[2], here[3], there = experts(
        [same[0], same[1], same[2], same[3], across[0], across[1]],
        [wide, wide, sent, sent, pair],
        held,
        expert_count,
    )
    late = lax.optimization_barrier((across[2], across[3], here[1]))[:2]
    far, last = experts(late, [sent, sent], held, expert_count)

    def total(*parts):
        return sum(part.astype(jnp.float32) for part in parts).astype(jnp.bfloat16)

    beside, forward = (moved(there, 0, flip_x=True), moved(here[2], -1))
    kept = lax.optimization_barrier((here[1], far))[0]
    arrived = [
        here[0],
        beside,
        moved(here[3], 1),
        moved(far, 2, flip_x=True),
        moved(last, 1, flip_x=True),
        moved(total(kept, beside[:, kept.shape[1] :], forward), -1),
    ]
    hvp, quad = pl.pallas_call(
        finish_kernel,
        out_shape=[
            jax.ShapeDtypeStruct((tok_dev, width), jnp.float32),
            jax.ShapeDtypeStruct((1, tok_dev), jnp.float32),
        ],
        compiler_params=pltpu.CompilerParams(vmem_limit_bytes=VMEM),
        cost_estimate=pl.CostEstimate(
            flops=40 * tok_dev * width, bytes_accessed=26 * tok_dev * width, transcendentals=0
        ),
    )(tokens, norm_gain.reshape(1, width), probe_signs, *arrived)
    return (hvp, quad.reshape(tok_dev))


def routed_rows(normed, normed_t, cotangent, routes, gates, weights):
    tok_dev, width = normed.shape
    groups_here = routes.shape[0]
    half = routes.shape[2]
    n_exp = lax.axis_size("expert")
    expert_count = n_exp // 2
    cap = capacity(tok_dev, half, expert_count)
    buffer_rows = expert_count * cap
    stack_z, stack_t, stack_c, stack_w = ([], [], [], [])
    for group in range(groups_here):
        target = slot_targets(routes[group], expert_count, cap)
        place = (jnp.arange(buffer_rows, dtype=jnp.int32)[:, None] == target[None, :]).reshape(
            buffer_rows, tok_dev, half
        )
        place_tok = jnp.sum(place.astype(jnp.float32), axis=2).astype(jnp.bfloat16)
        stack_w.append(jnp.sum(place.astype(jnp.float32) * gates[group][None, :, :], axis=2))
        stack_z.append(
            jnp.dot(place_tok, normed, preferred_element_type=jnp.float32).astype(jnp.bfloat16)
        )
        stack_t.append(
            jnp.dot(place_tok, normed_t, preferred_element_type=jnp.float32).astype(jnp.bfloat16)
        )
        stack_c.append(
            jnp.dot(place_tok, cotangent, preferred_element_type=jnp.float32).astype(jnp.bfloat16)
        )
    rows_z = jnp.stack(stack_z, 0)
    rows_t = jnp.stack(stack_t, 0)
    rows_c = jnp.stack(stack_c, 0)
    weighted = jnp.stack(stack_w, 0)

    def arrange(rows):
        shaped = rows.reshape(groups_here, expert_count, 1, cap, width)
        shaped = jnp.broadcast_to(shaped, (groups_here, expert_count, 2, cap, width))
        return jnp.transpose(shaped, (1, 2, 0, 3, 4)).reshape(n_exp, groups_here * cap, width)

    send_z, send_t, send_c = (arrange(rows_z), arrange(rows_t), arrange(rows_c))
    got_z = lax.all_to_all(send_z, "expert", split_axis=0, concat_axis=0, tiled=True)
    got_t = lax.all_to_all(send_t, "expert", split_axis=0, concat_axis=0, tiled=True)
    got_c = lax.all_to_all(send_c, "expert", split_axis=0, concat_axis=0, tiled=True)
    sources, items, cols = got_z.shape
    g_rows, t_rows = expert_terms(
        weights, got_z.reshape(-1, cols), got_t.reshape(-1, cols), got_c.reshape(-1, cols)
    )
    g_rows = g_rows.reshape(sources, items, cols)
    t_rows = t_rows.reshape(sources, items, cols)
    back_g = lax.all_to_all(g_rows, "expert", split_axis=0, concat_axis=0, tiled=True)
    back_t = lax.all_to_all(t_rows, "expert", split_axis=0, concat_axis=0, tiled=True)

    def restore(rows):
        shaped = jnp.sum(rows.reshape(expert_count, 2, groups_here, cap, width), axis=1)
        return jnp.transpose(shaped, (1, 0, 2, 3)).reshape(groups_here, buffer_rows, width)

    back_g = restore(back_g)
    back_t = restore(back_t)
    contract = (((0, 1), (0, 1)), ((), ()))
    grad_z = lax.dot_general(weighted, back_g, contract, precision=lax.Precision.HIGHEST)
    tan_z = lax.dot_general(weighted, back_t, contract, precision=lax.Precision.HIGHEST)
    return (grad_z, tan_z)


def local(tokens, norm_gain, probe_signs, cotangent, routes, gates, expert_weights):
    cap = capacity(tokens.shape[0], routes.shape[2], lax.axis_size("expert") // 2)
    layout = (lax.axis_size("expert"), lax.axis_size("node"))
    if layout == (16, 1) and routes.shape[0] * cap >= tokens.shape[0]:
        return dense_local(
            tokens, norm_gain, probe_signs, cotangent, routes, gates, expert_weights
        )
    xf = tokens.astype(jnp.float32)
    probe = (2 * probe_signs - 1).astype(jnp.float32)
    tok_dev, width = xf.shape
    scale = lax.rsqrt(jnp.mean(xf * xf, axis=1, keepdims=True) + EPS)
    along = jnp.mean(xf * probe, axis=1, keepdims=True)
    normed = (xf * scale * norm_gain).astype(jnp.bfloat16)
    normed_t = (norm_gain * (scale * probe - scale**3 * xf * along)).astype(jnp.bfloat16)
    own_half = lax.all_gather(expert_weights, "node", axis=2, tiled=True)
    grad_z, tan_z = routed_rows(normed, normed_t, cotangent, routes, gates, own_half)
    share = width // lax.axis_size("node")
    start = lax.axis_index("node") * share
    slope_r = -(scale**3) * along
    grad_z, tan_z = lax.psum((grad_z, tan_z), "node")
    lifted = norm_gain * grad_z
    lifted_t = norm_gain * tan_z
    first = jnp.mean(xf * lifted, axis=1, keepdims=True)
    second = jnp.mean(xf * lifted_t, axis=1, keepdims=True)
    third = jnp.mean(probe * lifted, axis=1, keepdims=True)
    whole_hvp = (
        scale * lifted_t
        + slope_r * lifted
        - 3.0 * scale**2 * slope_r * first * xf
        - scale**3 * first * probe
        - scale**3 * (second + third) * xf
    )
    quad = jnp.mean(probe * whole_hvp, axis=1)
    hvp = lax.dynamic_slice_in_dim(whole_hvp, start, share, 1)
    return (hvp, quad)


def solution(mesh):
    placed = (
        P(("groups", "expert"), None),
        P(),
        P(("groups", "expert"), None),
        P(("groups", "expert"), None),
        P("node", ("groups", "expert"), None),
        P("node", ("groups", "expert"), None),
        P(None, None, ("expert", "node")),
    )
    return jax.shard_map(
        local,
        mesh=mesh,
        in_specs=placed,
        out_specs=(P(("groups", "expert"), "node"), P(("groups", "expert"))),
        check_vma=False,
    )
```

```python
import functools

import jax
import jax.numpy as jnp
from jax import lax
from jax.experimental import pallas as pl
from jax.experimental.pallas import tpu as pltpu
from jax.sharding import PartitionSpec as P

EPS = 1e-06
VMEM = 24 * 1024 * 1024


def expert_terms(weights, rows, rows_t, cotan):
    count = rows.shape[0]
    both = jnp.concatenate([rows, rows_t], 0)
    pre_gate = jnp.dot(both, weights[0], preferred_element_type=jnp.float32)
    pre_up = jnp.dot(both, weights[1], preferred_element_type=jnp.float32)
    gate, gate_t = (pre_gate[:count], pre_gate[count:])
    up, up_t = (pre_up[:count], pre_up[count:])
    back = jnp.dot(cotan, weights[2], preferred_element_type=jnp.float32)
    sig = jax.nn.sigmoid(gate)
    act = gate * sig
    slope = sig * (1.0 + gate * (1.0 - sig))
    bend = sig * (1.0 - sig) * (2.0 + gate * (1.0 - 2.0 * sig))
    d_gate = (back * slope * up).astype(jnp.bfloat16)
    d_up = (back * act).astype(jnp.bfloat16)
    t_gate = (back * (bend * gate_t * up + slope * up_t)).astype(jnp.bfloat16)
    t_up = (back * slope * gate_t).astype(jnp.bfloat16)
    contract = (((1,), (1,)), ((), ()))
    lhs_gate = jnp.concatenate([d_gate, t_gate], 0)
    lhs_up = jnp.concatenate([d_up, t_up], 0)
    total = lax.dot_general(lhs_gate, weights[0], contract, preferred_element_type=jnp.float32)
    total = total + lax.dot_general(
        lhs_up, weights[1], contract, preferred_element_type=jnp.float32
    )
    return (total[:count], total[count:])


def slot_targets(route_ids, expert_count, capacity):
    flat = route_ids.reshape(-1)
    count = flat.shape[0]
    onehot = (flat[:, None] == jnp.arange(expert_count, dtype=jnp.int32)[None, :]).astype(
        jnp.float32
    )
    lower = (jnp.arange(count)[:, None] > jnp.arange(count)[None, :]).astype(jnp.float32)
    before = jnp.dot(lower, onehot, precision=lax.Precision.HIGHEST)
    rank = jnp.sum(before * onehot, axis=1).astype(jnp.int32)
    return flat * capacity + rank


def capacity(tok_dev, half, expert_count):
    return min(2 * ((2 * tok_dev * half + 3 * expert_count - 1) // (3 * expert_count)), tok_dev)


def rms_terms(xf, probe):
    scale = lax.rsqrt(jnp.mean(xf * xf, axis=1, keepdims=True) + EPS)
    along = jnp.mean(xf * probe, axis=1, keepdims=True)
    return scale, along


def pack_kernel(expert_count, *refs):
    sources, pack, held, sems = (refs[:6], refs[6], refs[7:13], refs[13])
    copies = [
        pltpu.make_async_copy(source, target, sems.at[n])
        for n, (source, target) in enumerate(zip(sources, held))
    ]
    for copy in copies:
        copy.start()
    for copy in copies:
        copy.wait()
    tokens, gain, signs, cotangent, routes, gates = held
    width = tokens.shape[1]
    xf = tokens[...].astype(jnp.float32)
    probe = (2 * signs[...] - 1).astype(jnp.float32)
    scale, along = rms_terms(xf, probe)
    pack[:, :width] = (xf * scale * gain[...]).astype(jnp.bfloat16)
    tangent = gain[...] * (scale * probe - scale**3 * xf * along)
    pack[:, width : 2 * width] = tangent.astype(jnp.bfloat16)
    pack[:, 2 * width : 3 * width] = cotangent[...]
    tok_dev, lanes = (tokens.shape[0], pack.shape[1] - 3 * width)
    lane = lax.broadcasted_iota(jnp.int32, (lanes, tok_dev), 0)
    expert = lax.rem(lane, expert_count)
    gate = jnp.zeros(lane.shape, jnp.float32)
    for group in range(routes.shape[0]):
        for slot in range(routes.shape[1]):
            named = routes[group, slot : slot + 1, :] == expert
            gate = gate + jnp.where(named, gates[group, slot : slot + 1, :], 0.0)
    high = gate.astype(jnp.bfloat16).astype(jnp.float32)
    tail = jnp.where(lane < expert_count, high, gate - high)
    tail = jnp.where(lane < 2 * expert_count, tail, 0.0).astype(jnp.bfloat16)
    turned = lax.dot_general(
        identity(tok_dev).astype(jnp.bfloat16),
        tail,
        (((1,), (1,)), ((), ())),
        preferred_element_type=jnp.float32,
    )
    lane = lax.broadcasted_iota(jnp.int32, (tok_dev, lanes), 1)
    place = 2 * expert_count
    for number in (scale, -(scale**3) * along):
        for _ in range(3):
            addend = number.astype(jnp.bfloat16).astype(jnp.float32)
            turned = jnp.where(lane == place, addend, turned)
            number = number - addend
            place += 1
    pack[:, 3 * width :] = turned.astype(jnp.bfloat16)


def identity(size):
    rows = lax.broadcasted_iota(jnp.int32, (size, size), 0)
    return (rows == lax.broadcasted_iota(jnp.int32, (size, size), 1)).astype(jnp.float32)


def packed(tokens, norm_gain, probe_signs, cotangent, routes, gates, expert_count):
    tok_dev, width = tokens.shape
    tail = -(-(2 * expert_count + 6) // 128) * 128
    token_minor = (0, 2, 1)
    operands = (
        tokens,
        norm_gain.reshape(1, width),
        probe_signs,
        cotangent,
        jnp.transpose(routes, token_minor),
        jnp.transpose(gates, token_minor),
    )
    return pl.pallas_call(
        functools.partial(pack_kernel, expert_count),
        out_shape=jax.ShapeDtypeStruct((tok_dev, 3 * width + tail), jnp.bfloat16),
        in_specs=[pl.BlockSpec(memory_space=pl.ANY)] * 6,
        out_specs=pl.BlockSpec(memory_space=pltpu.VMEM),
        scratch_shapes=[pltpu.VMEM(array.shape, array.dtype) for array in operands]
        + [pltpu.SemaphoreType.DMA((6,))],
        compiler_params=pltpu.CompilerParams(vmem_limit_bytes=VMEM),
        cost_estimate=pl.CostEstimate(
            flops=20 * tok_dev * width, bytes_accessed=14 * tok_dev * width, transcendentals=0
        ),
    )(*(pltpu.with_memory_space_constraint(array, pltpu.HBM) for array in operands))


def join_kernel(own, other, held, sems):
    half = own.shape[2]
    copies = [
        pltpu.make_async_copy(
            source.at[part], held.at[part, :, pl.ds(h * half, half)], sems.at[h, part]
        )
        for h, source in enumerate((own, other))
        for part in range(3)
    ]
    for copy in copies:
        copy.start()
    for copy in copies:
        copy.wait()


def joined(own, other):
    parts, width, half = own.shape
    return pl.pallas_call(
        join_kernel,
        out_shape=pltpu.VMEM((parts, width, 2 * half), own.dtype),
        in_specs=[pl.BlockSpec(memory_space=pl.ANY)] * 2,
        out_specs=pl.BlockSpec(memory_space=pltpu.VMEM),
        scratch_shapes=[pltpu.SemaphoreType.DMA((2, parts))],
        compiler_params=pltpu.CompilerParams(vmem_limit_bytes=VMEM),
        cost_estimate=pl.CostEstimate(
            flops=0, bytes_accessed=8 * parts * width * half, transcendentals=0
        ),
    )(pltpu.with_memory_space_constraint(own, pltpu.HBM), other)


def expert_kernel(count, expert_count, *refs):
    packs, held, outs = (refs[:count], refs[count], refs[count + 1 : -4])
    both, cotan, slopes, acc = refs[-4:]
    tok_dev = packs[0].shape[0]
    _, width, hidden = held.shape
    rows = count * tok_dev

    def stacked(start, size):
        return jnp.concatenate([p[:, start : start + size].astype(jnp.float32) for p in packs], 0)

    both[:rows, :] = stacked(0, width).astype(jnp.bfloat16)
    both[rows:, :] = stacked(width, width).astype(jnp.bfloat16)
    cotan[...] = stacked(2 * width, width).astype(jnp.bfloat16)
    tail = stacked(3 * width, packs[0].shape[1] - 3 * width)
    mine = lax.axis_index("expert") // 2
    lane = lax.broadcasted_iota(jnp.int32, tail.shape, 1)
    after = 2 * expert_count

    def picked(lanes):
        return jnp.sum(jnp.where(lanes, tail, 0.0), axis=1, keepdims=True)

    gate_row = picked((lane == mine) | (lane == mine + expert_count))
    scale_row = picked((lane >= after) & (lane < after + 3))
    slope_row = picked((lane >= after + 3) & (lane < after + 6))

    def weights(part, start, size):
        return held[part, :, start : start + size]

    block = 256 if hidden % 256 == 0 else 128
    contract = (((1,), (1,)), ((), ()))
    for start in range(0, hidden, block):
        pre_gate = jnp.dot(
            both[...], weights(0, start, block), preferred_element_type=jnp.float32
        )
        pre_up = jnp.dot(both[...], weights(1, start, block), preferred_element_type=jnp.float32)
        back = jnp.dot(cotan[...], weights(2, start, block), preferred_element_type=jnp.float32)
        gate, gate_t = (pre_gate[:rows], pre_gate[rows:])
        up, up_t = (pre_up[:rows], pre_up[rows:])
        sig = jax.nn.sigmoid(gate)
        act = gate * sig
        slope = sig * (1.0 + gate * (1.0 - sig))
        bend = sig * (1.0 - sig) * (2.0 + gate * (1.0 - 2.0 * sig))
        d_gate = (back * slope * up).astype(jnp.bfloat16)
        d_up = (back * act).astype(jnp.bfloat16)
        t_gate = (back * (bend * gate_t * up + slope * up_t)).astype(jnp.bfloat16)
        t_up = (back * slope * gate_t).astype(jnp.bfloat16)
        for n, (own, along) in enumerate(((d_gate, t_gate), (d_up, t_up))):
            slopes[n, :rows, start : start + block] = own
            slopes[n, rows:, start : start + block] = along
    block = 256 if width % 256 == 0 else width
    for start in range(0, width, block):
        acc[:, start : start + block] = sum(
            lax.dot_general(
                slopes[n],
                held[n, start : start + block, :],
                contract,
                preferred_element_type=jnp.float32,
            )
            for n in range(2)
        )
    homes = [out.at[:, pl.ds(at, width + 128)] for out in outs for at in range(0, out.shape[1], width + 128)]
    for n, home in enumerate(homes):
        part = slice(n * tok_dev, (n + 1) * tok_dev)
        later = slice(rows + n * tok_dev, rows + (n + 1) * tok_dev)
        grad, tan = (acc[part] * gate_row[part], acc[later] * gate_row[part])
        scale, slope_r = (scale_row[part], slope_row[part])
        normed = packs[n][:, :width].astype(jnp.float32)
        normed_t = packs[n][:, width : 2 * width].astype(jnp.float32)
        home[:, :width] = (scale * tan + slope_r * grad).astype(home.dtype)
        first = jnp.mean(normed * grad, axis=1, keepdims=True)
        second = jnp.mean(normed * tan + normed_t * grad, axis=1, keepdims=True)
        second = (second - slope_r / scale * first) / scale
        lane = lax.broadcasted_iota(jnp.int32, (tok_dev, 128), 1)
        sums = jnp.where(lane == 0, first / scale, jnp.where(lane == 1, second, 0.0))
        home[:, width:] = sums.astype(home.dtype)


def experts(packs, kinds, held, expert_count):
    count = len(packs)
    tok_dev = packs[0].shape[0]
    _, width, hidden = held.shape
    rows = count * tok_dev
    whole = pl.BlockSpec(memory_space=pltpu.VMEM)
    return pl.pallas_call(
        functools.partial(expert_kernel, count, expert_count),
        out_shape=[jax.ShapeDtypeStruct((tok_dev, n * (width + 128)), kind) for kind, n in kinds],
        in_specs=[whole] * (count + 1),
        out_specs=[whole] * len(kinds),
        scratch_shapes=[
            pltpu.VMEM((2 * rows, width), jnp.bfloat16),
            pltpu.VMEM((rows, width), jnp.bfloat16),
            pltpu.VMEM((2, 2 * rows, hidden), jnp.bfloat16),
            pltpu.VMEM((2 * rows, width), jnp.float32),
        ],
        compiler_params=pltpu.CompilerParams(vmem_limit_bytes=VMEM),
        cost_estimate=pl.CostEstimate(
            flops=2 * 9 * rows * width * hidden,
            bytes_accessed=6 * width * hidden,
            transcendentals=rows * hidden,
        ),
    )(*packs, pltpu.with_memory_space_constraint(held, pltpu.VMEM))


def finish_kernel(tokens, gain, signs, *refs):
    arrived, hvp, quad = (refs[:-2], refs[-2], refs[-1])
    width = tokens.shape[1]
    xf = tokens[...].astype(jnp.float32)
    probe = (2 * signs[...] - 1).astype(jnp.float32)
    scale, along = rms_terms(xf, probe)
    slope_r = -(scale**3) * along
    lanes = arrived[0].shape[1]
    rows = sum(part[:, :lanes].astype(jnp.float32) for part in arrived)
    first = rows[:, width : width + 1]
    second = rows[:, width + 1 : width + 2]
    whole = (
        gain[...] * rows[:, :width]
        - 3.0 * scale**2 * slope_r * first * xf
        - scale**3 * first * probe
        - scale**3 * second * xf
    )
    hvp[...] = whole
    column = jnp.mean(probe * whole, axis=1, keepdims=True)
    tok_dev = column.shape[0]
    quad[...] = jnp.sum(identity(tok_dev) * column, axis=0, keepdims=True)


def moved(rows, turns, flip_x=False, flip_core=False):
    count = lax.axis_size("expert")
    pairs = [
        (i, (i + 4 * turns) % count ^ (2 * flip_x) ^ (1 * flip_core)) for i in range(count)
    ]
    return lax.ppermute(rows, "expert", pairs)


def dense_local(tokens, norm_gain, probe_signs, cotangent, routes, gates, weights):
    tok_dev, width = tokens.shape
    n_exp = lax.axis_size("expert")
    expert_count = n_exp // 2
    pack = packed(tokens, norm_gain, probe_signs, cotangent, routes, gates, expert_count)
    held = joined(weights, moved(weights, 0, flip_core=True))
    same, across = {0: pack}, {}
    same[1] = moved(pack, 1)
    across[0] = moved(pack, 0, flip_x=True)
    same[1] = lax.optimization_barrier((same[1], across[0], held))[0]
    same[3] = moved(lax.optimization_barrier((pack, same[1]))[0], -1)
    same[2] = moved(same[1], 1)
    across[1] = moved(same[1], 0, flip_x=True)
    across[3] = moved(same[3], 0, flip_x=True)
    across[2] = moved(same[2], 0, flip_x=True)
    wide, sent, pair = ((jnp.float32, 1), (jnp.bfloat16, 1), (jnp.bfloat16, 2))
    here = {}
    here[0], here[1], here[2], here[3], there = experts(
        [same[0], same[1], same[2], same[3], across[0], across[1]],
        [wide, wide, sent, sent, pair],
        held,
        expert_count,
    )
    late = lax.optimization_barrier((across[2], across[3], here[1]))[:2]
    far, last = experts(late, [sent, sent], held, expert_count)

    def total(*parts):
        return sum(part.astype(jnp.float32) for part in parts).astype(jnp.bfloat16)

    beside, forward = (moved(there, 0, flip_x=True), moved(here[2], -1))
    kept = lax.optimization_barrier((here[1], far))[0]
    arrived = [
        here[0],
        beside,
        moved(here[3], 1),
        moved(far, 2, flip_x=True),
        moved(last, 1, flip_x=True),
        moved(total(kept, beside[:, kept.shape[1] :], forward), -1),
    ]
    hvp, quad = pl.pallas_call(
        finish_kernel,
        out_shape=[
            jax.ShapeDtypeStruct((tok_dev, width), jnp.float32),
            jax.ShapeDtypeStruct((1, tok_dev), jnp.float32),
        ],
        compiler_params=pltpu.CompilerParams(vmem_limit_bytes=VMEM),
        cost_estimate=pl.CostEstimate(
            flops=40 * tok_dev * width, bytes_accessed=26 * tok_dev * width, transcendentals=0
        ),
    )(tokens, norm_gain.reshape(1, width), probe_signs, *arrived)
    return (hvp, quad.reshape(tok_dev))


def routed_rows(normed, normed_t, cotangent, routes, gates, weights):
    tok_dev, width = normed.shape
    groups_here = routes.shape[0]
    half = routes.shape[2]
    n_exp = lax.axis_size("expert")
    expert_count = n_exp // 2
    cap = capacity(tok_dev, half, expert_count)
    buffer_rows = expert_count * cap
    stack_z, stack_t, stack_c, stack_w = ([], [], [], [])
    for group in range(groups_here):
        target = slot_targets(routes[group], expert_count, cap)
        place = (jnp.arange(buffer_rows, dtype=jnp.int32)[:, None] == target[None, :]).reshape(
            buffer_rows, tok_dev, half
        )
        place_tok = jnp.sum(place.astype(jnp.float32), axis=2).astype(jnp.bfloat16)
        stack_w.append(jnp.sum(place.astype(jnp.float32) * gates[group][None, :, :], axis=2))
        stack_z.append(
            jnp.dot(place_tok, normed, preferred_element_type=jnp.float32).astype(jnp.bfloat16)
        )
        stack_t.append(
            jnp.dot(place_tok, normed_t, preferred_element_type=jnp.float32).astype(jnp.bfloat16)
        )
        stack_c.append(
            jnp.dot(place_tok, cotangent, preferred_element_type=jnp.float32).astype(jnp.bfloat16)
        )
    rows_z = jnp.stack(stack_z, 0)
    rows_t = jnp.stack(stack_t, 0)
    rows_c = jnp.stack(stack_c, 0)
    weighted = jnp.stack(stack_w, 0)

    def arrange(rows):
        shaped = rows.reshape(groups_here, expert_count, 1, cap, width)
        shaped = jnp.broadcast_to(shaped, (groups_here, expert_count, 2, cap, width))
        return jnp.transpose(shaped, (1, 2, 0, 3, 4)).reshape(n_exp, groups_here * cap, width)

    send_z, send_t, send_c = (arrange(rows_z), arrange(rows_t), arrange(rows_c))
    got_z = lax.all_to_all(send_z, "expert", split_axis=0, concat_axis=0, tiled=True)
    got_t = lax.all_to_all(send_t, "expert", split_axis=0, concat_axis=0, tiled=True)
    got_c = lax.all_to_all(send_c, "expert", split_axis=0, concat_axis=0, tiled=True)
    sources, items, cols = got_z.shape
    g_rows, t_rows = expert_terms(
        weights, got_z.reshape(-1, cols), got_t.reshape(-1, cols), got_c.reshape(-1, cols)
    )
    g_rows = g_rows.reshape(sources, items, cols)
    t_rows = t_rows.reshape(sources, items, cols)
    back_g = lax.all_to_all(g_rows, "expert", split_axis=0, concat_axis=0, tiled=True)
    back_t = lax.all_to_all(t_rows, "expert", split_axis=0, concat_axis=0, tiled=True)

    def restore(rows):
        shaped = jnp.sum(rows.reshape(expert_count, 2, groups_here, cap, width), axis=1)
        return jnp.transpose(shaped, (1, 0, 2, 3)).reshape(groups_here, buffer_rows, width)

    back_g = restore(back_g)
    back_t = restore(back_t)
    contract = (((0, 1), (0, 1)), ((), ()))
    grad_z = lax.dot_general(weighted, back_g, contract, precision=lax.Precision.HIGHEST)
    tan_z = lax.dot_general(weighted, back_t, contract, precision=lax.Precision.HIGHEST)
    return (grad_z, tan_z)


def local(tokens, norm_gain, probe_signs, cotangent, routes, gates, expert_weights):
    cap = capacity(tokens.shape[0], routes.shape[2], lax.axis_size("expert") // 2)
    layout = (lax.axis_size("expert"), lax.axis_size("node"))
    if layout == (16, 1) and routes.shape[0] * cap >= tokens.shape[0]:
        return dense_local(
            tokens, norm_gain, probe_signs, cotangent, routes, gates, expert_weights
        )
    xf = tokens.astype(jnp.float32)
    probe = (2 * probe_signs - 1).astype(jnp.float32)
    tok_dev, width = xf.shape
    scale = lax.rsqrt(jnp.mean(xf * xf, axis=1, keepdims=True) + EPS)
    along = jnp.mean(xf * probe, axis=1, keepdims=True)
    normed = (xf * scale * norm_gain).astype(jnp.bfloat16)
    normed_t = (norm_gain * (scale * probe - scale**3 * xf * along)).astype(jnp.bfloat16)
    own_half = lax.all_gather(expert_weights, "node", axis=2, tiled=True)
    grad_z, tan_z = routed_rows(normed, normed_t, cotangent, routes, gates, own_half)
    share = width // lax.axis_size("node")
    start = lax.axis_index("node") * share
    slope_r = -(scale**3) * along
    grad_z, tan_z = lax.psum((grad_z, tan_z), "node")
    lifted = norm_gain * grad_z
    lifted_t = norm_gain * tan_z
    first = jnp.mean(xf * lifted, axis=1, keepdims=True)
    second = jnp.mean(xf * lifted_t, axis=1, keepdims=True)
    third = jnp.mean(probe * lifted, axis=1, keepdims=True)
    whole_hvp = (
        scale * lifted_t
        + slope_r * lifted
        - 3.0 * scale**2 * slope_r * first * xf
        - scale**3 * first * probe
        - scale**3 * (second + third) * xf
    )
    quad = jnp.mean(probe * whole_hvp, axis=1)
    hvp = lax.dynamic_slice_in_dim(whole_hvp, start, share, 1)
    return (hvp, quad)


def solution(mesh):
    placed = (
        P(("groups", "expert"), None),
        P(),
        P(("groups", "expert"), None),
        P(("groups", "expert"), None),
        P("node", ("groups", "expert"), None),
        P("node", ("groups", "expert"), None),
        P(None, None, ("expert", "node")),
    )
    return jax.shard_map(
        local,
        mesh=mesh,
        in_specs=placed,
        out_specs=(P(("groups", "expert"), "node"), P(("groups", "expert"))),
        check_vma=False,
    )
```

```python
import functools

import jax
import jax.numpy as jnp
from jax import lax
from jax.experimental import pallas as pl
from jax.experimental.pallas import tpu as pltpu
from jax.sharding import PartitionSpec as P

EPS = 1e-06
VMEM = 24 * 1024 * 1024


def expert_terms(weights, rows, rows_t, cotan):
    count = rows.shape[0]
    both = jnp.concatenate([rows, rows_t], 0)
    pre_gate = jnp.dot(both, weights[0], preferred_element_type=jnp.float32)
    pre_up = jnp.dot(both, weights[1], preferred_element_type=jnp.float32)
    gate, gate_t = (pre_gate[:count], pre_gate[count:])
    up, up_t = (pre_up[:count], pre_up[count:])
    back = jnp.dot(cotan, weights[2], preferred_element_type=jnp.float32)
    sig = jax.nn.sigmoid(gate)
    act = gate * sig
    slope = sig * (1.0 + gate * (1.0 - sig))
    bend = sig * (1.0 - sig) * (2.0 + gate * (1.0 - 2.0 * sig))
    d_gate = (back * slope * up).astype(jnp.bfloat16)
    d_up = (back * act).astype(jnp.bfloat16)
    t_gate = (back * (bend * gate_t * up + slope * up_t)).astype(jnp.bfloat16)
    t_up = (back * slope * gate_t).astype(jnp.bfloat16)
    contract = (((1,), (1,)), ((), ()))
    lhs_gate = jnp.concatenate([d_gate, t_gate], 0)
    lhs_up = jnp.concatenate([d_up, t_up], 0)
    total = lax.dot_general(lhs_gate, weights[0], contract, preferred_element_type=jnp.float32)
    total = total + lax.dot_general(
        lhs_up, weights[1], contract, preferred_element_type=jnp.float32
    )
    return (total[:count], total[count:])


def slot_targets(route_ids, expert_count, capacity):
    flat = route_ids.reshape(-1)
    count = flat.shape[0]
    onehot = (flat[:, None] == jnp.arange(expert_count, dtype=jnp.int32)[None, :]).astype(
        jnp.float32
    )
    lower = (jnp.arange(count)[:, None] > jnp.arange(count)[None, :]).astype(jnp.float32)
    before = jnp.dot(lower, onehot, precision=lax.Precision.HIGHEST)
    rank = jnp.sum(before * onehot, axis=1).astype(jnp.int32)
    return flat * capacity + rank


def capacity(tok_dev, half, expert_count):
    return min(2 * ((2 * tok_dev * half + 3 * expert_count - 1) // (3 * expert_count)), tok_dev)


def rms_terms(xf, probe):
    scale = lax.rsqrt(jnp.mean(xf * xf, axis=1, keepdims=True) + EPS)
    along = jnp.mean(xf * probe, axis=1, keepdims=True)
    return scale, along


def pack_kernel(expert_count, *refs):
    sources, pack, held, sems = (refs[:6], refs[6], refs[7:13], refs[13])
    copies = [
        pltpu.make_async_copy(source, target, sems.at[n])
        for n, (source, target) in enumerate(zip(sources, held))
    ]
    for copy in copies:
        copy.start()
    for copy in copies:
        copy.wait()
    tokens, gain, signs, cotangent, routes, gates = held
    width = tokens.shape[1]
    xf = tokens[...].astype(jnp.float32)
    probe = (2 * signs[...] - 1).astype(jnp.float32)
    scale, along = rms_terms(xf, probe)
    pack[:, :width] = (xf * scale * gain[...]).astype(jnp.bfloat16)
    tangent = gain[...] * (scale * probe - scale**3 * xf * along)
    pack[:, width : 2 * width] = tangent.astype(jnp.bfloat16)
    pack[:, 2 * width : 3 * width] = cotangent[...]
    tok_dev, lanes = (tokens.shape[0], pack.shape[1] - 3 * width)
    lane = lax.broadcasted_iota(jnp.int32, (lanes, tok_dev), 0)
    expert = lax.rem(lane, expert_count)
    gate = jnp.zeros(lane.shape, jnp.float32)
    for group in range(routes.shape[0]):
        for slot in range(routes.shape[1]):
            named = routes[group, slot : slot + 1, :] == expert
            gate = gate + jnp.where(named, gates[group, slot : slot + 1, :], 0.0)
    high = gate.astype(jnp.bfloat16).astype(jnp.float32)
    tail = jnp.where(lane < expert_count, high, gate - high)
    tail = jnp.where(lane < 2 * expert_count, tail, 0.0).astype(jnp.bfloat16)
    turned = lax.dot_general(
        identity(tok_dev).astype(jnp.bfloat16),
        tail,
        (((1,), (1,)), ((), ())),
        preferred_element_type=jnp.float32,
    )
    lane = lax.broadcasted_iota(jnp.int32, (tok_dev, lanes), 1)
    place = 2 * expert_count
    for number in (scale, -(scale**3) * along):
        for _ in range(3):
            addend = number.astype(jnp.bfloat16).astype(jnp.float32)
            turned = jnp.where(lane == place, addend, turned)
            number = number - addend
            place += 1
    pack[:, 3 * width :] = turned.astype(jnp.bfloat16)


def identity(size):
    rows = lax.broadcasted_iota(jnp.int32, (size, size), 0)
    return (rows == lax.broadcasted_iota(jnp.int32, (size, size), 1)).astype(jnp.float32)


def packed(tokens, norm_gain, probe_signs, cotangent, routes, gates, expert_count):
    tok_dev, width = tokens.shape
    tail = -(-(2 * expert_count + 6) // 128) * 128
    token_minor = (0, 2, 1)
    operands = (
        tokens,
        norm_gain.reshape(1, width),
        probe_signs,
        cotangent,
        jnp.transpose(routes, token_minor),
        jnp.transpose(gates, token_minor),
    )
    return pl.pallas_call(
        functools.partial(pack_kernel, expert_count),
        out_shape=jax.ShapeDtypeStruct((tok_dev, 3 * width + tail), jnp.bfloat16),
        in_specs=[pl.BlockSpec(memory_space=pl.ANY)] * 6,
        out_specs=pl.BlockSpec(memory_space=pltpu.VMEM),
        scratch_shapes=[pltpu.VMEM(array.shape, array.dtype) for array in operands]
        + [pltpu.SemaphoreType.DMA((6,))],
        compiler_params=pltpu.CompilerParams(vmem_limit_bytes=VMEM),
        cost_estimate=pl.CostEstimate(
            flops=20 * tok_dev * width, bytes_accessed=14 * tok_dev * width, transcendentals=0
        ),
    )(*(pltpu.with_memory_space_constraint(array, pltpu.HBM) for array in operands))


def join_kernel(own, other, held, sems):
    half = own.shape[2]
    copies = [
        pltpu.make_async_copy(
            source.at[part], held.at[part, :, pl.ds(h * half, half)], sems.at[h, part]
        )
        for h, source in enumerate((own, other))
        for part in range(3)
    ]
    for copy in copies:
        copy.start()
    for copy in copies:
        copy.wait()


def joined(own, other):
    parts, width, half = own.shape
    return pl.pallas_call(
        join_kernel,
        out_shape=pltpu.VMEM((parts, width, 2 * half), own.dtype),
        in_specs=[pl.BlockSpec(memory_space=pl.ANY)] * 2,
        out_specs=pl.BlockSpec(memory_space=pltpu.VMEM),
        scratch_shapes=[pltpu.SemaphoreType.DMA((2, parts))],
        compiler_params=pltpu.CompilerParams(vmem_limit_bytes=VMEM),
        cost_estimate=pl.CostEstimate(
            flops=0, bytes_accessed=8 * parts * width * half, transcendentals=0
        ),
    )(pltpu.with_memory_space_constraint(own, pltpu.HBM), other)


def expert_kernel(count, expert_count, *refs):
    packs, held, outs = (refs[:count], refs[count], refs[count + 1 : -4])
    both, cotan, slopes, acc = refs[-4:]
    tok_dev = packs[0].shape[0]
    _, width, hidden = held.shape
    rows = count * tok_dev

    def stacked(start, size):
        return jnp.concatenate([p[:, start : start + size].astype(jnp.float32) for p in packs], 0)

    both[:rows, :] = stacked(0, width).astype(jnp.bfloat16)
    both[rows:, :] = stacked(width, width).astype(jnp.bfloat16)
    cotan[...] = stacked(2 * width, width).astype(jnp.bfloat16)
    tail = stacked(3 * width, packs[0].shape[1] - 3 * width)
    mine = lax.axis_index("expert") // 2
    lane = lax.broadcasted_iota(jnp.int32, tail.shape, 1)
    after = 2 * expert_count

    def picked(lanes):
        return jnp.sum(jnp.where(lanes, tail, 0.0), axis=1, keepdims=True)

    gate_row = picked((lane == mine) | (lane == mine + expert_count))
    scale_row = picked((lane >= after) & (lane < after + 3))
    slope_row = picked((lane >= after + 3) & (lane < after + 6))

    def weights(part, start, size):
        return held[part, :, start : start + size]

    block = 256 if hidden % 256 == 0 else 128
    contract = (((1,), (1,)), ((), ()))
    for start in range(0, hidden, block):
        pre_gate = jnp.dot(
            both[...], weights(0, start, block), preferred_element_type=jnp.float32
        )
        pre_up = jnp.dot(both[...], weights(1, start, block), preferred_element_type=jnp.float32)
        back = jnp.dot(cotan[...], weights(2, start, block), preferred_element_type=jnp.float32)
        gate, gate_t = (pre_gate[:rows], pre_gate[rows:])
        up, up_t = (pre_up[:rows], pre_up[rows:])
        sig = jax.nn.sigmoid(gate)
        act = gate * sig
        slope = sig * (1.0 + gate * (1.0 - sig))
        bend = sig * (1.0 - sig) * (2.0 + gate * (1.0 - 2.0 * sig))
        d_gate = (back * slope * up).astype(jnp.bfloat16)
        d_up = (back * act).astype(jnp.bfloat16)
        t_gate = (back * (bend * gate_t * up + slope * up_t)).astype(jnp.bfloat16)
        t_up = (back * slope * gate_t).astype(jnp.bfloat16)
        for n, (own, along) in enumerate(((d_gate, t_gate), (d_up, t_up))):
            slopes[n, :rows, start : start + block] = own
            slopes[n, rows:, start : start + block] = along
    block = 256 if width % 256 == 0 else width
    for start in range(0, width, block):
        acc[:, start : start + block] = sum(
            lax.dot_general(
                slopes[n],
                held[n, start : start + block, :],
                contract,
                preferred_element_type=jnp.float32,
            )
            for n in range(2)
        )
    homes = [out.at[:, pl.ds(at, width + 128)] for out in outs for at in range(0, out.shape[1], width + 128)]
    for n, home in enumerate(homes):
        part = slice(n * tok_dev, (n + 1) * tok_dev)
        later = slice(rows + n * tok_dev, rows + (n + 1) * tok_dev)
        grad, tan = (acc[part] * gate_row[part], acc[later] * gate_row[part])
        scale, slope_r = (scale_row[part], slope_row[part])
        normed = packs[n][:, :width].astype(jnp.float32)
        normed_t = packs[n][:, width : 2 * width].astype(jnp.float32)
        home[:, :width] = (scale * tan + slope_r * grad).astype(home.dtype)
        first = jnp.mean(normed * grad, axis=1, keepdims=True)
        second = jnp.mean(normed * tan + normed_t * grad, axis=1, keepdims=True)
        second = (second - slope_r / scale * first) / scale
        lane = lax.broadcasted_iota(jnp.int32, (tok_dev, 128), 1)
        sums = jnp.where(lane == 0, first / scale, jnp.where(lane == 1, second, 0.0))
        home[:, width:] = sums.astype(home.dtype)


def experts(packs, kinds, held, expert_count):
    count = len(packs)
    tok_dev = packs[0].shape[0]
    _, width, hidden = held.shape
    rows = count * tok_dev
    whole = pl.BlockSpec(memory_space=pltpu.VMEM)
    return pl.pallas_call(
        functools.partial(expert_kernel, count, expert_count),
        out_shape=[jax.ShapeDtypeStruct((tok_dev, n * (width + 128)), kind) for kind, n in kinds],
        in_specs=[whole] * (count + 1),
        out_specs=[whole] * len(kinds),
        scratch_shapes=[
            pltpu.VMEM((2 * rows, width), jnp.bfloat16),
            pltpu.VMEM((rows, width), jnp.bfloat16),
            pltpu.VMEM((2, 2 * rows, hidden), jnp.bfloat16),
            pltpu.VMEM((2 * rows, width), jnp.float32),
        ],
        compiler_params=pltpu.CompilerParams(vmem_limit_bytes=VMEM),
        cost_estimate=pl.CostEstimate(
            flops=2 * 9 * rows * width * hidden,
            bytes_accessed=6 * width * hidden,
            transcendentals=rows * hidden,
        ),
    )(*packs, pltpu.with_memory_space_constraint(held, pltpu.VMEM))


def finish_kernel(tokens, gain, signs, *refs):
    arrived, hvp, quad = (refs[:-2], refs[-2], refs[-1])
    width = tokens.shape[1]
    xf = tokens[...].astype(jnp.float32)
    probe = (2 * signs[...] - 1).astype(jnp.float32)
    scale, along = rms_terms(xf, probe)
    slope_r = -(scale**3) * along
    lanes = arrived[0].shape[1]
    rows = sum(part[:, :lanes].astype(jnp.float32) for part in arrived)
    first = rows[:, width : width + 1]
    second = rows[:, width + 1 : width + 2]
    whole = (
        gain[...] * rows[:, :width]
        - 3.0 * scale**2 * slope_r * first * xf
        - scale**3 * first * probe
        - scale**3 * second * xf
    )
    hvp[...] = whole
    column = jnp.mean(probe * whole, axis=1, keepdims=True)
    tok_dev = column.shape[0]
    quad[...] = jnp.sum(identity(tok_dev) * column, axis=0, keepdims=True)


def moved(rows, turns, flip_x=False, flip_core=False):
    count = lax.axis_size("expert")
    pairs = [
        (i, (i + 4 * turns) % count ^ (2 * flip_x) ^ (1 * flip_core)) for i in range(count)
    ]
    return lax.ppermute(rows, "expert", pairs)


def dense_local(tokens, norm_gain, probe_signs, cotangent, routes, gates, weights):
    tok_dev, width = tokens.shape
    n_exp = lax.axis_size("expert")
    expert_count = n_exp // 2
    pack = packed(tokens, norm_gain, probe_signs, cotangent, routes, gates, expert_count)
    held = joined(weights, moved(weights, 0, flip_core=True))
    same, across = {0: pack}, {}
    same[1] = moved(pack, 1)
    across[0] = moved(pack, 0, flip_x=True)
    same[1] = lax.optimization_barrier((same[1], across[0]))[0]
    same[3] = moved(lax.optimization_barrier((pack, same[1], held))[0], -1)
    same[2] = moved(same[1], 1)
    across[1] = moved(same[1], 0, flip_x=True)
    across[3] = moved(same[3], 0, flip_x=True)
    across[2] = moved(same[2], 0, flip_x=True)
    wide, sent, pair = ((jnp.float32, 1), (jnp.bfloat16, 1), (jnp.bfloat16, 2))
    here = {}
    here[0], here[1], here[2], here[3], there = experts(
        [same[0], same[1], same[2], same[3], across[0], across[1]],
        [wide, wide, sent, sent, pair],
        held,
        expert_count,
    )
    late = lax.optimization_barrier((across[2], across[3], here[1]))[:2]
    far, last = experts(late, [sent, sent], held, expert_count)

    def total(*parts):
        return sum(part.astype(jnp.float32) for part in parts).astype(jnp.bfloat16)

    beside, forward = (moved(there, 0, flip_x=True), moved(here[2], -1))
    kept = lax.optimization_barrier((here[1], far))[0]
    arrived = [
        here[0],
        beside,
        moved(here[3], 1),
        moved(far, 2, flip_x=True),
        moved(last, 1, flip_x=True),
        moved(total(kept, beside[:, kept.shape[1] :], forward), -1),
    ]
    hvp, quad = pl.pallas_call(
        finish_kernel,
        out_shape=[
            jax.ShapeDtypeStruct((tok_dev, width), jnp.float32),
            jax.ShapeDtypeStruct((1, tok_dev), jnp.float32),
        ],
        compiler_params=pltpu.CompilerParams(vmem_limit_bytes=VMEM),
        cost_estimate=pl.CostEstimate(
            flops=40 * tok_dev * width, bytes_accessed=26 * tok_dev * width, transcendentals=0
        ),
    )(tokens, norm_gain.reshape(1, width), probe_signs, *arrived)
    return (hvp, quad.reshape(tok_dev))


def routed_rows(normed, normed_t, cotangent, routes, gates, weights):
    tok_dev, width = normed.shape
    groups_here = routes.shape[0]
    half = routes.shape[2]
    n_exp = lax.axis_size("expert")
    expert_count = n_exp // 2
    cap = capacity(tok_dev, half, expert_count)
    buffer_rows = expert_count * cap
    stack_z, stack_t, stack_c, stack_w = ([], [], [], [])
    for group in range(groups_here):
        target = slot_targets(routes[group], expert_count, cap)
        place = (jnp.arange(buffer_rows, dtype=jnp.int32)[:, None] == target[None, :]).reshape(
            buffer_rows, tok_dev, half
        )
        place_tok = jnp.sum(place.astype(jnp.float32), axis=2).astype(jnp.bfloat16)
        stack_w.append(jnp.sum(place.astype(jnp.float32) * gates[group][None, :, :], axis=2))
        stack_z.append(
            jnp.dot(place_tok, normed, preferred_element_type=jnp.float32).astype(jnp.bfloat16)
        )
        stack_t.append(
            jnp.dot(place_tok, normed_t, preferred_element_type=jnp.float32).astype(jnp.bfloat16)
        )
        stack_c.append(
            jnp.dot(place_tok, cotangent, preferred_element_type=jnp.float32).astype(jnp.bfloat16)
        )
    rows_z = jnp.stack(stack_z, 0)
    rows_t = jnp.stack(stack_t, 0)
    rows_c = jnp.stack(stack_c, 0)
    weighted = jnp.stack(stack_w, 0)

    def arrange(rows):
        shaped = rows.reshape(groups_here, expert_count, 1, cap, width)
        shaped = jnp.broadcast_to(shaped, (groups_here, expert_count, 2, cap, width))
        return jnp.transpose(shaped, (1, 2, 0, 3, 4)).reshape(n_exp, groups_here * cap, width)

    send_z, send_t, send_c = (arrange(rows_z), arrange(rows_t), arrange(rows_c))
    got_z = lax.all_to_all(send_z, "expert", split_axis=0, concat_axis=0, tiled=True)
    got_t = lax.all_to_all(send_t, "expert", split_axis=0, concat_axis=0, tiled=True)
    got_c = lax.all_to_all(send_c, "expert", split_axis=0, concat_axis=0, tiled=True)
    sources, items, cols = got_z.shape
    g_rows, t_rows = expert_terms(
        weights, got_z.reshape(-1, cols), got_t.reshape(-1, cols), got_c.reshape(-1, cols)
    )
    g_rows = g_rows.reshape(sources, items, cols)
    t_rows = t_rows.reshape(sources, items, cols)
    back_g = lax.all_to_all(g_rows, "expert", split_axis=0, concat_axis=0, tiled=True)
    back_t = lax.all_to_all(t_rows, "expert", split_axis=0, concat_axis=0, tiled=True)

    def restore(rows):
        shaped = jnp.sum(rows.reshape(expert_count, 2, groups_here, cap, width), axis=1)
        return jnp.transpose(shaped, (1, 0, 2, 3)).reshape(groups_here, buffer_rows, width)

    back_g = restore(back_g)
    back_t = restore(back_t)
    contract = (((0, 1), (0, 1)), ((), ()))
    grad_z = lax.dot_general(weighted, back_g, contract, precision=lax.Precision.HIGHEST)
    tan_z = lax.dot_general(weighted, back_t, contract, precision=lax.Precision.HIGHEST)
    return (grad_z, tan_z)


def local(tokens, norm_gain, probe_signs, cotangent, routes, gates, expert_weights):
    cap = capacity(tokens.shape[0], routes.shape[2], lax.axis_size("expert") // 2)
    layout = (lax.axis_size("expert"), lax.axis_size("node"))
    if layout == (16, 1) and routes.shape[0] * cap >= tokens.shape[0]:
        return dense_local(
            tokens, norm_gain, probe_signs, cotangent, routes, gates, expert_weights
        )
    xf = tokens.astype(jnp.float32)
    probe = (2 * probe_signs - 1).astype(jnp.float32)
    tok_dev, width = xf.shape
    scale = lax.rsqrt(jnp.mean(xf * xf, axis=1, keepdims=True) + EPS)
    along = jnp.mean(xf * probe, axis=1, keepdims=True)
    normed = (xf * scale * norm_gain).astype(jnp.bfloat16)
    normed_t = (norm_gain * (scale * probe - scale**3 * xf * along)).astype(jnp.bfloat16)
    own_half = lax.all_gather(expert_weights, "node", axis=2, tiled=True)
    grad_z, tan_z = routed_rows(normed, normed_t, cotangent, routes, gates, own_half)
    share = width // lax.axis_size("node")
    start = lax.axis_index("node") * share
    slope_r = -(scale**3) * along
    grad_z, tan_z = lax.psum((grad_z, tan_z), "node")
    lifted = norm_gain * grad_z
    lifted_t = norm_gain * tan_z
    first = jnp.mean(xf * lifted, axis=1, keepdims=True)
    second = jnp.mean(xf * lifted_t, axis=1, keepdims=True)
    third = jnp.mean(probe * lifted, axis=1, keepdims=True)
    whole_hvp = (
        scale * lifted_t
        + slope_r * lifted
        - 3.0 * scale**2 * slope_r * first * xf
        - scale**3 * first * probe
        - scale**3 * (second + third) * xf
    )
    quad = jnp.mean(probe * whole_hvp, axis=1)
    hvp = lax.dynamic_slice_in_dim(whole_hvp, start, share, 1)
    return (hvp, quad)


def solution(mesh):
    placed = (
        P(("groups", "expert"), None),
        P(),
        P(("groups", "expert"), None),
        P(("groups", "expert"), None),
        P("node", ("groups", "expert"), None),
        P("node", ("groups", "expert"), None),
        P(None, None, ("expert", "node")),
    )
    return jax.shard_map(
        local,
        mesh=mesh,
        in_specs=placed,
        out_specs=(P(("groups", "expert"), "node"), P(("groups", "expert"))),
        check_vma=False,
    )
```

```python
import functools

import jax
import jax.numpy as jnp
from jax import lax
from jax.experimental import pallas as pl
from jax.experimental.pallas import tpu as pltpu
from jax.sharding import PartitionSpec as P

EPS = 1e-06
VMEM = 24 * 1024 * 1024


def expert_terms(weights, rows, rows_t, cotan):
    count = rows.shape[0]
    both = jnp.concatenate([rows, rows_t], 0)
    pre_gate = jnp.dot(both, weights[0], preferred_element_type=jnp.float32)
    pre_up = jnp.dot(both, weights[1], preferred_element_type=jnp.float32)
    gate, gate_t = (pre_gate[:count], pre_gate[count:])
    up, up_t = (pre_up[:count], pre_up[count:])
    back = jnp.dot(cotan, weights[2], preferred_element_type=jnp.float32)
    sig = jax.nn.sigmoid(gate)
    act = gate * sig
    slope = sig * (1.0 + gate * (1.0 - sig))
    bend = sig * (1.0 - sig) * (2.0 + gate * (1.0 - 2.0 * sig))
    d_gate = (back * slope * up).astype(jnp.bfloat16)
    d_up = (back * act).astype(jnp.bfloat16)
    t_gate = (back * (bend * gate_t * up + slope * up_t)).astype(jnp.bfloat16)
    t_up = (back * slope * gate_t).astype(jnp.bfloat16)
    contract = (((1,), (1,)), ((), ()))
    lhs_gate = jnp.concatenate([d_gate, t_gate], 0)
    lhs_up = jnp.concatenate([d_up, t_up], 0)
    total = lax.dot_general(lhs_gate, weights[0], contract, preferred_element_type=jnp.float32)
    total = total + lax.dot_general(
        lhs_up, weights[1], contract, preferred_element_type=jnp.float32
    )
    return (total[:count], total[count:])


def slot_targets(route_ids, expert_count, capacity):
    flat = route_ids.reshape(-1)
    count = flat.shape[0]
    onehot = (flat[:, None] == jnp.arange(expert_count, dtype=jnp.int32)[None, :]).astype(
        jnp.float32
    )
    lower = (jnp.arange(count)[:, None] > jnp.arange(count)[None, :]).astype(jnp.float32)
    before = jnp.dot(lower, onehot, precision=lax.Precision.HIGHEST)
    rank = jnp.sum(before * onehot, axis=1).astype(jnp.int32)
    return flat * capacity + rank


def capacity(tok_dev, half, expert_count):
    return min(2 * ((2 * tok_dev * half + 3 * expert_count - 1) // (3 * expert_count)), tok_dev)


def rms_terms(xf, probe):
    scale = lax.rsqrt(jnp.mean(xf * xf, axis=1, keepdims=True) + EPS)
    along = jnp.mean(xf * probe, axis=1, keepdims=True)
    return scale, along


def pack_kernel(expert_count, *refs):
    sources, pack, held, sems = (refs[:6], refs[6], refs[7:13], refs[13])
    copies = [
        pltpu.make_async_copy(source, target, sems.at[n])
        for n, (source, target) in enumerate(zip(sources, held))
    ]
    for copy in copies:
        copy.start()
    for copy in copies:
        copy.wait()
    tokens, gain, signs, cotangent, routes, gates = held
    width = tokens.shape[1]
    xf = tokens[...].astype(jnp.float32)
    probe = (2 * signs[...] - 1).astype(jnp.float32)
    scale, along = rms_terms(xf, probe)
    pack[:, :width] = (xf * scale * gain[...]).astype(jnp.bfloat16)
    tangent = gain[...] * (scale * probe - scale**3 * xf * along)
    pack[:, width : 2 * width] = tangent.astype(jnp.bfloat16)
    pack[:, 2 * width : 3 * width] = cotangent[...]
    tok_dev, lanes = (tokens.shape[0], pack.shape[1] - 3 * width)
    lane = lax.broadcasted_iota(jnp.int32, (lanes, tok_dev), 0)
    expert = lax.rem(lane, expert_count)
    gate = jnp.zeros(lane.shape, jnp.float32)
    for group in range(routes.shape[0]):
        for slot in range(routes.shape[1]):
            named = routes[group, slot : slot + 1, :] == expert
            gate = gate + jnp.where(named, gates[group, slot : slot + 1, :], 0.0)
    high = gate.astype(jnp.bfloat16).astype(jnp.float32)
    tail = jnp.where(lane < expert_count, high, gate - high)
    tail = jnp.where(lane < 2 * expert_count, tail, 0.0).astype(jnp.bfloat16)
    turned = lax.dot_general(
        identity(tok_dev).astype(jnp.bfloat16),
        tail,
        (((1,), (1,)), ((), ())),
        preferred_element_type=jnp.float32,
    )
    lane = lax.broadcasted_iota(jnp.int32, (tok_dev, lanes), 1)
    place = 2 * expert_count
    for number in (scale, -(scale**3) * along):
        for _ in range(3):
            addend = number.astype(jnp.bfloat16).astype(jnp.float32)
            turned = jnp.where(lane == place, addend, turned)
            number = number - addend
            place += 1
    pack[:, 3 * width :] = turned.astype(jnp.bfloat16)


def identity(size):
    rows = lax.broadcasted_iota(jnp.int32, (size, size), 0)
    return (rows == lax.broadcasted_iota(jnp.int32, (size, size), 1)).astype(jnp.float32)


def packed(tokens, norm_gain, probe_signs, cotangent, routes, gates, expert_count):
    tok_dev, width = tokens.shape
    tail = -(-(2 * expert_count + 6) // 128) * 128
    token_minor = (0, 2, 1)
    operands = (
        tokens,
        norm_gain.reshape(1, width),
        probe_signs,
        cotangent,
        jnp.transpose(routes, token_minor),
        jnp.transpose(gates, token_minor),
    )
    return pl.pallas_call(
        functools.partial(pack_kernel, expert_count),
        out_shape=jax.ShapeDtypeStruct((tok_dev, 3 * width + tail), jnp.bfloat16),
        in_specs=[pl.BlockSpec(memory_space=pl.ANY)] * 6,
        out_specs=pl.BlockSpec(memory_space=pltpu.VMEM),
        scratch_shapes=[pltpu.VMEM(array.shape, array.dtype) for array in operands]
        + [pltpu.SemaphoreType.DMA((6,))],
        compiler_params=pltpu.CompilerParams(vmem_limit_bytes=VMEM),
        cost_estimate=pl.CostEstimate(
            flops=20 * tok_dev * width, bytes_accessed=14 * tok_dev * width, transcendentals=0
        ),
    )(*(pltpu.with_memory_space_constraint(array, pltpu.HBM) for array in operands))


def join_kernel(own, other, held, sems):
    half = own.shape[2]
    copies = [
        pltpu.make_async_copy(
            source.at[part], held.at[part, :, pl.ds(h * half, half)], sems.at[h, part]
        )
        for h, source in enumerate((own, other))
        for part in range(3)
    ]
    for copy in copies:
        copy.start()
    for copy in copies:
        copy.wait()


def joined(own, other):
    parts, width, half = own.shape
    return pl.pallas_call(
        join_kernel,
        out_shape=pltpu.VMEM((parts, width, 2 * half), own.dtype),
        in_specs=[pl.BlockSpec(memory_space=pl.ANY)] * 2,
        out_specs=pl.BlockSpec(memory_space=pltpu.VMEM),
        scratch_shapes=[pltpu.SemaphoreType.DMA((2, parts))],
        compiler_params=pltpu.CompilerParams(vmem_limit_bytes=VMEM),
        cost_estimate=pl.CostEstimate(
            flops=0, bytes_accessed=8 * parts * width * half, transcendentals=0
        ),
    )(pltpu.with_memory_space_constraint(own, pltpu.HBM), other)


def expert_kernel(count, expert_count, *refs):
    packs, held, outs = (refs[:count], refs[count], refs[count + 1 : -4])
    both, cotan, slopes, acc = refs[-4:]
    tok_dev = packs[0].shape[0]
    _, width, hidden = held.shape
    rows = count * tok_dev

    def stacked(start, size):
        return jnp.concatenate([p[:, start : start + size].astype(jnp.float32) for p in packs], 0)

    both[:rows, :] = stacked(0, width).astype(jnp.bfloat16)
    both[rows:, :] = stacked(width, width).astype(jnp.bfloat16)
    cotan[...] = stacked(2 * width, width).astype(jnp.bfloat16)
    tail = stacked(3 * width, packs[0].shape[1] - 3 * width)
    mine = lax.axis_index("expert") // 2
    lane = lax.broadcasted_iota(jnp.int32, tail.shape, 1)
    after = 2 * expert_count

    def picked(lanes):
        return jnp.sum(jnp.where(lanes, tail, 0.0), axis=1, keepdims=True)

    gate_row = picked((lane == mine) | (lane == mine + expert_count))
    scale_row = picked((lane >= after) & (lane < after + 3))
    slope_row = picked((lane >= after + 3) & (lane < after + 6))

    def weights(part, start, size):
        return held[part, :, start : start + size]

    block = 256 if hidden % 256 == 0 else 128
    contract = (((1,), (1,)), ((), ()))
    for start in range(0, hidden, block):
        pre_gate = jnp.dot(
            both[...], weights(0, start, block), preferred_element_type=jnp.float32
        )
        pre_up = jnp.dot(both[...], weights(1, start, block), preferred_element_type=jnp.float32)
        back = jnp.dot(cotan[...], weights(2, start, block), preferred_element_type=jnp.float32)
        gate, gate_t = (pre_gate[:rows], pre_gate[rows:])
        up, up_t = (pre_up[:rows], pre_up[rows:])
        sig = jax.nn.sigmoid(gate)
        act = gate * sig
        slope = sig * (1.0 + gate * (1.0 - sig))
        bend = sig * (1.0 - sig) * (2.0 + gate * (1.0 - 2.0 * sig))
        d_gate = (back * slope * up).astype(jnp.bfloat16)
        d_up = (back * act).astype(jnp.bfloat16)
        t_gate = (back * (bend * gate_t * up + slope * up_t)).astype(jnp.bfloat16)
        t_up = (back * slope * gate_t).astype(jnp.bfloat16)
        for n, (own, along) in enumerate(((d_gate, t_gate), (d_up, t_up))):
            slopes[n, :rows, start : start + block] = own
            slopes[n, rows:, start : start + block] = along
    block = 256 if width % 256 == 0 else width
    for start in range(0, width, block):
        acc[:, start : start + block] = sum(
            lax.dot_general(
                slopes[n],
                held[n, start : start + block, :],
                contract,
                preferred_element_type=jnp.float32,
            )
            for n in range(2)
        )
    homes = [out.at[:, pl.ds(at, width + 128)] for out in outs for at in range(0, out.shape[1], width + 128)]
    for n, home in enumerate(homes):
        part = slice(n * tok_dev, (n + 1) * tok_dev)
        later = slice(rows + n * tok_dev, rows + (n + 1) * tok_dev)
        grad, tan = (acc[part] * gate_row[part], acc[later] * gate_row[part])
        scale, slope_r = (scale_row[part], slope_row[part])
        normed = packs[n][:, :width].astype(jnp.float32)
        normed_t = packs[n][:, width : 2 * width].astype(jnp.float32)
        home[:, :width] = (scale * tan + slope_r * grad).astype(home.dtype)
        first = jnp.mean(normed * grad, axis=1, keepdims=True)
        second = jnp.mean(normed * tan + normed_t * grad, axis=1, keepdims=True)
        second = (second - slope_r / scale * first) / scale
        lane = lax.broadcasted_iota(jnp.int32, (tok_dev, 128), 1)
        sums = jnp.where(lane == 0, first / scale, jnp.where(lane == 1, second, 0.0))
        home[:, width:] = sums.astype(home.dtype)


def experts(packs, kinds, held, expert_count):
    count = len(packs)
    tok_dev = packs[0].shape[0]
    _, width, hidden = held.shape
    rows = count * tok_dev
    whole = pl.BlockSpec(memory_space=pltpu.VMEM)
    return pl.pallas_call(
        functools.partial(expert_kernel, count, expert_count),
        out_shape=[jax.ShapeDtypeStruct((tok_dev, n * (width + 128)), kind) for kind, n in kinds],
        in_specs=[whole] * (count + 1),
        out_specs=[whole] * len(kinds),
        scratch_shapes=[
            pltpu.VMEM((2 * rows, width), jnp.bfloat16),
            pltpu.VMEM((rows, width), jnp.bfloat16),
            pltpu.VMEM((2, 2 * rows, hidden), jnp.bfloat16),
            pltpu.VMEM((2 * rows, width), jnp.float32),
        ],
        compiler_params=pltpu.CompilerParams(vmem_limit_bytes=VMEM),
        cost_estimate=pl.CostEstimate(
            flops=2 * 9 * rows * width * hidden,
            bytes_accessed=6 * width * hidden,
            transcendentals=rows * hidden,
        ),
    )(*packs, pltpu.with_memory_space_constraint(held, pltpu.VMEM))


def finish_kernel(tokens, gain, signs, *refs):
    arrived, hvp, quad = (refs[:-2], refs[-2], refs[-1])
    width = tokens.shape[1]
    xf = tokens[...].astype(jnp.float32)
    probe = (2 * signs[...] - 1).astype(jnp.float32)
    scale, along = rms_terms(xf, probe)
    slope_r = -(scale**3) * along
    lanes = arrived[0].shape[1]
    rows = sum(part[:, :lanes].astype(jnp.float32) for part in arrived)
    first = rows[:, width : width + 1]
    second = rows[:, width + 1 : width + 2]
    whole = (
        gain[...] * rows[:, :width]
        - 3.0 * scale**2 * slope_r * first * xf
        - scale**3 * first * probe
        - scale**3 * second * xf
    )
    hvp[...] = whole
    column = jnp.mean(probe * whole, axis=1, keepdims=True)
    tok_dev = column.shape[0]
    quad[...] = jnp.sum(identity(tok_dev) * column, axis=0, keepdims=True)


def moved(rows, turns, flip_x=False, flip_core=False):
    count = lax.axis_size("expert")
    pairs = [
        (i, (i + 4 * turns) % count ^ (2 * flip_x) ^ (1 * flip_core)) for i in range(count)
    ]
    return lax.ppermute(rows, "expert", pairs)


def dense_local(tokens, norm_gain, probe_signs, cotangent, routes, gates, weights):
    tok_dev, width = tokens.shape
    n_exp = lax.axis_size("expert")
    expert_count = n_exp // 2
    pack = packed(tokens, norm_gain, probe_signs, cotangent, routes, gates, expert_count)
    held = joined(weights, moved(weights, 0, flip_core=True))
    same, across = {0: pack}, {}
    same[1] = moved(pack, 1)
    across[0] = moved(pack, 0, flip_x=True)
    same[1] = lax.optimization_barrier((same[1], across[0]))[0]
    same[3] = moved(lax.optimization_barrier((pack, same[1]))[0], -1)
    same[2] = moved(same[1], 1)
    same[2] = lax.optimization_barrier((same[2], held))[0]
    across[1] = moved(same[1], 0, flip_x=True)
    across[3] = moved(same[3], 0, flip_x=True)
    across[2] = moved(same[2], 0, flip_x=True)
    wide, sent, pair = ((jnp.float32, 1), (jnp.bfloat16, 1), (jnp.bfloat16, 2))
    here = {}
    here[0], here[1], here[2], here[3], there = experts(
        [same[0], same[1], same[2], same[3], across[0], across[1]],
        [wide, wide, sent, sent, pair],
        held,
        expert_count,
    )
    late = lax.optimization_barrier((across[2], across[3], here[1]))[:2]
    far, last = experts(late, [sent, sent], held, expert_count)

    def total(*parts):
        return sum(part.astype(jnp.float32) for part in parts).astype(jnp.bfloat16)

    beside, forward = (moved(there, 0, flip_x=True), moved(here[2], -1))
    kept = lax.optimization_barrier((here[1], far))[0]
    arrived = [
        here[0],
        beside,
        moved(here[3], 1),
        moved(far, 2, flip_x=True),
        moved(last, 1, flip_x=True),
        moved(total(kept, beside[:, kept.shape[1] :], forward), -1),
    ]
    hvp, quad = pl.pallas_call(
        finish_kernel,
        out_shape=[
            jax.ShapeDtypeStruct((tok_dev, width), jnp.float32),
            jax.ShapeDtypeStruct((1, tok_dev), jnp.float32),
        ],
        compiler_params=pltpu.CompilerParams(vmem_limit_bytes=VMEM),
        cost_estimate=pl.CostEstimate(
            flops=40 * tok_dev * width, bytes_accessed=26 * tok_dev * width, transcendentals=0
        ),
    )(tokens, norm_gain.reshape(1, width), probe_signs, *arrived)
    return (hvp, quad.reshape(tok_dev))


def routed_rows(normed, normed_t, cotangent, routes, gates, weights):
    tok_dev, width = normed.shape
    groups_here = routes.shape[0]
    half = routes.shape[2]
    n_exp = lax.axis_size("expert")
    expert_count = n_exp // 2
    cap = capacity(tok_dev, half, expert_count)
    buffer_rows = expert_count * cap
    stack_z, stack_t, stack_c, stack_w = ([], [], [], [])
    for group in range(groups_here):
        target = slot_targets(routes[group], expert_count, cap)
        place = (jnp.arange(buffer_rows, dtype=jnp.int32)[:, None] == target[None, :]).reshape(
            buffer_rows, tok_dev, half
        )
        place_tok = jnp.sum(place.astype(jnp.float32), axis=2).astype(jnp.bfloat16)
        stack_w.append(jnp.sum(place.astype(jnp.float32) * gates[group][None, :, :], axis=2))
        stack_z.append(
            jnp.dot(place_tok, normed, preferred_element_type=jnp.float32).astype(jnp.bfloat16)
        )
        stack_t.append(
            jnp.dot(place_tok, normed_t, preferred_element_type=jnp.float32).astype(jnp.bfloat16)
        )
        stack_c.append(
            jnp.dot(place_tok, cotangent, preferred_element_type=jnp.float32).astype(jnp.bfloat16)
        )
    rows_z = jnp.stack(stack_z, 0)
    rows_t = jnp.stack(stack_t, 0)
    rows_c = jnp.stack(stack_c, 0)
    weighted = jnp.stack(stack_w, 0)

    def arrange(rows):
        shaped = rows.reshape(groups_here, expert_count, 1, cap, width)
        shaped = jnp.broadcast_to(shaped, (groups_here, expert_count, 2, cap, width))
        return jnp.transpose(shaped, (1, 2, 0, 3, 4)).reshape(n_exp, groups_here * cap, width)

    send_z, send_t, send_c = (arrange(rows_z), arrange(rows_t), arrange(rows_c))
    got_z = lax.all_to_all(send_z, "expert", split_axis=0, concat_axis=0, tiled=True)
    got_t = lax.all_to_all(send_t, "expert", split_axis=0, concat_axis=0, tiled=True)
    got_c = lax.all_to_all(send_c, "expert", split_axis=0, concat_axis=0, tiled=True)
    sources, items, cols = got_z.shape
    g_rows, t_rows = expert_terms(
        weights, got_z.reshape(-1, cols), got_t.reshape(-1, cols), got_c.reshape(-1, cols)
    )
    g_rows = g_rows.reshape(sources, items, cols)
    t_rows = t_rows.reshape(sources, items, cols)
    back_g = lax.all_to_all(g_rows, "expert", split_axis=0, concat_axis=0, tiled=True)
    back_t = lax.all_to_all(t_rows, "expert", split_axis=0, concat_axis=0, tiled=True)

    def restore(rows):
        shaped = jnp.sum(rows.reshape(expert_count, 2, groups_here, cap, width), axis=1)
        return jnp.transpose(shaped, (1, 0, 2, 3)).reshape(groups_here, buffer_rows, width)

    back_g = restore(back_g)
    back_t = restore(back_t)
    contract = (((0, 1), (0, 1)), ((), ()))
    grad_z = lax.dot_general(weighted, back_g, contract, precision=lax.Precision.HIGHEST)
    tan_z = lax.dot_general(weighted, back_t, contract, precision=lax.Precision.HIGHEST)
    return (grad_z, tan_z)


def local(tokens, norm_gain, probe_signs, cotangent, routes, gates, expert_weights):
    cap = capacity(tokens.shape[0], routes.shape[2], lax.axis_size("expert") // 2)
    layout = (lax.axis_size("expert"), lax.axis_size("node"))
    if layout == (16, 1) and routes.shape[0] * cap >= tokens.shape[0]:
        return dense_local(
            tokens, norm_gain, probe_signs, cotangent, routes, gates, expert_weights
        )
    xf = tokens.astype(jnp.float32)
    probe = (2 * probe_signs - 1).astype(jnp.float32)
    tok_dev, width = xf.shape
    scale = lax.rsqrt(jnp.mean(xf * xf, axis=1, keepdims=True) + EPS)
    along = jnp.mean(xf * probe, axis=1, keepdims=True)
    normed = (xf * scale * norm_gain).astype(jnp.bfloat16)
    normed_t = (norm_gain * (scale * probe - scale**3 * xf * along)).astype(jnp.bfloat16)
    own_half = lax.all_gather(expert_weights, "node", axis=2, tiled=True)
    grad_z, tan_z = routed_rows(normed, normed_t, cotangent, routes, gates, own_half)
    share = width // lax.axis_size("node")
    start = lax.axis_index("node") * share
    slope_r = -(scale**3) * along
    grad_z, tan_z = lax.psum((grad_z, tan_z), "node")
    lifted = norm_gain * grad_z
    lifted_t = norm_gain * tan_z
    first = jnp.mean(xf * lifted, axis=1, keepdims=True)
    second = jnp.mean(xf * lifted_t, axis=1, keepdims=True)
    third = jnp.mean(probe * lifted, axis=1, keepdims=True)
    whole_hvp = (
        scale * lifted_t
        + slope_r * lifted
        - 3.0 * scale**2 * slope_r * first * xf
        - scale**3 * first * probe
        - scale**3 * (second + third) * xf
    )
    quad = jnp.mean(probe * whole_hvp, axis=1)
    hvp = lax.dynamic_slice_in_dim(whole_hvp, start, share, 1)
    return (hvp, quad)


def solution(mesh):
    placed = (
        P(("groups", "expert"), None),
        P(),
        P(("groups", "expert"), None),
        P(("groups", "expert"), None),
        P("node", ("groups", "expert"), None),
        P("node", ("groups", "expert"), None),
        P(None, None, ("expert", "node")),
    )
    return jax.shard_map(
        local,
        mesh=mesh,
        in_specs=placed,
        out_specs=(P(("groups", "expert"), "node"), P(("groups", "expert"))),
        check_vma=False,
    )
```

```python
import functools

import jax
import jax.numpy as jnp
from jax import lax
from jax.experimental import pallas as pl
from jax.experimental.pallas import tpu as pltpu
from jax.sharding import PartitionSpec as P

EPS = 1e-06
VMEM = 24 * 1024 * 1024


def expert_terms(weights, rows, rows_t, cotan):
    count = rows.shape[0]
    both = jnp.concatenate([rows, rows_t], 0)
    pre_gate = jnp.dot(both, weights[0], preferred_element_type=jnp.float32)
    pre_up = jnp.dot(both, weights[1], preferred_element_type=jnp.float32)
    gate, gate_t = (pre_gate[:count], pre_gate[count:])
    up, up_t = (pre_up[:count], pre_up[count:])
    back = jnp.dot(cotan, weights[2], preferred_element_type=jnp.float32)
    sig = jax.nn.sigmoid(gate)
    act = gate * sig
    slope = sig * (1.0 + gate * (1.0 - sig))
    bend = sig * (1.0 - sig) * (2.0 + gate * (1.0 - 2.0 * sig))
    d_gate = (back * slope * up).astype(jnp.bfloat16)
    d_up = (back * act).astype(jnp.bfloat16)
    t_gate = (back * (bend * gate_t * up + slope * up_t)).astype(jnp.bfloat16)
    t_up = (back * slope * gate_t).astype(jnp.bfloat16)
    contract = (((1,), (1,)), ((), ()))
    lhs_gate = jnp.concatenate([d_gate, t_gate], 0)
    lhs_up = jnp.concatenate([d_up, t_up], 0)
    total = lax.dot_general(lhs_gate, weights[0], contract, preferred_element_type=jnp.float32)
    total = total + lax.dot_general(
        lhs_up, weights[1], contract, preferred_element_type=jnp.float32
    )
    return (total[:count], total[count:])


def slot_targets(route_ids, expert_count, capacity):
    flat = route_ids.reshape(-1)
    count = flat.shape[0]
    onehot = (flat[:, None] == jnp.arange(expert_count, dtype=jnp.int32)[None, :]).astype(
        jnp.float32
    )
    lower = (jnp.arange(count)[:, None] > jnp.arange(count)[None, :]).astype(jnp.float32)
    before = jnp.dot(lower, onehot, precision=lax.Precision.HIGHEST)
    rank = jnp.sum(before * onehot, axis=1).astype(jnp.int32)
    return flat * capacity + rank


def capacity(tok_dev, half, expert_count):
    return min(2 * ((2 * tok_dev * half + 3 * expert_count - 1) // (3 * expert_count)), tok_dev)


def rms_terms(xf, probe):
    scale = lax.rsqrt(jnp.mean(xf * xf, axis=1, keepdims=True) + EPS)
    along = jnp.mean(xf * probe, axis=1, keepdims=True)
    return scale, along


def pack_kernel(expert_count, *refs):
    sources, pack, held, sems = (refs[:6], refs[6], refs[7:13], refs[13])
    copies = [
        pltpu.make_async_copy(source, target, sems.at[n])
        for n, (source, target) in enumerate(zip(sources, held))
    ]
    for copy in copies:
        copy.start()
    for copy in copies:
        copy.wait()
    tokens, gain, signs, cotangent, routes, gates = held
    width = tokens.shape[1]
    xf = tokens[...].astype(jnp.float32)
    probe = (2 * signs[...] - 1).astype(jnp.float32)
    scale, along = rms_terms(xf, probe)
    pack[:, :width] = (xf * scale * gain[...]).astype(jnp.bfloat16)
    tangent = gain[...] * (scale * probe - scale**3 * xf * along)
    pack[:, width : 2 * width] = tangent.astype(jnp.bfloat16)
    pack[:, 2 * width : 3 * width] = cotangent[...]
    tok_dev, lanes = (tokens.shape[0], pack.shape[1] - 3 * width)
    lane = lax.broadcasted_iota(jnp.int32, (lanes, tok_dev), 0)
    expert = lax.rem(lane, expert_count)
    gate = jnp.zeros(lane.shape, jnp.float32)
    for group in range(routes.shape[0]):
        for slot in range(routes.shape[1]):
            named = routes[group, slot : slot + 1, :] == expert
            gate = gate + jnp.where(named, gates[group, slot : slot + 1, :], 0.0)
    high = gate.astype(jnp.bfloat16).astype(jnp.float32)
    tail = jnp.where(lane < expert_count, high, gate - high)
    tail = jnp.where(lane < 2 * expert_count, tail, 0.0).astype(jnp.bfloat16)
    turned = lax.dot_general(
        identity(tok_dev).astype(jnp.bfloat16),
        tail,
        (((1,), (1,)), ((), ())),
        preferred_element_type=jnp.float32,
    )
    lane = lax.broadcasted_iota(jnp.int32, (tok_dev, lanes), 1)
    place = 2 * expert_count
    for number in (scale, -(scale**3) * along):
        for _ in range(3):
            addend = number.astype(jnp.bfloat16).astype(jnp.float32)
            turned = jnp.where(lane == place, addend, turned)
            number = number - addend
            place += 1
    pack[:, 3 * width :] = turned.astype(jnp.bfloat16)


def identity(size):
    rows = lax.broadcasted_iota(jnp.int32, (size, size), 0)
    return (rows == lax.broadcasted_iota(jnp.int32, (size, size), 1)).astype(jnp.float32)


def packed(tokens, norm_gain, probe_signs, cotangent, routes, gates, expert_count):
    tok_dev, width = tokens.shape
    tail = -(-(2 * expert_count + 6) // 128) * 128
    token_minor = (0, 2, 1)
    operands = (
        tokens,
        norm_gain.reshape(1, width),
        probe_signs,
        cotangent,
        jnp.transpose(routes, token_minor),
        jnp.transpose(gates, token_minor),
    )
    return pl.pallas_call(
        functools.partial(pack_kernel, expert_count),
        out_shape=jax.ShapeDtypeStruct((tok_dev, 3 * width + tail), jnp.bfloat16),
        in_specs=[pl.BlockSpec(memory_space=pl.ANY)] * 6,
        out_specs=pl.BlockSpec(memory_space=pltpu.VMEM),
        scratch_shapes=[pltpu.VMEM(array.shape, array.dtype) for array in operands]
        + [pltpu.SemaphoreType.DMA((6,))],
        compiler_params=pltpu.CompilerParams(vmem_limit_bytes=VMEM),
        cost_estimate=pl.CostEstimate(
            flops=20 * tok_dev * width, bytes_accessed=14 * tok_dev * width, transcendentals=0
        ),
    )(*(pltpu.with_memory_space_constraint(array, pltpu.HBM) for array in operands))


def join_kernel(own, other, held, sems):
    half = own.shape[2]
    copies = [
        pltpu.make_async_copy(
            source.at[part], held.at[part, :, pl.ds(h * half, half)], sems.at[h, part]
        )
        for h, source in enumerate((own, other))
        for part in range(3)
    ]
    for copy in copies:
        copy.start()
    for copy in copies:
        copy.wait()


def joined(own, other):
    parts, width, half = own.shape
    return pl.pallas_call(
        join_kernel,
        out_shape=pltpu.VMEM((parts, width, 2 * half), own.dtype),
        in_specs=[pl.BlockSpec(memory_space=pl.ANY)] * 2,
        out_specs=pl.BlockSpec(memory_space=pltpu.VMEM),
        scratch_shapes=[pltpu.SemaphoreType.DMA((2, parts))],
        compiler_params=pltpu.CompilerParams(vmem_limit_bytes=VMEM),
        cost_estimate=pl.CostEstimate(
            flops=0, bytes_accessed=8 * parts * width * half, transcendentals=0
        ),
    )(pltpu.with_memory_space_constraint(own, pltpu.HBM), other)


def expert_kernel(count, expert_count, *refs):
    packs, held, outs = (refs[:count], refs[count], refs[count + 1 : -4])
    both, cotan, slopes, acc = refs[-4:]
    tok_dev = packs[0].shape[0]
    _, width, hidden = held.shape
    rows = count * tok_dev

    def stacked(start, size):
        return jnp.concatenate([p[:, start : start + size].astype(jnp.float32) for p in packs], 0)

    both[:rows, :] = stacked(0, width).astype(jnp.bfloat16)
    both[rows:, :] = stacked(width, width).astype(jnp.bfloat16)
    cotan[...] = stacked(2 * width, width).astype(jnp.bfloat16)
    tail = stacked(3 * width, packs[0].shape[1] - 3 * width)
    mine = lax.axis_index("expert") // 2
    lane = lax.broadcasted_iota(jnp.int32, tail.shape, 1)
    after = 2 * expert_count

    def picked(lanes):
        return jnp.sum(jnp.where(lanes, tail, 0.0), axis=1, keepdims=True)

    gate_row = picked((lane == mine) | (lane == mine + expert_count))
    scale_row = picked((lane >= after) & (lane < after + 3))
    slope_row = picked((lane >= after + 3) & (lane < after + 6))

    def weights(part, start, size):
        return held[part, :, start : start + size]

    block = 256 if hidden % 256 == 0 else 128
    contract = (((1,), (1,)), ((), ()))
    for start in range(0, hidden, block):
        pre_gate = jnp.dot(
            both[...], weights(0, start, block), preferred_element_type=jnp.float32
        )
        pre_up = jnp.dot(both[...], weights(1, start, block), preferred_element_type=jnp.float32)
        back = jnp.dot(cotan[...], weights(2, start, block), preferred_element_type=jnp.float32)
        gate, gate_t = (pre_gate[:rows], pre_gate[rows:])
        up, up_t = (pre_up[:rows], pre_up[rows:])
        sig = jax.nn.sigmoid(gate)
        act = gate * sig
        slope = sig * (1.0 + gate * (1.0 - sig))
        bend = sig * (1.0 - sig) * (2.0 + gate * (1.0 - 2.0 * sig))
        d_gate = (back * slope * up).astype(jnp.bfloat16)
        d_up = (back * act).astype(jnp.bfloat16)
        t_gate = (back * (bend * gate_t * up + slope * up_t)).astype(jnp.bfloat16)
        t_up = (back * slope * gate_t).astype(jnp.bfloat16)
        for n, (own, along) in enumerate(((d_gate, t_gate), (d_up, t_up))):
            slopes[n, :rows, start : start + block] = own
            slopes[n, rows:, start : start + block] = along
    block = 256 if width % 256 == 0 else width
    for start in range(0, width, block):
        acc[:, start : start + block] = sum(
            lax.dot_general(
                slopes[n],
                held[n, start : start + block, :],
                contract,
                preferred_element_type=jnp.float32,
            )
            for n in range(2)
        )
    homes = [out.at[:, pl.ds(at, width + 128)] for out in outs for at in range(0, out.shape[1], width + 128)]
    for n, home in enumerate(homes):
        part = slice(n * tok_dev, (n + 1) * tok_dev)
        later = slice(rows + n * tok_dev, rows + (n + 1) * tok_dev)
        grad, tan = (acc[part] * gate_row[part], acc[later] * gate_row[part])
        scale, slope_r = (scale_row[part], slope_row[part])
        normed = packs[n][:, :width].astype(jnp.float32)
        normed_t = packs[n][:, width : 2 * width].astype(jnp.float32)
        home[:, :width] = (scale * tan + slope_r * grad).astype(home.dtype)
        first = jnp.mean(normed * grad, axis=1, keepdims=True)
        second = jnp.mean(normed * tan + normed_t * grad, axis=1, keepdims=True)
        second = (second - slope_r / scale * first) / scale
        lane = lax.broadcasted_iota(jnp.int32, (tok_dev, 128), 1)
        sums = jnp.where(lane == 0, first / scale, jnp.where(lane == 1, second, 0.0))
        home[:, width:] = sums.astype(home.dtype)


def experts(packs, kinds, held, expert_count):
    count = len(packs)
    tok_dev = packs[0].shape[0]
    _, width, hidden = held.shape
    rows = count * tok_dev
    whole = pl.BlockSpec(memory_space=pltpu.VMEM)
    return pl.pallas_call(
        functools.partial(expert_kernel, count, expert_count),
        out_shape=[jax.ShapeDtypeStruct((tok_dev, n * (width + 128)), kind) for kind, n in kinds],
        in_specs=[whole] * (count + 1),
        out_specs=[whole] * len(kinds),
        scratch_shapes=[
            pltpu.VMEM((2 * rows, width), jnp.bfloat16),
            pltpu.VMEM((rows, width), jnp.bfloat16),
            pltpu.VMEM((2, 2 * rows, hidden), jnp.bfloat16),
            pltpu.VMEM((2 * rows, width), jnp.float32),
        ],
        compiler_params=pltpu.CompilerParams(vmem_limit_bytes=VMEM),
        cost_estimate=pl.CostEstimate(
            flops=2 * 9 * rows * width * hidden,
            bytes_accessed=6 * width * hidden,
            transcendentals=rows * hidden,
        ),
    )(*packs, pltpu.with_memory_space_constraint(held, pltpu.VMEM))


def finish_kernel(tokens, gain, signs, *refs):
    arrived, hvp, quad = (refs[:-2], refs[-2], refs[-1])
    width = tokens.shape[1]
    xf = tokens[...].astype(jnp.float32)
    probe = (2 * signs[...] - 1).astype(jnp.float32)
    scale, along = rms_terms(xf, probe)
    slope_r = -(scale**3) * along
    lanes = arrived[0].shape[1]
    rows = sum(part[:, :lanes].astype(jnp.float32) for part in arrived)
    first = rows[:, width : width + 1]
    second = rows[:, width + 1 : width + 2]
    whole = (
        gain[...] * rows[:, :width]
        - 3.0 * scale**2 * slope_r * first * xf
        - scale**3 * first * probe
        - scale**3 * second * xf
    )
    hvp[...] = whole
    column = jnp.mean(probe * whole, axis=1, keepdims=True)
    tok_dev = column.shape[0]
    quad[...] = jnp.sum(identity(tok_dev) * column, axis=0, keepdims=True)


def moved(rows, turns, flip_x=False, flip_core=False):
    count = lax.axis_size("expert")
    pairs = [
        (i, (i + 4 * turns) % count ^ (2 * flip_x) ^ (1 * flip_core)) for i in range(count)
    ]
    return lax.ppermute(rows, "expert", pairs)


def dense_local(tokens, norm_gain, probe_signs, cotangent, routes, gates, weights):
    tok_dev, width = tokens.shape
    n_exp = lax.axis_size("expert")
    expert_count = n_exp // 2
    pack = packed(tokens, norm_gain, probe_signs, cotangent, routes, gates, expert_count)
    held = joined(weights, moved(weights, 0, flip_core=True))
    same, across = {0: pack}, {}
    same[1] = moved(pack, 1)
    across[0] = moved(pack, 0, flip_x=True)
    same[3] = moved(lax.optimization_barrier((pack, same[1]))[0], -1)
    same[2] = moved(same[1], 1)
    same[2] = lax.optimization_barrier((same[2], held))[0]
    across[1] = moved(lax.optimization_barrier((same[1], across[0]))[0], 0, flip_x=True)
    across[3] = moved(same[3], 0, flip_x=True)
    across[2] = moved(same[2], 0, flip_x=True)
    wide, sent, pair = ((jnp.float32, 1), (jnp.bfloat16, 1), (jnp.bfloat16, 2))
    here = {}
    here[0], here[1], here[2], here[3], there = experts(
        [same[0], same[1], same[2], same[3], across[0], across[1]],
        [wide, wide, sent, sent, pair],
        held,
        expert_count,
    )
    late = lax.optimization_barrier((across[2], across[3], here[1]))[:2]
    far, last = experts(late, [sent, sent], held, expert_count)

    def total(*parts):
        return sum(part.astype(jnp.float32) for part in parts).astype(jnp.bfloat16)

    beside, forward = (moved(there, 0, flip_x=True), moved(here[2], -1))
    kept = lax.optimization_barrier((here[1], far))[0]
    arrived = [
        here[0],
        beside,
        moved(here[3], 1),
        moved(far, 2, flip_x=True),
        moved(last, 1, flip_x=True),
        moved(total(kept, beside[:, kept.shape[1] :], forward), -1),
    ]
    hvp, quad = pl.pallas_call(
        finish_kernel,
        out_shape=[
            jax.ShapeDtypeStruct((tok_dev, width), jnp.float32),
            jax.ShapeDtypeStruct((1, tok_dev), jnp.float32),
        ],
        compiler_params=pltpu.CompilerParams(vmem_limit_bytes=VMEM),
        cost_estimate=pl.CostEstimate(
            flops=40 * tok_dev * width, bytes_accessed=26 * tok_dev * width, transcendentals=0
        ),
    )(tokens, norm_gain.reshape(1, width), probe_signs, *arrived)
    return (hvp, quad.reshape(tok_dev))


def routed_rows(normed, normed_t, cotangent, routes, gates, weights):
    tok_dev, width = normed.shape
    groups_here = routes.shape[0]
    half = routes.shape[2]
    n_exp = lax.axis_size("expert")
    expert_count = n_exp // 2
    cap = capacity(tok_dev, half, expert_count)
    buffer_rows = expert_count * cap
    stack_z, stack_t, stack_c, stack_w = ([], [], [], [])
    for group in range(groups_here):
        target = slot_targets(routes[group], expert_count, cap)
        place = (jnp.arange(buffer_rows, dtype=jnp.int32)[:, None] == target[None, :]).reshape(
            buffer_rows, tok_dev, half
        )
        place_tok = jnp.sum(place.astype(jnp.float32), axis=2).astype(jnp.bfloat16)
        stack_w.append(jnp.sum(place.astype(jnp.float32) * gates[group][None, :, :], axis=2))
        stack_z.append(
            jnp.dot(place_tok, normed, preferred_element_type=jnp.float32).astype(jnp.bfloat16)
        )
        stack_t.append(
            jnp.dot(place_tok, normed_t, preferred_element_type=jnp.float32).astype(jnp.bfloat16)
        )
        stack_c.append(
            jnp.dot(place_tok, cotangent, preferred_element_type=jnp.float32).astype(jnp.bfloat16)
        )
    rows_z = jnp.stack(stack_z, 0)
    rows_t = jnp.stack(stack_t, 0)
    rows_c = jnp.stack(stack_c, 0)
    weighted = jnp.stack(stack_w, 0)

    def arrange(rows):
        shaped = rows.reshape(groups_here, expert_count, 1, cap, width)
        shaped = jnp.broadcast_to(shaped, (groups_here, expert_count, 2, cap, width))
        return jnp.transpose(shaped, (1, 2, 0, 3, 4)).reshape(n_exp, groups_here * cap, width)

    send_z, send_t, send_c = (arrange(rows_z), arrange(rows_t), arrange(rows_c))
    got_z = lax.all_to_all(send_z, "expert", split_axis=0, concat_axis=0, tiled=True)
    got_t = lax.all_to_all(send_t, "expert", split_axis=0, concat_axis=0, tiled=True)
    got_c = lax.all_to_all(send_c, "expert", split_axis=0, concat_axis=0, tiled=True)
    sources, items, cols = got_z.shape
    g_rows, t_rows = expert_terms(
        weights, got_z.reshape(-1, cols), got_t.reshape(-1, cols), got_c.reshape(-1, cols)
    )
    g_rows = g_rows.reshape(sources, items, cols)
    t_rows = t_rows.reshape(sources, items, cols)
    back_g = lax.all_to_all(g_rows, "expert", split_axis=0, concat_axis=0, tiled=True)
    back_t = lax.all_to_all(t_rows, "expert", split_axis=0, concat_axis=0, tiled=True)

    def restore(rows):
        shaped = jnp.sum(rows.reshape(expert_count, 2, groups_here, cap, width), axis=1)
        return jnp.transpose(shaped, (1, 0, 2, 3)).reshape(groups_here, buffer_rows, width)

    back_g = restore(back_g)
    back_t = restore(back_t)
    contract = (((0, 1), (0, 1)), ((), ()))
    grad_z = lax.dot_general(weighted, back_g, contract, precision=lax.Precision.HIGHEST)
    tan_z = lax.dot_general(weighted, back_t, contract, precision=lax.Precision.HIGHEST)
    return (grad_z, tan_z)


def local(tokens, norm_gain, probe_signs, cotangent, routes, gates, expert_weights):
    cap = capacity(tokens.shape[0], routes.shape[2], lax.axis_size("expert") // 2)
    layout = (lax.axis_size("expert"), lax.axis_size("node"))
    if layout == (16, 1) and routes.shape[0] * cap >= tokens.shape[0]:
        return dense_local(
            tokens, norm_gain, probe_signs, cotangent, routes, gates, expert_weights
        )
    xf = tokens.astype(jnp.float32)
    probe = (2 * probe_signs - 1).astype(jnp.float32)
    tok_dev, width = xf.shape
    scale = lax.rsqrt(jnp.mean(xf * xf, axis=1, keepdims=True) + EPS)
    along = jnp.mean(xf * probe, axis=1, keepdims=True)
    normed = (xf * scale * norm_gain).astype(jnp.bfloat16)
    normed_t = (norm_gain * (scale * probe - scale**3 * xf * along)).astype(jnp.bfloat16)
    own_half = lax.all_gather(expert_weights, "node", axis=2, tiled=True)
    grad_z, tan_z = routed_rows(normed, normed_t, cotangent, routes, gates, own_half)
    share = width // lax.axis_size("node")
    start = lax.axis_index("node") * share
    slope_r = -(scale**3) * along
    grad_z, tan_z = lax.psum((grad_z, tan_z), "node")
    lifted = norm_gain * grad_z
    lifted_t = norm_gain * tan_z
    first = jnp.mean(xf * lifted, axis=1, keepdims=True)
    second = jnp.mean(xf * lifted_t, axis=1, keepdims=True)
    third = jnp.mean(probe * lifted, axis=1, keepdims=True)
    whole_hvp = (
        scale * lifted_t
        + slope_r * lifted
        - 3.0 * scale**2 * slope_r * first * xf
        - scale**3 * first * probe
        - scale**3 * (second + third) * xf
    )
    quad = jnp.mean(probe * whole_hvp, axis=1)
    hvp = lax.dynamic_slice_in_dim(whole_hvp, start, share, 1)
    return (hvp, quad)


def solution(mesh):
    placed = (
        P(("groups", "expert"), None),
        P(),
        P(("groups", "expert"), None),
        P(("groups", "expert"), None),
        P("node", ("groups", "expert"), None),
        P("node", ("groups", "expert"), None),
        P(None, None, ("expert", "node")),
    )
    return jax.shard_map(
        local,
        mesh=mesh,
        in_specs=placed,
        out_specs=(P(("groups", "expert"), "node"), P(("groups", "expert"))),
        check_vma=False,
    )
```
